32 devices in a mesh: tp: 4 (over y, x), dp: 8 (over z, core).
Axes of the slice: x: 2, y: 2, z: 4, core: 2. Of those that a mesh axis runs over, the one named last changes fastest.
Arguments:
- tokens: bfloat16 [8, 1024, 2048], P('dp', 'tp'), may hold values from -6 to 6
- seq_lengths: int32 [8, 3], P('dp'), may hold values from 64 to 896, as said below
- out_cotangent: bfloat16 [8, 1024, 2048], P('dp', 'tp'), may hold values from -6 to 6
- attn_norm_gain: float32 [2048], replicated, may hold values from 0.5 to 1.5
- query_weight: bfloat16 [2048, 2048], P(None, 'tp'), may hold values from -0.125 to 0.125
- key_weight: bfloat16 [2048, 2048], P(None, 'tp'), may hold values from -0.125 to 0.125
- value_weight: bfloat16 [2048, 2048], P(None, 'tp'), may hold values from -0.125 to 0.125
- out_gate_weight: bfloat16 [2048, 2048], P(None, 'tp'), may hold values from -0.125 to 0.125
- head_scalar_weight: bfloat16 [2048, 16, 2], P(None, 'tp'), may hold values from -0.125 to 0.125
- conv_weight: float32 [3, 4, 2048], P(None, None, 'tp'), may hold values from -3 to 3
- decay_log: float32 [16], P('tp'), may hold values from -6 to 1
- decay_bias: float32 [16], P('tp'), may hold values from -4 to -1
- head_norm_gain: float32 [128], replicated, may hold values from 0.5 to 1.5
- output_weight: bfloat16 [2048, 2048], P('tp'), may hold values from -0.1875 to 0.1875
- mlp_norm_gain: float32 [2048], replicated, may hold values from 0.5 to 1.5
- mlp_gate_weight: bfloat16 [2048, 5632], P(None, 'tp'), may hold values from -0.125 to 0.125
- mlp_up_weight: bfloat16 [2048, 5632], P(None, 'tp'), may hold values from -0.125 to 0.125
- mlp_down_weight: bfloat16 [5632, 2048], P('tp'), may hold values from -0.109375 to 0.109375
Outputs:
- block_output: bfloat16 [8, 1024, 2048], P('dp', 'tp')
- input_grad: bfloat16 [8, 1024, 2048], P('dp', 'tp')
- grad_attn_norm_gain: float32 [2048], replicated
- grad_query_weight: float32 [2048, 2048], P(None, 'tp')
- grad_key_weight: float32 [2048, 2048], P(None, 'tp')
- grad_value_weight: float32 [2048, 2048], P(None, 'tp')
- grad_out_gate_weight: float32 [2048, 2048], P(None, 'tp')
- grad_head_scalar_weight: float32 [2048, 16, 2], P(None, 'tp')
- grad_conv_weight: float32 [3, 4, 2048], P(None, None, 'tp')
- grad_decay_log: float32 [16], P('tp')
- grad_decay_bias: float32 [16], P('tp')
- grad_head_norm_gain: float32 [128], replicated
- grad_output_weight: float32 [2048, 2048], P('tp')
- grad_mlp_norm_gain: float32 [2048], replicated
- grad_mlp_gate_weight: float32 [2048, 5632], P(None, 'tp')
- grad_mlp_up_weight: float32 [2048, 5632], P(None, 'tp')
- grad_mlp_down_weight: float32 [5632, 2048], P('tp')
The draws below stay inside these ranges and needn't reach their ends.
Inputs may be any that keep to these rules, and one draw needn't show every extreme that they name: `seq_lengths`: every document length is a multiple of 64; the 3 lengths of a group sum to 1024, and one of them is at least 512.
All inputs are finite; a program needn't handle non-finite values.
Results may differ from the reference program's by a relative error of at most 0.02.
Values may be sent and summed in bfloat16 or wider, within the bound.
No kernel may reach another device: no remote copies, remote signals or barrier semaphores. Data moves between devices by JAX's collectives and lax.ppermute only.
A program may use at most 320 MiB of HBM per device.

```python
import jax
import jax.numpy as jnp
from jax import lax

D = 2048
HEADS = 16
HEAD_DIM = 128
CONV = 4
SPAN = 64
FF = 5632
TOK = 1024
GROUPS = 8


def draw_seq_lengths(key, part):
    key = jax.random.fold_in(key, 7)
    first_key, second_key, third_key = jax.random.split(key, 3)
    blocks = TOK // SPAN
    longest = jax.random.randint(first_key, (GROUPS,), blocks // 2, blocks - 1)
    remain = blocks - longest
    leading = jax.random.randint(second_key, (GROUPS,), 1, remain)
    trailing = remain - leading
    turned = jax.random.randint(third_key, (GROUPS,), 0, 3)
    trio = jnp.stack([leading, longest, trailing], axis=1)
    picks = (jnp.arange(3, dtype=jnp.int32)[None, :] - turned[:, None]) % 3
    rolled = jnp.take_along_axis(trio, picks, axis=1)
    return (rolled * SPAN).astype(jnp.int32)


def block_scale(rng, dims, shards, least, top_value):
    def one(axis_at, parts):
        heights = jax.random.uniform(jax.random.fold_in(jax.random.fold_in(rng, 6), axis_at), (parts,), jnp.float32, least / len(shards), top_value / len(shards))
        return jnp.repeat(jnp.exp(heights), dims[axis_at] // parts).reshape((-1,) + (1,) * (len(dims) - axis_at - 1))

    factor_of = one(*shards[0])
    for cut in shards[1:]:
        factor_of = factor_of * one(*cut)
    return factor_of


def bell_draw(rng, extent, width, bound, pieces=(), kind=jnp.bfloat16):
    level = block_scale(rng, extent, pieces, -0.22, 0.18) if pieces else 1.0
    array = jax.random.normal(rng, extent, jnp.float32) * width * level
    return jnp.minimum(jnp.maximum(array, -bound), bound).astype(kind)


def setup_inputs(seed: int = 0) -> dict:
    seeds = jax.random.split(jax.random.key(seed), 19)
    tokens = bell_draw(seeds[0], (GROUPS, TOK, D), 1.0, 6.0, ((0, 8), (1, 4)))
    seq_lengths = draw_seq_lengths(jax.random.fold_in(seeds[18], 71), 0)
    out_cotangent = bell_draw(seeds[2], (GROUPS, TOK, D), 1.0, 6.0, ((0, 8), (1, 4)))
    attn_norm_gain = jnp.clip(1.0 + 0.1 * jax.random.normal(seeds[3], (D,), jnp.float32), 0.5, 1.5)
    query_weight = bell_draw(seeds[4], (D, D), D ** -0.5, 0.125, ((1, 4),))
    key_weight = bell_draw(seeds[5], (D, D), D ** -0.5, 0.125, ((1, 4),))
    value_weight = bell_draw(seeds[6], (D, D), D ** -0.5, 0.125, ((1, 4),))
    out_gate_weight = bell_draw(seeds[7], (D, D), D ** -0.5, 0.125, ((1, 4),))
    head_scalar_weight = bell_draw(seeds[8], (D, HEADS, 2), D ** -0.5, 0.125, ((1, 4),))
    conv_weight = bell_draw(seeds[9], (3, CONV, D), 0.5, 3.0, ((2, 4),), jnp.float32)
    decay_log = jnp.clip(-6.0 + 7.0 * jax.random.uniform(seeds[10], (HEADS,), jnp.float32) ** block_scale(seeds[10], (HEADS,), ((0, 4),), -0.2, 0.2), -6.0, 1.0)
    decay_bias = jnp.clip(-4.0 + 3.0 * jax.random.uniform(seeds[11], (HEADS,), jnp.float32) ** block_scale(seeds[11], (HEADS,), ((0, 4),), -0.2, 0.2), -4.0, -1.0)
    head_norm_gain = jnp.clip(1.0 + 0.1 * jax.random.normal(seeds[12], (HEAD_DIM,), jnp.float32), 0.5, 1.5)
    output_weight = bell_draw(seeds[13], (D, D), (D // 2) ** -0.5, 0.1875, ((0, 4),))
    mlp_norm_gain = jnp.clip(1.0 + 0.1 * jax.random.normal(seeds[14], (D,), jnp.float32), 0.5, 1.5)
    mlp_gate_weight = bell_draw(seeds[15], (D, FF), D ** -0.5, 0.125, ((1, 4),))
    mlp_up_weight = bell_draw(seeds[16], (D, FF), D ** -0.5, 0.125, ((1, 4),))
    mlp_down_weight = bell_draw(seeds[17], (FF, D), (FF // 2) ** -0.5, 0.109375, ((0, 4),))
    return dict(tokens=tokens, seq_lengths=seq_lengths, out_cotangent=out_cotangent, attn_norm_gain=attn_norm_gain, query_weight=query_weight, key_weight=key_weight, value_weight=value_weight, out_gate_weight=out_gate_weight, head_scalar_weight=head_scalar_weight, conv_weight=conv_weight, decay_log=decay_log, decay_bias=decay_bias, head_norm_gain=head_norm_gain, output_weight=output_weight, mlp_norm_gain=mlp_norm_gain, mlp_gate_weight=mlp_gate_weight, mlp_up_weight=mlp_up_weight, mlp_down_weight=mlp_down_weight)


epsilon = 1e-06
head_epsilon = 0.001
maximum_level = lax.Precision.HIGHEST

@jax.custom_vjp
def low(v):
    return lax.optimization_barrier(v.astype(jnp.bfloat16)).astype(jnp.float32)

@jax.custom_vjp
def low_back(v):
    return v

def low_keep(v):
    return (low(v), None)

def low_pass(kept, grad):
    return (grad,)

def back_keep(v):
    return (v, None)

def back_low(kept, grad):
    return (low(grad),)
low.defvjp(low_keep, low_pass)
low_back.defvjp(back_keep, back_low)

def product(left, right):
    return jnp.dot(left, right, precision=maximum_level, preferred_element_type=jnp.float32)

def rms_scale(values):
    return lax.rsqrt(lax.optimization_barrier(jnp.mean(values * values, axis=-1, keepdims=True)) + epsilon)

def head_scale(values):
    return lax.rsqrt(lax.optimization_barrier(jnp.mean(values * values, axis=-1, keepdims=True)) + head_epsilon)

def doc_layout(lengths, length_sum):
    lengths = lengths.astype(jnp.int32)
    ends = jnp.cumsum(lengths).astype(jnp.int32)
    starts = (ends - lengths).astype(jnp.int32)
    places = jnp.arange(length_sum, dtype=jnp.int32)
    begins = lax.optimization_barrier(jnp.sum(jnp.where(ends[None, :] <= places[:, None], lengths[None, :], 0), axis=1)).astype(jnp.int32)
    positions = places - begins
    firsts = jnp.arange(length_sum // SPAN, dtype=jnp.int32) * SPAN
    carried = 1.0 - lax.optimization_barrier(jnp.sum((starts[None, :] == firsts[:, None]).astype(jnp.float32), axis=1))
    return (positions, carried)

def conv_silu(values, taps, positions):
    summed = values * taps[0]
    for offset in range(1, CONV):
        moved = jnp.concatenate([jnp.zeros((offset, values.shape[1]), jnp.float32), values[:-offset]], axis=0)
        summed = summed + moved * taps[offset] * (positions >= offset).astype(jnp.float32)[:, None]
    return jax.nn.silu(summed)

def heads_prepare(query_proj, key_proj, value_proj, scalar_proj, conv_taps, decay_log, decay_bias, positions):
    rows_here = query_proj.shape[0]
    queries = conv_silu(query_proj, conv_taps[0], positions).reshape(rows_here, -1, HEAD_DIM)
    keys_all = conv_silu(key_proj, conv_taps[1], positions).reshape(rows_here, -1, HEAD_DIM)
    values_all = conv_silu(value_proj, conv_taps[2], positions).reshape(rows_here, -1, HEAD_DIM)
    queries = queries * lax.rsqrt(lax.optimization_barrier(jnp.sum(queries * queries, axis=-1, keepdims=True)) + epsilon) * HEAD_DIM ** (-0.5)
    keys_all = keys_all * lax.rsqrt(lax.optimization_barrier(jnp.sum(keys_all * keys_all, axis=-1, keepdims=True)) + epsilon)
    writes = jax.nn.sigmoid(scalar_proj[..., 1])
    log_decay = -jnp.exp(decay_log) * jax.nn.softplus(scalar_proj[..., 0] + decay_bias)
    return (queries, keys_all, values_all, log_decay, writes)

def recurrence(queries, keys_all, values_all, log_decay, writes, carried):
    rows_here, heads_here, head_width = queries.shape
    blocks = rows_here // SPAN

    def to_blocks(source):
        return source.reshape((blocks, SPAN) + source.shape[1:])

    def block_step(current_state, inputs):
        query_tile_rows, key_block, value_block, decay_block, write_block, carry_flag = inputs
        current_state = current_state * carry_flag

        def token_step(recurrent_state, token_row):
            query_token, key_token, value_token, decay_tok, write_token = token_row
            recurrent_state = recurrent_state * jnp.exp(decay_tok)[:, None, None]
            state_prediction = jnp.einsum('mqr,mq->mr', recurrent_state, key_token, precision=maximum_level)
            recurrent_state = recurrent_state + jnp.einsum('lt,lx->ltx', key_token, write_token[:, None] * (value_token - state_prediction), precision=maximum_level)
            return (recurrent_state, jnp.einsum('mqr,mq->mr', recurrent_state, query_token, precision=maximum_level))
        return lax.scan(token_step, current_state, (query_tile_rows, key_block, value_block, decay_block, write_block))
    initial = jnp.zeros((heads_here, head_width, head_width), jnp.float32)
    final_state, outputs = lax.scan(jax.checkpoint(block_step), initial, (to_blocks(queries), to_blocks(keys_all), to_blocks(values_all), to_blocks(log_decay), to_blocks(writes), carried))
    return outputs.reshape(rows_here, heads_here, head_width)

def layer(tokens_in, lengths, params):
    attn_norm_gain, query_weight, key_weight, value_weight, out_gate_weight, head_scalar_weight, conv_weight, decay_log, decay_bias, head_norm_gain, output_weight, mlp_norm_gain, mlp_gate_weight, mlp_up_weight, mlp_down_weight = params
    rows_here = tokens_in.shape[0]
    positions, carried = doc_layout(lengths, rows_here)
    normed_in = low(tokens_in * rms_scale(tokens_in) * attn_norm_gain)
    query_proj = low_back(product(normed_in, query_weight))
    key_proj = low_back(product(normed_in, key_weight))
    value_proj = low_back(product(normed_in, value_weight))
    gate_proj = low_back(product(normed_in, out_gate_weight))
    scalar_proj = low_back(product(normed_in, head_scalar_weight.reshape(D, -1))).reshape(rows_here, HEADS, 2)
    queries, keys_all, values_all, log_decay, writes = heads_prepare(query_proj, key_proj, value_proj, scalar_proj, conv_weight, decay_log, decay_bias, positions)
    mixed = recurrence(queries, keys_all, values_all, log_decay, writes, carried)
    normed_heads = mixed * head_scale(mixed) * head_norm_gain
    gated = low(normed_heads.reshape(rows_here, D) * jax.nn.silu(gate_proj))
    middle = tokens_in + low_back(product(gated, output_weight))
    normed_mid = low(middle * rms_scale(middle) * mlp_norm_gain)
    gate_pre = low_back(product(normed_mid, mlp_gate_weight))
    up_pre = low_back(product(normed_mid, mlp_up_weight))
    hidden = low(jax.nn.silu(gate_pre) * up_pre)
    return middle + low_back(product(hidden, mlp_down_weight))

def reference(tokens, seq_lengths, out_cotangent, attn_norm_gain, query_weight, key_weight, value_weight, out_gate_weight, head_scalar_weight, conv_weight, decay_log, decay_bias, head_norm_gain, output_weight, mlp_norm_gain, mlp_gate_weight, mlp_up_weight, mlp_down_weight):
    params = tuple((weight.astype(jnp.float32) for weight in (attn_norm_gain, query_weight, key_weight, value_weight, out_gate_weight, head_scalar_weight, conv_weight, decay_log, decay_bias, head_norm_gain, output_weight, mlp_norm_gain, mlp_gate_weight, mlp_up_weight, mlp_down_weight)))

    def group_step(sums, inputs):
        tokens_group, lengths_group, cotangent_group = inputs

        def forward(tokens_in, weights):
            return layer(tokens_in, lengths_group, weights)
        result, pullback = jax.vjp(forward, tokens_group.astype(jnp.float32), params)
        grad_input, weight_grads = pullback(cotangent_group.astype(jnp.float32))
        sums = jax.tree.map(lambda left, right: left + right, sums, weight_grads)
        return (sums, (result.astype(jnp.bfloat16), grad_input.astype(jnp.bfloat16)))
    initial_sums = jax.tree.map(jnp.zeros_like, params)
    grads, (outputs, input_grads) = lax.scan(group_step, initial_sums, (tokens, seq_lengths, out_cotangent))
    return (outputs, input_grads, grads[0], grads[1], grads[2], grads[3], grads[4], grads[5], grads[6], grads[7], grads[8], grads[9], grads[10], grads[11], grads[12], grads[13], grads[14])
```

```python
from functools import partial

import jax
import jax.numpy as jnp
from jax import lax
from jax.experimental import pallas as pl
from jax.experimental.pallas import tpu as pltpu
from jax.sharding import PartitionSpec as P

HEAD_DIM = 128
CONV = 4
SPAN = 64
TILE = 2 * SPAN
VMEM_BYTES = 48 * 1024 * 1024
epsilon = 1e-06
head_epsilon = 0.001
f32 = jnp.float32
bf16 = jnp.bfloat16


def dot(left, right, dims=((1,), (0,)), precise=False):
    return lax.dot_general(
        left, right, (dims, ((), ())), preferred_element_type=f32,
        precision=lax.Precision.HIGHEST if precise else None,
    )


def iota(shape, axis):
    return lax.broadcasted_iota(jnp.int32, shape, axis)


def spread(packed):
    left = iota(packed.shape, 1) < SPAN
    none = jnp.zeros_like(packed)
    return jnp.concatenate([jnp.where(left, packed, none), jnp.where(left, none, packed)], axis=0)


def halves(full):
    left = iota((SPAN, TILE), 1) < SPAN
    return jnp.where(left, full[:SPAN], full[SPAN:])


def packed_masks():
    row, col = iota((SPAN, TILE), 0), iota((SPAN, TILE), 1) % SPAN
    return row, col


def unit_inverse(stricts):
    row, col = packed_masks()
    near = (row // 2) == (col // 2)
    eye = jnp.where(row == col, 1.0, 0.0)
    results = [eye - jnp.where(near, strict, 0.0) for strict in stricts]
    width = 2
    while width < SPAN:
        inside = ((row // (2 * width)) == (col // (2 * width))) & ((row // width) != (col // width))
        pieces = [jnp.where(inside, strict, 0.0).astype(bf16) for strict in stricts]
        kept = [result.astype(bf16) for result in results]
        moved = [dot(piece, spread(keep)) for piece, keep in zip(pieces, kept)]
        results = [result - dot(keep, spread(move.astype(bf16))) for result, keep, move in zip(results, kept, moved)]
        width *= 2
    return results


def softplus(value):
    return jnp.maximum(value, 0.0) + jnp.log1p(jnp.exp(-jnp.abs(value)))


def row_places(first, rows, starts_ref):
    place = iota((rows, HEAD_DIM), 0) + first
    one, two = starts_ref[1], starts_ref[2]
    start = jnp.where(place >= two, two, jnp.where(place >= one, one, 0))
    end = jnp.where(place >= two, 1 << 30, jnp.where(place >= one, two, one))
    return place, start, end


def carry_flag(first, starts_ref):
    fresh = (first == 0) | (first == starts_ref[1]) | (first == starts_ref[2])
    return jnp.where(fresh, 0.0, 1.0).astype(f32)


def decay_parts(scalars, rates, biases):
    row, col = iota((TILE, TILE), 0), iota((TILE, TILE), 1)
    running = jnp.where((row >= col) & ((row // SPAN) == (col // SPAN)), 1.0, 0.0)
    log_decay = -jnp.exp(rates) * softplus(scalars + biases)
    total = dot(running, log_decay, precise=True)
    return log_decay, total, total.T


def fading_of(total, total_rows, head):
    row, col = packed_masks()
    left = iota((SPAN, TILE), 1) < SPAN
    column = jnp.broadcast_to(total[:, head:head + 1], (TILE, TILE))
    gaps = jnp.where(left, column[:SPAN], column[SPAN:]) - total_rows[head:head + 1, :]
    incl = row >= col
    return jnp.where(incl, jnp.exp(jnp.where(incl, gaps, 0.0)), 0.0)


def last_rows(total, head):
    ends = [jnp.broadcast_to(total[SPAN * i + SPAN - 1:SPAN * (i + 1), head:head + 1], (SPAN, TILE)) for i in range(2)]
    return jnp.concatenate(ends, axis=0)


def forward_kernel(tiles, heads, starts_ref, q_ref, k_ref, v_ref, gate_ref, sp_ref, taps_ref, rate_ref, bias_ref, gain_ref,
                   gated_ref, mixed_ref, cq_ref, ck_ref, cv_ref, inv_ref, qk_ref, gram_ref, w_ref, u_ref, s_ref,
                   ext_ref, state_ref):
    step = pl.program_id(0)
    rows = tiles * TILE

    @pl.when(step == 0)
    def _():
        ext_ref[:, :8, :] = jnp.zeros((3, 8, heads * HEAD_DIM), f32)
        state_ref[...] = jnp.zeros(state_ref.shape, f32)

    ones = jnp.ones((HEAD_DIM, HEAD_DIM), bf16)
    place, start, _ = row_places(step * rows, rows, starts_ref)
    position = place - start
    masks = [jnp.where(position >= j, 1.0, 0.0) for j in range(1, CONV)]
    for which, source in enumerate((q_ref, k_ref, v_ref)):
        ext_ref[which, 8:8 + rows, :] = source[...].astype(f32)

    def activated(which, head, out):
        lanes = slice(head * HEAD_DIM, (head + 1) * HEAD_DIM)
        conv = ext_ref[which, 8:8 + rows, lanes] * taps_ref[which * CONV:which * CONV + 1, lanes]
        for j in range(1, CONV):
            conv = conv + ext_ref[which, 8 - j:8 - j + rows, lanes] * masks[j - 1] * taps_ref[which * CONV + j:which * CONV + j + 1, lanes]
        low = conv.astype(bf16)
        out[:, lanes] = low
        conv = low.astype(f32)
        return conv * jax.nn.sigmoid(conv)

    active = [[activated(which, h, out) for h in range(heads)] for which, out in enumerate((cq_ref, ck_ref, cv_ref))]
    norms = [[dot((one * one).astype(bf16), ones) for one in active[which]] for which in range(2)]
    queries = [one * (lax.rsqrt(norm + epsilon) * HEAD_DIM ** -0.5) for one, norm in zip(active[0], norms[0])]
    keys = [one * lax.rsqrt(norm + epsilon) for one, norm in zip(active[1], norms[1])]
    values = active[2]
    for which in range(3):
        ext_ref[which, :8, :] = ext_ref[which, rows:rows + 8, :]

    lanes_of = lambda head: slice(head * HEAD_DIM, (head + 1) * HEAD_DIM)
    row, col = packed_masks()
    left = iota((SPAN, TILE), 1) < SPAN
    pairs = [(tile, head) for tile in range(tiles) for head in range(heads)]
    spans = [slice(tile * TILE, (tile + 1) * TILE) for tile in range(tiles)]
    packs = [slice(tile * SPAN, (tile + 1) * SPAN) for tile in range(tiles)]
    scalars = [sp_ref[span, :] for span in spans]
    decays = [decay_parts(one, rate_ref[...], bias_ref[...]) for one in scalars]
    writes = [jax.nn.sigmoid(one) for one in scalars]
    grams = []
    for tile, head in pairs:
        k_low = keys[head][spans[tile]].astype(bf16)
        grams.append(dot(jnp.concatenate([queries[head][spans[tile]].astype(bf16), k_low], axis=0), k_low, ((1,), (1,))))
    stricts, scores, spread_writes, columns = [], [], [], []
    for (tile, head), both in zip(pairs, grams):
        _, total, total_rows = decays[tile]
        write = jnp.broadcast_to(writes[tile][:, heads + head:heads + head + 1], (TILE, HEAD_DIM))
        column = jnp.broadcast_to(total[:, head:head + 1], (TILE, HEAD_DIM))
        gaps = jnp.where(left, column[:SPAN], column[SPAN:]) - total_rows[head:head + 1, :]
        fading = jnp.where(row >= col, jnp.exp(jnp.where(row >= col, gaps, 0.0)), 0.0)
        qk, gram = halves(both[:TILE]), halves(both[TILE:])
        qk_ref[packs[tile], lanes_of(head)] = qk.astype(bf16)
        gram_ref[packs[tile], lanes_of(head)] = gram.astype(bf16)
        write_pack = jnp.where(left, write[:SPAN], write[SPAN:])
        stricts.append(jnp.where(row > col, write_pack * gram * fading, 0.0))
        scores.append(spread((qk * fading).astype(bf16)))
        spread_writes.append(write)
        columns.append(column)
    inverses = [one.astype(bf16) for one in unit_inverse(stricts)]
    weighted, free, q_grown, k_tail, ends = [], [], [], [], []
    for (tile, head), inverse, write, column in zip(pairs, inverses, spread_writes, columns):
        total = decays[tile][1]
        q, k, v = queries[head][spans[tile]], keys[head][spans[tile]], values[head][spans[tile]]
        grown = jnp.exp(column)
        tails = jnp.exp(last_rows(total, head) - column)
        inv_ref[packs[tile], lanes_of(head)] = inverse
        sides = jnp.concatenate([(write * grown * k).astype(bf16), (write * v).astype(bf16)], axis=1)
        solved = dot(spread(inverse), sides)
        low = solved[:, :HEAD_DIM].astype(bf16)
        w_ref[spans[tile], lanes_of(head)] = low
        weighted.append(low)
        free.append(solved[:, HEAD_DIM:])
        q_grown.append((q * grown).astype(bf16))
        k_tail.append((k * tails).astype(bf16))
        ends.append([jnp.exp(total[SPAN * i + SPAN - 1:SPAN * (i + 1), head:head + 1]) for i in range(2)])

    states = [state_ref[head] for head in range(heads)]
    for tile in range(tiles):
        at = tile * heads
        seen, changes = [[] for _ in range(heads)], [[] for _ in range(heads)]
        for i in range(2):
            flag = carry_flag(step * rows + tile * TILE + i * SPAN, starts_ref)
            states = [state * flag for state in states]
            lows = [state.astype(bf16) for state in states]
            base = (tile * 2 + i) * HEAD_DIM
            part = slice(i * SPAN, (i + 1) * SPAN)
            both = [dot(jnp.concatenate([weighted[at + h][part], q_grown[at + h][part]], axis=0), lows[h]) for h in range(heads)]
            new = [(free[at + h][part] - both[h][:SPAN]).astype(bf16) for h in range(heads)]
            states = [ends[at + h][i] * states[h] + dot(k_tail[at + h][part], new[h], ((0,), (0,))) for h in range(heads)]
            for h in range(heads):
                s_ref[base:base + HEAD_DIM, lanes_of(h)] = lows[h]
                seen[h].append(both[h][SPAN:])
                changes[h].append(new[h])
        change = [jnp.concatenate(parts, axis=0) for parts in changes]
        mixed = [jnp.concatenate(seen[h], axis=0) + dot(scores[at + h], change[h]) for h in range(heads)]
        squares = [dot((one * one).astype(bf16), ones) * (1.0 / HEAD_DIM) for one in mixed]
        for h in range(heads):
            u_ref[spans[tile], lanes_of(h)] = change[h]
            mixed_ref[spans[tile], lanes_of(h)] = mixed[h].astype(bf16)
            normed = mixed[h] * lax.rsqrt(squares[h] + head_epsilon) * gain_ref[...]
            gate = gate_ref[spans[tile], lanes_of(h)].astype(f32)
            gated_ref[spans[tile], lanes_of(h)] = (normed * gate * jax.nn.sigmoid(gate)).astype(bf16)
    for h in range(heads):
        state_ref[h] = states[h]


def blocked(rows, width, place):
    return pl.BlockSpec((rows, width), lambda i, s: (place(i) ^ s[0], 0))


def constant(shape):
    return pl.BlockSpec(shape, lambda i, s: (0,) * len(shape))


def mixer_forward(starts, q, k, v, gate, sp, taps, rate, bias, gain):
    rows, width = q.shape
    heads = width // HEAD_DIM
    block = rows // 4
    tiles = block // TILE
    spec = lambda r, w: blocked(r, w, lambda i: i)
    wide, half, state = spec(block, width), spec(block // 2, width), spec(block * 2, width)
    shape = lambda r: jax.ShapeDtypeStruct((r, width), bf16)
    return pl.pallas_call(
        partial(forward_kernel, tiles, heads),
        grid_spec=pltpu.PrefetchScalarGridSpec(
            num_scalar_prefetch=1,
            grid=(4,),
            in_specs=[wide] * 4 + [spec(block, HEAD_DIM)] + [constant(a.shape) for a in (taps, rate, bias, gain)],
            out_specs=[wide] * 5 + [half] * 3 + [wide] * 2 + [state],
            scratch_shapes=[pltpu.VMEM((3, block + 8, width), f32), pltpu.VMEM((heads, HEAD_DIM, HEAD_DIM), f32)],
        ),
        out_shape=[shape(rows)] * 5 + [shape(rows // 2)] * 3 + [shape(rows)] * 2 + [shape(rows * 2)],
        compiler_params=pltpu.CompilerParams(dimension_semantics=("arbitrary",), vmem_limit_bytes=VMEM_BYTES),
        cost_estimate=pl.CostEstimate(flops=10 * 10**9, bytes_accessed=16 * 10**6, transcendentals=10**6),
    )(starts, q, k, v, gate, sp, taps, rate, bias, gain)


def row_sums(product, ones_tall):
    high = product.astype(bf16)
    low = (product - high.astype(f32)).astype(bf16)
    return dot(jnp.concatenate([high, low], axis=1), ones_tall)


def backward_kernel(tiles, heads, starts_ref, gg_ref, mixed_ref, gate_ref, cq_ref, ck_ref, cv_ref, q_ref, k_ref, v_ref, sp_ref,
                    inv_ref, qk_ref, gram_ref, w_ref, u_ref, s_ref, taps_ref, rate_ref, bias_ref, gain_ref,
                    dq_ref, dk_ref, dv_ref, dgate_ref, dsp_ref, dtaps_ref, dmisc_ref, ext_ref, state_ref):
    step = pl.num_programs(0) - 1 - pl.program_id(0)
    rows = tiles * TILE

    @pl.when(pl.program_id(0) == 0)
    def _():
        ext_ref[:, rows:, :] = jnp.zeros((3, 8, heads * HEAD_DIM), f32)
        state_ref[...] = jnp.zeros(state_ref.shape, f32)
        dtaps_ref[...] = jnp.zeros(dtaps_ref.shape, f32)
        dmisc_ref[...] = jnp.zeros(dmisc_ref.shape, f32)

    ones = jnp.ones((HEAD_DIM, HEAD_DIM), bf16)
    ones_tall = jnp.ones((2 * HEAD_DIM, HEAD_DIM), bf16)
    lanes_of = lambda head: slice(head * HEAD_DIM, (head + 1) * HEAD_DIM)
    row, col = packed_masks()
    left = iota((SPAN, TILE), 1) < SPAN
    full_row, full_col = iota((TILE, TILE), 0), iota((TILE, TILE), 1)
    same = (full_row // SPAN) == (full_col // SPAN)
    pairs = [(tile, head) for tile in range(tiles) for head in range(heads)]
    spans = [slice(tile * TILE, (tile + 1) * TILE) for tile in range(tiles)]
    packs = [slice(tile * SPAN, (tile + 1) * SPAN) for tile in range(tiles)]
    gain = gain_ref[...]

    mixed = [mixed_ref[spans[t], lanes_of(h)].astype(f32) for t, h in pairs]
    squares = [dot((one * one).astype(bf16), ones) * (1.0 / HEAD_DIM) for one in mixed]
    partial_gain = jnp.zeros((1, HEAD_DIM), f32)
    scales, pulled, inner = [], [], []
    for (t, h), one, square in zip(pairs, mixed, squares):
        scale = lax.rsqrt(square + head_epsilon)
        gate = gate_ref[spans[t], lanes_of(h)].astype(f32)
        grad = gg_ref[spans[t], lanes_of(h)].astype(f32)
        sig = jax.nn.sigmoid(gate)
        unit = one * scale
        dgate_ref[spans[t], lanes_of(h)] = (grad * unit * gain * (sig * (1.0 + gate * (1.0 - sig)))).astype(bf16)
        norm_grad = grad * gate * sig
        partial_gain = partial_gain + jnp.sum(norm_grad * unit, axis=0, keepdims=True)
        norm_grad = norm_grad * gain
        scales.append(scale)
        pulled.append(norm_grad)
        inner.append(dot((norm_grad * unit).astype(bf16), ones) * (1.0 / HEAD_DIM))
    dmisc_ref[2:3, :] = dmisc_ref[2:3, :] + partial_gain
    dout = [(scale * (grad - one * scale * mean)).astype(bf16) for scale, grad, one, mean in zip(scales, pulled, mixed, inner)]

    def silu_parts(ref, t, h):
        conv = ref[spans[t], lanes_of(h)].astype(f32)
        sig = jax.nn.sigmoid(conv)
        return conv * sig, sig * (1.0 + conv * (1.0 - sig))

    raw_q = [silu_parts(cq_ref, t, h) for t, h in pairs]
    raw_k = [silu_parts(ck_ref, t, h) for t, h in pairs]
    norm_q = [lax.rsqrt(dot((one[0] * one[0]).astype(bf16), ones) + epsilon) for one in raw_q]
    norm_k = [lax.rsqrt(dot((one[0] * one[0]).astype(bf16), ones) + epsilon) for one in raw_k]
    decays = [decay_parts(sp_ref[span, :], rate_ref[...], bias_ref[...]) for span in spans]
    writes = [jax.nn.sigmoid(sp_ref[span, :]) for span in spans]
    queries, keys, fadings, growns, tails, spread_writes, write_packs, ends = [], [], [], [], [], [], [], []
    for n, (t, h) in enumerate(pairs):
        _, total, total_rows = decays[t]
        queries.append(raw_q[n][0] * (norm_q[n] * HEAD_DIM ** -0.5))
        keys.append(raw_k[n][0] * norm_k[n])
        write = jnp.broadcast_to(writes[t][:, heads + h:heads + h + 1], (TILE, HEAD_DIM))
        column = jnp.broadcast_to(total[:, h:h + 1], (TILE, HEAD_DIM))
        gaps = jnp.where(left, column[:SPAN], column[SPAN:]) - total_rows[h:h + 1, :]
        fadings.append(jnp.where(row >= col, jnp.exp(jnp.where(row >= col, gaps, 0.0)), 0.0))
        growns.append(jnp.exp(column))
        tails.append(jnp.exp(last_rows(total, h) - column))
        spread_writes.append(write)
        write_packs.append(jnp.where(left, write[:SPAN], write[SPAN:]))
        ends.append([jnp.exp(total[SPAN * i + SPAN - 1:SPAN * (i + 1), h:h + 1]) for i in range(2)])
    qk = [qk_ref[packs[t], lanes_of(h)].astype(f32) for t, h in pairs]
    score_grads = [dot(spread((qk[n] * fadings[n]).astype(bf16)), dout[n], ((0,), (0,))) for n in range(len(pairs))]
    q_grown = [(queries[n] * growns[n]).astype(bf16) for n in range(len(pairs))]
    k_tail = [(keys[n] * tails[n]).astype(bf16) for n in range(len(pairs))]
    parts = [slice(0, SPAN), slice(SPAN, TILE)]
    q_outs = [[dot(q_grown[n][part], dout[n][part], ((0,), (0,))) for part in parts] for n in range(len(pairs))]

    states = [state_ref[h] for h in range(heads)]
    change_grads = [[None, None] for _ in pairs]
    tail_grads = [[None, None] for _ in pairs]
    end_grads = [[None, None] for _ in pairs]
    for t in reversed(range(tiles)):
        for i in (1, 0):
            part = parts[i]
            here = slice(t * TILE + i * SPAN, t * TILE + (i + 1) * SPAN)
            at = slice((t * 2 + i) * HEAD_DIM, (t * 2 + i + 1) * HEAD_DIM)
            flag = carry_flag(step * rows + t * TILE + i * SPAN, starts_ref)
            lows = [one.astype(bf16) for one in states]
            news = []
            for h in range(heads):
                n = t * heads + h
                news.append((score_grads[n][part] + dot(k_tail[n][part], lows[h])).astype(bf16))
            for h in range(heads):
                n = t * heads + h
                change_grads[n][i] = news[h]
                tail_grads[n][i] = dot(u_ref[here, lanes_of(h)], lows[h], ((1,), (1,)))
                held = jnp.sum(states[h] * s_ref[at, lanes_of(h)].astype(f32), axis=0, keepdims=True)
                end_grads[n][i] = ends[n][i] * jnp.sum(held, axis=1, keepdims=True)
            states = [
                flag * (ends[t * heads + h][i] * states[h] + q_outs[t * heads + h][i] - dot(w_ref[here, lanes_of(h)], news[h], ((0,), (0,))))
                for h in range(heads)
            ]
    for h in range(heads):
        state_ref[h] = states[h]

    change_grads = [jnp.concatenate(one, axis=0) for one in change_grads]
    side_grads = [dot(spread(inv_ref[packs[t], lanes_of(h)]), change_grads[n], ((0,), (0,))) for n, (t, h) in enumerate(pairs)]
    side_low = [one.astype(bf16) for one in side_grads]
    crossed = []
    for n, (t, h) in enumerate(pairs):
        through = []
        for i, part in enumerate(parts):
            at = slice((t * 2 + i) * HEAD_DIM, (t * 2 + i + 1) * HEAD_DIM)
            through.append(dot(jnp.concatenate([side_low[n][part], dout[n][part]], axis=0), s_ref[at, lanes_of(h)], ((1,), (1,))))
        grams = dot(jnp.concatenate([dout[n], side_low[n]], axis=0), u_ref[spans[t], lanes_of(h)], ((1,), (1,)))
        crossed.append((through, grams))
    query_grads, key_grads = [], []
    flat_q = [one.astype(bf16) for one in queries]
    flat_k = [one.astype(bf16) for one in keys]
    products = []
    for n, (t, h) in enumerate(pairs):
        through, grams = crossed[n]
        weighted_grad = -jnp.concatenate([one[:SPAN] for one in through], axis=0)
        grown_grad = jnp.concatenate([one[SPAN:] for one in through], axis=0)
        gram = gram_ref[packs[t], lanes_of(h)].astype(f32)
        pair_grad = halves(grams[:TILE]) * fadings[n]
        strict_grad = jnp.where(row > col, -halves(grams[TILE:]), 0.0) * fadings[n]
        gram_grad = strict_grad * write_packs[n]
        matrix = jnp.concatenate([spread(pair_grad.astype(bf16)), spread(gram_grad.astype(bf16))], axis=0)
        forward = dot(matrix, flat_k[n])
        backward = dot(matrix, jnp.concatenate([flat_q[n], flat_k[n]], axis=0), ((0,), (0,)))
        tail_grad = jnp.concatenate(tail_grads[n], axis=0)
        grown_key = growns[n] * keys[n]
        write = spread_writes[n]
        query_grads.append(forward[:TILE] + grown_grad * growns[n])
        key_grads.append(forward[TILE:] + backward + tail_grad * tails[n] + weighted_grad * write * growns[n])
        value = cv_ref[spans[t], lanes_of(h)].astype(f32)
        value = value * jax.nn.sigmoid(value)
        moving = pair_grad * qk[n] + gram_grad * gram
        inner_key = weighted_grad * grown_key
        products.append((
            spread(strict_grad * gram) + inner_key + side_grads[n] * value,
            spread(moving) + grown_grad * growns[n] * queries[n] + inner_key * write,
            tail_grad * tails[n] * keys[n],
            jnp.sum(moving, axis=0, keepdims=True),
        ))
    sums = [[row_sums(one, ones_tall) for one in three[:3]] for three in products]
    upper = jnp.where((full_row <= full_col) & same, 1.0, 0.0)
    lower = jnp.where((full_row > full_col) & same, 1.0, 0.0)
    for t in range(tiles):
        gap_grad = jnp.zeros((TILE, HEAD_DIM), f32)
        tail_sum = jnp.zeros((TILE, HEAD_DIM), f32)
        write_grad = jnp.zeros((TILE, HEAD_DIM), f32)
        ends_grad = jnp.zeros((TILE, HEAD_DIM), f32)
        across = jnp.zeros((TILE, HEAD_DIM), f32)
        for h in range(heads):
            n = t * heads + h
            mine = full_col == h
            gap_grad = jnp.where(mine, sums[n][1], gap_grad)
            tail_sum = jnp.where(mine, sums[n][2], tail_sum)
            write_grad = jnp.where(full_col == heads + h, sums[n][0], write_grad)
            across = jnp.where(full_row == h, products[n][3], across)
            ends_grad = jnp.where(mine, jnp.where(full_row < SPAN, end_grads[n][0], end_grads[n][1]), ends_grad)
        log_grad = dot(upper, gap_grad - across.T, precise=True) + dot(lower, tail_sum, precise=True) + ends_grad
        scalars = sp_ref[spans[t], :]
        rate = -jnp.exp(rate_ref[...])
        inside = log_grad * rate * jax.nn.sigmoid(scalars + bias_ref[...])
        write = writes[t]
        out = jnp.where(full_col < heads, inside, write_grad * write * (1.0 - write))
        dsp_ref[spans[t], :] = jnp.where(full_col < 2 * heads, out, 0.0).astype(bf16)
        dmisc_ref[0:1, :] = dmisc_ref[0:1, :] + jnp.sum(log_grad * decays[t][0], axis=0, keepdims=True)
        dmisc_ref[1:2, :] = dmisc_ref[1:2, :] + jnp.sum(inside, axis=0, keepdims=True)

    inner_q = [dot((query_grads[n] * raw_q[n][0]).astype(bf16), ones) for n in range(len(pairs))]
    inner_k = [dot((key_grads[n] * raw_k[n][0]).astype(bf16), ones) for n in range(len(pairs))]
    for n, (t, h) in enumerate(pairs):
        scale = norm_q[n]
        grad = (query_grads[n] - raw_q[n][0] * (scale * scale * inner_q[n])) * (scale * HEAD_DIM ** -0.5)
        ext_ref[0, spans[t], lanes_of(h)] = grad * raw_q[n][1]
        scale = norm_k[n]
        grad = (key_grads[n] - raw_k[n][0] * (scale * scale * inner_k[n])) * scale
        ext_ref[1, spans[t], lanes_of(h)] = grad * raw_k[n][1]
        ext_ref[2, spans[t], lanes_of(h)] = side_grads[n] * spread_writes[n] * silu_parts(cv_ref, t, h)[1]
    place, _, end = row_places(step * rows, rows, starts_ref)
    masks = [None] + [jnp.where(place + j < end, 1.0, 0.0) for j in range(1, CONV)]
    for which, (source, out) in enumerate(((q_ref, dq_ref), (k_ref, dk_ref), (v_ref, dv_ref))):
        for h in range(heads):
            lanes = lanes_of(h)
            proj = source[:, lanes].astype(f32)
            total = None
            for j in range(CONV):
                moved = ext_ref[which, j:j + rows, lanes]
                if j:
                    moved = moved * masks[j]
                at = which * CONV + j
                dtaps_ref[at:at + 1, lanes] = dtaps_ref[at:at + 1, lanes] + jnp.sum(proj * moved, axis=0, keepdims=True)
                term = moved * taps_ref[at:at + 1, lanes]
                total = term if total is None else total + term
            out[:, lanes] = total.astype(bf16)
        ext_ref[which, rows:, :] = ext_ref[which, :8, :]


def mixer_backward(starts, gg, gate, q, k, v, sp, kept, taps, rate, bias, gain):
    mixed, cq, ck, cv, inv, qk, gram, w, u, s = kept
    rows, width = q.shape
    heads = width // HEAD_DIM
    block = rows // 4
    tiles = block // TILE
    spec = lambda r, w: blocked(r, w, lambda i: 3 - i)
    wide, half, state, scal = spec(block, width), spec(block // 2, width), spec(block * 2, width), spec(block, HEAD_DIM)
    shape = lambda r: jax.ShapeDtypeStruct((r, width), bf16)
    return pl.pallas_call(
        partial(backward_kernel, tiles, heads),
        grid_spec=pltpu.PrefetchScalarGridSpec(
            num_scalar_prefetch=1,
            grid=(4,),
            in_specs=[wide] * 9 + [scal] + [half] * 3 + [wide] * 2 + [state] + [constant(a.shape) for a in (taps, rate, bias, gain)],
            out_specs=[wide] * 4 + [scal, constant((3 * CONV, width)), constant((8, HEAD_DIM))],
            scratch_shapes=[pltpu.VMEM((3, block + 8, width), f32), pltpu.VMEM((heads, HEAD_DIM, HEAD_DIM), f32)],
        ),
        out_shape=[shape(rows)] * 4
        + [
            jax.ShapeDtypeStruct((rows, HEAD_DIM), bf16),
            jax.ShapeDtypeStruct((3 * CONV, width), f32),
            jax.ShapeDtypeStruct((8, HEAD_DIM), f32),
        ],
        compiler_params=pltpu.CompilerParams(dimension_semantics=("arbitrary",), vmem_limit_bytes=VMEM_BYTES),
        cost_estimate=pl.CostEstimate(flops=20 * 10**9, bytes_accessed=24 * 10**6, transcendentals=10**6),
    )(starts, gg, mixed, gate, cq, ck, cv, q, k, v, sp, inv, qk, gram, w, u, s, taps, rate, bias, gain)


def xor_pairs(size, mask):
    return [(i, i ^ mask) for i in range(size)]


def tied(first, *rest):
    return lax.optimization_barrier((first,) + rest)


def gather_rows(mine):
    size = lax.axis_size("tp")
    half = mine.shape[0] // 2
    across = lax.ppermute(mine, "tp", xor_pairs(size, 1))
    down = lax.ppermute(mine, "tp", xor_pairs(size, 2))
    far_top = lax.ppermute(down[:half], "tp", xor_pairs(size, 1))
    far_low = lax.ppermute(across[half:], "tp", xor_pairs(size, 2))
    return [mine, across, down, jnp.concatenate([far_top, far_low], axis=0)]


def scatter_rows(parts):
    size = lax.axis_size("tp")
    mine, across, down, far = parts
    half = mine.shape[0] // 2
    far_top = lax.ppermute(far[:half], "tp", xor_pairs(size, 1))
    far_low = lax.ppermute(far[half:], "tp", xor_pairs(size, 2))
    down = jnp.concatenate([down[:half] + far_top, down[half:]], axis=0)
    across = jnp.concatenate([across[:half], across[half:] + far_low], axis=0)
    return (
        mine.astype(f32)
        + lax.ppermute(across, "tp", xor_pairs(size, 1)).astype(f32)
        + lax.ppermute(down, "tp", xor_pairs(size, 2)).astype(f32)
    )


def sum_small(values, axis):
    size, mask = lax.axis_size(axis), 1
    while mask < size:
        values = values + lax.ppermute(values, axis, xor_pairs(size, mask))
        mask *= 2
    return values


def line_sums(chunks):
    size = lax.axis_size("dp")
    stride = size // 4
    hops = [
        [(j, j + stride) for j in range(stride)] + [(j + 3 * stride, j + 2 * stride) for j in range(stride)],
        [(j + stride, j + 2 * stride) for j in range(stride)] + [(j + 2 * stride, j + stride) for j in range(stride)],
        [(j + stride, j) for j in range(stride)] + [(j + 2 * stride, j + 3 * stride) for j in range(stride)],
    ]
    place = lax.axis_index("dp") // stride
    center = (place == 1) | (place == 2)
    chunks = list(chunks)
    count = len(chunks)
    sums, wholes, results = {}, {}, []
    gone = ()
    for step in range(count + 2):
        going = []
        if step < count:
            chunk = chunks[step]
            mask = 2
            while mask < stride:
                chunk = chunk + lax.ppermute(chunk, "dp", xor_pairs(size, mask))
                mask *= 2
            going.append((0, step, chunk))
        if 0 <= step - 1 < count:
            going.append((1, step - 1, sums.pop(step - 1)))
        if 0 <= step - 2 < count:
            going.append((2, step - 2, wholes.pop(step - 2)))
        held = lax.optimization_barrier(tuple(one[2] for one in going) + gone)
        gone = ()
        for (stage, which, _), value in zip(going, held):
            moved = lax.ppermute(value, "dp", hops[stage])
            gone += (moved,)
            if stage == 0:
                sums[which] = value + moved
            elif stage == 1:
                wholes[which] = value + moved
            else:
                results.append(jnp.where(center, value, moved))
    return results


def core_sum(keep, send):
    return keep + lax.ppermute(send, "dp", xor_pairs(lax.axis_size("dp"), 1))


def core_join(part, axis, first):
    other = lax.ppermute(part, "dp", xor_pairs(lax.axis_size("dp"), 1))
    low = jnp.where(first, part, other)
    high = jnp.where(first, other, part)
    return jnp.concatenate([low, high], axis=axis).astype(f32)


def rms_scale(values):
    return lax.rsqrt(jnp.mean(values * values, axis=-1, keepdims=True) + epsilon)


def product(left, right):
    return jnp.dot(left, right, preferred_element_type=f32)


def product_t(left, right):
    return jnp.einsum("td,ld->tl", left, right, preferred_element_type=f32)


def outer(left, right):
    return jnp.einsum("ta,tb->ab", left, right, preferred_element_type=f32).astype(bf16)


def body(
    tokens,
    seq_lengths,
    out_cotangent,
    attn_norm_gain,
    query_weight,
    key_weight,
    value_weight,
    out_gate_weight,
    head_scalar_weight,
    conv_weight,
    decay_log,
    decay_bias,
    head_norm_gain,
    output_weight,
    mlp_norm_gain,
    mlp_gate_weight,
    mlp_up_weight,
    mlp_down_weight,
):
    width = tokens.shape[2]
    half = width // 2
    heads = decay_log.shape[0]
    first_core = lax.axis_index("dp") % 2 == 0
    rank = lax.axis_index("tp").astype(jnp.int32)
    lengths = seq_lengths[0]
    starts = jnp.stack([rank, lengths[0], lengths[0] + lengths[1]])

    def mine_first(values):
        low, high = values[:, :half], values[:, half:]
        return jnp.where(first_core, low, high), jnp.where(first_core, high, low)

    token_parts = gather_rows(tokens[0])
    weight_part = jnp.where(first_core, output_weight[:, :half], output_weight[:, half:])
    weight_part, _ = tied(weight_part, token_parts[3])
    weight_mine = jnp.concatenate(gather_rows(weight_part), axis=0)
    weight_other = lax.ppermute(weight_mine, "dp", xor_pairs(lax.axis_size("dp"), 1))
    weight_full = jnp.concatenate(
        [jnp.where(first_core, weight_mine, weight_other), jnp.where(first_core, weight_other, weight_mine)], axis=1
    )
    cotangent_part, _ = tied(out_cotangent[0], weight_mine)

    scalar_weight = jnp.pad(
        jnp.transpose(head_scalar_weight, (0, 2, 1)).reshape(width, 2 * heads), ((0, 0), (0, HEAD_DIM - 2 * heads))
    )
    pad_row = lambda row: jnp.pad(row, (0, HEAD_DIM - heads))[None]
    rates, biases = pad_row(decay_log), pad_row(decay_bias)
    taps = conv_weight.reshape(3 * CONV, -1)
    inputs = jnp.concatenate(token_parts, axis=0).astype(f32)
    scale_in = rms_scale(inputs)
    normed_in = (inputs * scale_in * attn_norm_gain).astype(bf16)
    query_proj = product(normed_in, query_weight).astype(bf16)
    key_proj = product(normed_in, key_weight).astype(bf16)
    value_proj = product(normed_in, value_weight).astype(bf16)
    gate_proj = product(normed_in, out_gate_weight).astype(bf16)
    scalar_proj = product(normed_in, scalar_weight)
    gated, *kept = mixer_forward(
        starts, query_proj, key_proj, value_proj, gate_proj, scalar_proj, taps, rates, biases, head_norm_gain[None]
    )
    rows = tokens.shape[1]
    order = lambda values, mask: jnp.concatenate([values[(m ^ mask) * rows:((m ^ mask) + 1) * rows] for m in range(4)], axis=0)
    gated_parts = gather_rows(gated)
    gated_full = jnp.concatenate([order(part, mask) for mask, part in enumerate(gated_parts)], axis=1)
    middle = inputs + product(gated_full, weight_full)
    scale_mid = rms_scale(middle)
    normed_mid = (middle * scale_mid * mlp_norm_gain).astype(bf16)

    gate_pre = product(normed_mid, mlp_gate_weight)
    up_pre = product(normed_mid, mlp_up_weight)
    sigmoid_gate = jax.nn.sigmoid(gate_pre)
    silu_gate = gate_pre * sigmoid_gate
    hidden = (silu_gate * up_pre).astype(bf16)
    cotangent_part, _ = tied(cotangent_part, gated_parts[3])
    cotangent_all = jnp.concatenate(gather_rows(cotangent_part), axis=0)
    cot_keep, cot_send = mine_first(cotangent_all)
    down_sum = core_sum(outer(hidden, cot_keep), outer(hidden, cot_send))
    hidden_grad = product_t(cotangent_all, mlp_down_weight)
    gate_grad = (hidden_grad * up_pre * sigmoid_gate * (1.0 + gate_pre * (1.0 - sigmoid_gate))).astype(bf16)
    up_grad = (hidden_grad * silu_gate).astype(bf16)
    split = lambda values: [values[m * rows:(m + 1) * rows] for m in range(4)]
    mid_partial = (product_t(gate_grad, mlp_gate_weight) + product_t(up_grad, mlp_up_weight)).astype(bf16)
    mid_normed_grad = scatter_rows(split(mid_partial))
    mid_keep, mid_send = mine_first(normed_mid)
    gate_sum = core_sum(outer(mid_keep, gate_grad), outer(mid_send, gate_grad))
    up_sum = core_sum(outer(mid_keep, up_grad), outer(mid_send, up_grad))

    middle_mine, scale_mine = middle[:rows], scale_mid[:rows]
    unit_mid = middle_mine * scale_mine
    gain_mid = jnp.sum(mid_normed_grad * unit_mid, axis=0)
    unit_grad = mid_normed_grad * mlp_norm_gain
    middle_grad = out_cotangent[0].astype(f32) + scale_mine * (
        unit_grad - unit_mid * jnp.mean(unit_grad * unit_mid, axis=-1, keepdims=True)
    )
    attn_grad = jnp.concatenate(gather_rows(middle_grad.astype(bf16)), axis=0)
    gated_grad = product_t(attn_grad, output_weight).astype(bf16)
    result_partial, _ = tied(product(hidden, mlp_down_weight).astype(bf16), attn_grad)
    result = middle_mine + scatter_rows(split(result_partial))
    attn_keep, attn_send = mine_first(attn_grad)
    out_sum = core_sum(outer(gated, attn_keep), outer(gated, attn_send))
    query_low, key_low, value_low, gate_low, scalar_low, grad_taps, misc = mixer_backward(
        starts, gated_grad, gate_proj, query_proj, key_proj, value_proj, scalar_proj, kept, taps, rates, biases, head_norm_gain[None]
    )
    in_keep, in_send = mine_first(normed_in)
    gate_proj_sum = core_sum(outer(in_keep, gate_low), outer(in_send, gate_low))
    query_sum = core_sum(outer(in_keep, query_low), outer(in_send, query_low))
    key_sum = core_sum(outer(in_keep, key_low), outer(in_send, key_low))
    value_sum = core_sum(outer(in_keep, value_low), outer(in_send, value_low))
    in_partial = (
        product_t(query_low, query_weight)
        + product_t(key_low, key_weight)
        + product_t(value_low, value_weight)
        + product_t(gate_low, out_gate_weight)
        + product_t(scalar_low, scalar_weight)
    ).astype(bf16)
    in_normed_grad = scatter_rows(split(in_partial))
    unit_in = inputs[:rows] * scale_in[:rows]
    gain_in = jnp.sum(in_normed_grad * unit_in, axis=0)
    unit_grad_in = in_normed_grad * attn_norm_gain
    input_grad = middle_grad + scale_in[:rows] * (
        unit_grad_in - unit_in * jnp.mean(unit_grad_in * unit_in, axis=-1, keepdims=True)
    )

    cut = lambda values: jnp.split(values, 2, axis=0)
    down_low, down_high = cut(down_sum)
    gate_top, gate_low_rows = cut(gate_sum)
    up_top, up_low_rows = cut(up_sum)
    even = line_sums([down_low, gate_top, up_top, out_sum, query_sum, value_sum])
    odd = line_sums([down_high, gate_low_rows, up_low_rows, gate_proj_sum, key_sum])
    join = lambda part, axis: core_join(part, axis, first_core)
    grad_down = join(jnp.concatenate([even[0], odd[0]], axis=0), 1)
    grad_mlp_gate = join(jnp.concatenate([even[1], odd[1]], axis=0), 0)
    grad_mlp_up = join(jnp.concatenate([even[2], odd[2]], axis=0), 0)
    grad_output = join(even[3], 1)
    grad_gate = join(odd[3], 0)
    grad_query = join(even[4], 0)
    grad_key = join(odd[4], 0)
    grad_value = join(even[5], 0)

    scalar_grad = jnp.einsum("td,tl->dl", normed_in, scalar_low, preferred_element_type=f32)[:, :2 * heads]
    shared = jnp.concatenate([gain_in, gain_mid, misc[2]])
    shared = sum_small(shared, "tp")
    small = jnp.concatenate([scalar_grad.reshape(-1), grad_taps.reshape(-1), misc[0, :heads], misc[1, :heads], shared])
    small = sum_small(small, "dp")
    pieces = []
    at = 0
    for size in (width * 2 * heads, grad_taps.size, heads, heads, width, width, HEAD_DIM):
        pieces.append(small[at:at + size])
        at += size
    scalar_sum, taps_sum, log_sum, bias_sum, gain_in, gain_mid, gain_head = pieces
    return (
        result.astype(bf16)[None],
        input_grad.astype(bf16)[None],
        gain_in,
        grad_query,
        grad_key,
        grad_value,
        grad_gate,
        jnp.transpose(scalar_sum.reshape(width, 2, heads), (0, 2, 1)),
        taps_sum.reshape(conv_weight.shape),
        log_sum,
        bias_sum,
        gain_head,
        grad_output,
        gain_mid,
        grad_mlp_gate,
        grad_mlp_up,
        grad_down,
    )


def solution(mesh):
    return jax.shard_map(
        body,
        mesh=mesh,
        in_specs=(
            P("dp", "tp", None),
            P("dp", None),
            P("dp", "tp", None),
            P(),
            P(None, "tp"),
            P(None, "tp"),
            P(None, "tp"),
            P(None, "tp"),
            P(None, "tp", None),
            P(None, None, "tp"),
            P("tp"),
            P("tp"),
            P(),
            P("tp", None),
            P(),
            P(None, "tp"),
            P(None, "tp"),
            P("tp", None),
        ),
        out_specs=(
            P("dp", "tp", None),
            P("dp", "tp", None),
            P(),
            P(None, "tp"),
            P(None, "tp"),
            P(None, "tp"),
            P(None, "tp"),
            P(None, "tp", None),
            P(None, None, "tp"),
            P("tp"),
            P("tp"),
            P(),
            P("tp", None),
            P(),
            P(None, "tp"),
            P(None, "tp"),
            P("tp", None),
        ),
        check_vma=False,
    )
```

```python
import math
from functools import partial

import jax
import jax.numpy as jnp
from jax import lax
from jax.experimental import pallas as pl
from jax.experimental.pallas import tpu as pltpu
from jax.sharding import PartitionSpec as P

HEAD_DIM = 128
CONV = 4
SPAN = 64
TILE = 2 * SPAN
VMEM_BYTES = 60 * 1024 * 1024
SMALL = pl.CostEstimate(flops=0, bytes_accessed=0, transcendentals=0)
epsilon = 1e-06
head_epsilon = 0.001
f32 = jnp.float32
bf16 = jnp.bfloat16


def dot(left, right, dims=((1,), (0,)), precise=False):
    return lax.dot_general(
        left, right, (dims, ((), ())), preferred_element_type=f32,
        precision=lax.Precision.HIGHEST if precise else None,
    )


def iota(shape, axis):
    return lax.broadcasted_iota(jnp.int32, shape, axis)


def spread(packed):
    left = iota(packed.shape, 1) < SPAN
    none = jnp.zeros_like(packed)
    return jnp.concatenate([jnp.where(left, packed, none), jnp.where(left, none, packed)], axis=0)


def halves(full):
    left = iota((SPAN, TILE), 1) < SPAN
    return jnp.where(left, full[:SPAN], full[SPAN:])


def packed_masks():
    row, col = iota((SPAN, TILE), 0), iota((SPAN, TILE), 1) % SPAN
    return row, col


def unit_inverse(stricts):
    row, col = packed_masks()
    near = (row // 2) == (col // 2)
    eye = jnp.where(row == col, 1.0, 0.0)
    results = [eye - jnp.where(near, strict, 0.0) for strict in stricts]
    width = 2
    while width < SPAN:
        inside = ((row // (2 * width)) == (col // (2 * width))) & ((row // width) != (col // width))
        pieces = [jnp.where(inside, strict, 0.0).astype(bf16) for strict in stricts]
        kept = [result.astype(bf16) for result in results]
        moved = [dot(piece, spread(keep)) for piece, keep in zip(pieces, kept)]
        results = [result - dot(keep, spread(move.astype(bf16))) for result, keep, move in zip(results, kept, moved)]
        width *= 2
    return results


def softplus(value):
    return jnp.maximum(value, 0.0) + jnp.log1p(jnp.exp(-jnp.abs(value)))


def row_places(first, rows, starts_ref):
    place = iota((rows, HEAD_DIM), 0) + first
    one, two = starts_ref[1], starts_ref[2]
    start = jnp.where(place >= two, two, jnp.where(place >= one, one, 0))
    end = jnp.where(place >= two, 1 << 30, jnp.where(place >= one, two, one))
    return place, start, end


def carry_flag(first, starts_ref):
    fresh = (first == 0) | (first == starts_ref[1]) | (first == starts_ref[2])
    return jnp.where(fresh, 0.0, 1.0).astype(f32)


def decay_parts(scalars, rates, biases):
    row, col = iota((TILE, TILE), 0), iota((TILE, TILE), 1)
    running = jnp.where((row >= col) & ((row // SPAN) == (col // SPAN)), 1.0, 0.0)
    log_decay = -jnp.exp(rates) * softplus(scalars + biases)
    total = dot(running, log_decay, precise=True)
    return log_decay, total, total.T


def fading_of(total, total_rows, head):
    row, col = packed_masks()
    left = iota((SPAN, TILE), 1) < SPAN
    column = jnp.broadcast_to(total[:, head:head + 1], (TILE, TILE))
    gaps = jnp.where(left, column[:SPAN], column[SPAN:]) - total_rows[head:head + 1, :]
    incl = row >= col
    return jnp.where(incl, jnp.exp(jnp.where(incl, gaps, 0.0)), 0.0)


def last_rows(total, head):
    ends = [jnp.broadcast_to(total[SPAN * i + SPAN - 1:SPAN * (i + 1), head:head + 1], (SPAN, TILE)) for i in range(2)]
    return jnp.concatenate(ends, axis=0)


def forward_kernel(tiles, heads, starts_ref, q_ref, k_ref, v_ref, gate_ref, sp_ref, taps_ref, rate_ref, bias_ref, gain_ref,
                   gated_ref, mixed_ref, cq_ref, ck_ref, cv_ref, inv_ref, qk_ref, gram_ref, w_ref, u_ref, s_ref,
                   ext_ref, state_ref):
    step = pl.program_id(0)
    rows = tiles * TILE

    @pl.when(step == 0)
    def _():
        ext_ref[:, :8, :] = jnp.zeros((3, 8, heads * HEAD_DIM), f32)
        state_ref[...] = jnp.zeros(state_ref.shape, f32)

    ones = jnp.ones((HEAD_DIM, HEAD_DIM), bf16)
    place, start, _ = row_places(step * rows, rows, starts_ref)
    position = place - start
    masks = [jnp.where(position >= j, 1.0, 0.0) for j in range(1, CONV)]
    for which, source in enumerate((q_ref, k_ref, v_ref)):
        ext_ref[which, 8:8 + rows, :] = source[...].astype(f32)

    def activated(which, head, out):
        lanes = slice(head * HEAD_DIM, (head + 1) * HEAD_DIM)
        conv = ext_ref[which, 8:8 + rows, lanes] * taps_ref[which * CONV:which * CONV + 1, lanes]
        for j in range(1, CONV):
            conv = conv + ext_ref[which, 8 - j:8 - j + rows, lanes] * masks[j - 1] * taps_ref[which * CONV + j:which * CONV + j + 1, lanes]
        low = conv.astype(bf16)
        out[:, lanes] = low
        conv = low.astype(f32)
        return conv * jax.nn.sigmoid(conv)

    active = [[activated(which, h, out) for h in range(heads)] for which, out in enumerate((cq_ref, ck_ref, cv_ref))]
    norms = [[dot((one * one).astype(bf16), ones) for one in active[which]] for which in range(2)]
    queries = [one * (lax.rsqrt(norm + epsilon) * HEAD_DIM ** -0.5) for one, norm in zip(active[0], norms[0])]
    keys = [one * lax.rsqrt(norm + epsilon) for one, norm in zip(active[1], norms[1])]
    values = active[2]
    for which in range(3):
        ext_ref[which, :8, :] = ext_ref[which, rows:rows + 8, :]

    lanes_of = lambda head: slice(head * HEAD_DIM, (head + 1) * HEAD_DIM)
    row, col = packed_masks()
    left = iota((SPAN, TILE), 1) < SPAN
    pairs = [(tile, head) for tile in range(tiles) for head in range(heads)]
    spans = [slice(tile * TILE, (tile + 1) * TILE) for tile in range(tiles)]
    packs = [slice(tile * SPAN, (tile + 1) * SPAN) for tile in range(tiles)]
    scalars = [sp_ref[span, :] for span in spans]
    decays = [decay_parts(one, rate_ref[...], bias_ref[...]) for one in scalars]
    writes = [jax.nn.sigmoid(one) for one in scalars]
    grams = []
    for tile, head in pairs:
        k_low = keys[head][spans[tile]].astype(bf16)
        grams.append(dot(jnp.concatenate([queries[head][spans[tile]].astype(bf16), k_low], axis=0), k_low, ((1,), (1,))))
    stricts, scores, spread_writes, columns = [], [], [], []
    for (tile, head), both in zip(pairs, grams):
        _, total, total_rows = decays[tile]
        write = jnp.broadcast_to(writes[tile][:, heads + head:heads + head + 1], (TILE, HEAD_DIM))
        column = jnp.broadcast_to(total[:, head:head + 1], (TILE, HEAD_DIM))
        gaps = jnp.where(left, column[:SPAN], column[SPAN:]) - total_rows[head:head + 1, :]
        fading = jnp.where(row >= col, jnp.exp(jnp.where(row >= col, gaps, 0.0)), 0.0)
        qk, gram = halves(both[:TILE]), halves(both[TILE:])
        qk_ref[packs[tile], lanes_of(head)] = qk.astype(bf16)
        gram_ref[packs[tile], lanes_of(head)] = gram.astype(bf16)
        write_pack = jnp.where(left, write[:SPAN], write[SPAN:])
        stricts.append(jnp.where(row > col, write_pack * gram * fading, 0.0))
        scores.append(spread((qk * fading).astype(bf16)))
        spread_writes.append(write)
        columns.append(column)
    inverses = [one.astype(bf16) for one in unit_inverse(stricts)]
    weighted, free, q_grown, k_tail, ends = [], [], [], [], []
    for (tile, head), inverse, write, column in zip(pairs, inverses, spread_writes, columns):
        total = decays[tile][1]
        q, k, v = queries[head][spans[tile]], keys[head][spans[tile]], values[head][spans[tile]]
        grown = jnp.exp(column)
        tails = jnp.exp(last_rows(total, head) - column)
        inv_ref[packs[tile], lanes_of(head)] = inverse
        sides = jnp.concatenate([(write * grown * k).astype(bf16), (write * v).astype(bf16)], axis=1)
        solved = dot(spread(inverse), sides)
        low = solved[:, :HEAD_DIM].astype(bf16)
        w_ref[spans[tile], lanes_of(head)] = low
        weighted.append(low)
        free.append(solved[:, HEAD_DIM:])
        q_grown.append((q * grown).astype(bf16))
        k_tail.append((k * tails).astype(bf16))
        ends.append([jnp.exp(total[SPAN * i + SPAN - 1:SPAN * (i + 1), head:head + 1]) for i in range(2)])

    states = [state_ref[head] for head in range(heads)]
    for tile in range(tiles):
        at = tile * heads
        seen, changes = [[] for _ in range(heads)], [[] for _ in range(heads)]
        for i in range(2):
            flag = carry_flag(step * rows + tile * TILE + i * SPAN, starts_ref)
            states = [state * flag for state in states]
            lows = [state.astype(bf16) for state in states]
            base = (tile * 2 + i) * HEAD_DIM
            part = slice(i * SPAN, (i + 1) * SPAN)
            both = [dot(jnp.concatenate([weighted[at + h][part], q_grown[at + h][part]], axis=0), lows[h]) for h in range(heads)]
            new = [(free[at + h][part] - both[h][:SPAN]).astype(bf16) for h in range(heads)]
            states = [ends[at + h][i] * states[h] + dot(k_tail[at + h][part], new[h], ((0,), (0,))) for h in range(heads)]
            for h in range(heads):
                s_ref[base:base + HEAD_DIM, lanes_of(h)] = lows[h]
                seen[h].append(both[h][SPAN:])
                changes[h].append(new[h])
        change = [jnp.concatenate(parts, axis=0) for parts in changes]
        mixed = [jnp.concatenate(seen[h], axis=0) + dot(scores[at + h], change[h]) for h in range(heads)]
        squares = [dot((one * one).astype(bf16), ones) * (1.0 / HEAD_DIM) for one in mixed]
        for h in range(heads):
            u_ref[spans[tile], lanes_of(h)] = change[h]
            mixed_ref[spans[tile], lanes_of(h)] = mixed[h].astype(bf16)
            normed = mixed[h] * lax.rsqrt(squares[h] + head_epsilon) * gain_ref[...]
            gate = gate_ref[spans[tile], lanes_of(h)].astype(f32)
            gated_ref[spans[tile], lanes_of(h)] = (normed * gate * jax.nn.sigmoid(gate)).astype(bf16)
    for h in range(heads):
        state_ref[h] = states[h]


def blocked(rows, width, place):
    return pl.BlockSpec((rows, width), lambda i, s: (place(i) ^ s[0], 0))


def constant(shape):
    return pl.BlockSpec(shape, lambda i, s: (0,) * len(shape))


def mixer_forward(count, starts, q, k, v, gate, sp, taps, rate, bias, gain):
    rows, width = q.shape
    heads = width // HEAD_DIM
    block = rows // count
    tiles = block // TILE
    spec = lambda r, w: blocked(r, w, lambda i: i)
    wide, half, state = spec(block, width), spec(block // 2, width), spec(block * 2, width)
    shape = lambda r: jax.ShapeDtypeStruct((r, width), bf16)
    return pl.pallas_call(
        partial(forward_kernel, tiles, heads),
        grid_spec=pltpu.PrefetchScalarGridSpec(
            num_scalar_prefetch=1,
            grid=(count,),
            in_specs=[wide] * 4 + [spec(block, HEAD_DIM)] + [constant(a.shape) for a in (taps, rate, bias, gain)],
            out_specs=[wide] * 5 + [half] * 3 + [wide] * 2 + [state],
            scratch_shapes=[pltpu.VMEM((3, block + 8, width), f32), pltpu.VMEM((heads, HEAD_DIM, HEAD_DIM), f32)],
        ),
        out_shape=[shape(rows)] * 5 + [shape(rows // 2)] * 3 + [shape(rows)] * 2 + [shape(rows * 2)],
        compiler_params=pltpu.CompilerParams(dimension_semantics=("arbitrary",), vmem_limit_bytes=VMEM_BYTES),
        cost_estimate=SMALL,
    )(starts, q, k, v, gate, sp, taps, rate, bias, gain)


def row_sums(product, ones_tall):
    high = product.astype(bf16)
    low = (product - high.astype(f32)).astype(bf16)
    return dot(jnp.concatenate([high, low], axis=1), ones_tall)


def backward_kernel(tiles, heads, starts_ref, gg_ref, mixed_ref, gate_ref, cq_ref, ck_ref, cv_ref, q_ref, k_ref, v_ref, sp_ref,
                    inv_ref, qk_ref, gram_ref, w_ref, u_ref, s_ref, taps_ref, rate_ref, bias_ref, gain_ref,
                    flat_ref, dsp_ref, dtaps_ref, dmisc_ref, ext_ref, state_ref):
    step = pl.num_programs(0) - 1 - pl.program_id(0)
    rows = tiles * TILE

    @pl.when(pl.program_id(0) == 0)
    def _():
        ext_ref[:, rows:, :] = jnp.zeros((3, 8, heads * HEAD_DIM), f32)
        state_ref[...] = jnp.zeros(state_ref.shape, f32)
        dtaps_ref[...] = jnp.zeros(dtaps_ref.shape, f32)
        dmisc_ref[...] = jnp.zeros(dmisc_ref.shape, f32)

    ones = jnp.ones((HEAD_DIM, HEAD_DIM), bf16)
    ones_tall = jnp.ones((2 * HEAD_DIM, HEAD_DIM), bf16)
    lanes_of = lambda head: slice(head * HEAD_DIM, (head + 1) * HEAD_DIM)
    row, col = packed_masks()
    left = iota((SPAN, TILE), 1) < SPAN
    full_row, full_col = iota((TILE, TILE), 0), iota((TILE, TILE), 1)
    same = (full_row // SPAN) == (full_col // SPAN)
    pairs = [(tile, head) for tile in range(tiles) for head in range(heads)]
    spans = [slice(tile * TILE, (tile + 1) * TILE) for tile in range(tiles)]
    packs = [slice(tile * SPAN, (tile + 1) * SPAN) for tile in range(tiles)]
    gain = gain_ref[...]

    mixed = [mixed_ref[spans[t], lanes_of(h)].astype(f32) for t, h in pairs]
    squares = [dot((one * one).astype(bf16), ones) * (1.0 / HEAD_DIM) for one in mixed]
    partial_gain = jnp.zeros((1, HEAD_DIM), f32)
    scales, pulled, inner = [], [], []
    for (t, h), one, square in zip(pairs, mixed, squares):
        scale = lax.rsqrt(square + head_epsilon)
        gate = gate_ref[spans[t], lanes_of(h)].astype(f32)
        grad = gg_ref[spans[t], lanes_of(h)].astype(f32)
        sig = jax.nn.sigmoid(gate)
        unit = one * scale
        flat_ref[spans[t], lanes_of(3 * heads + h)] = (grad * unit * gain * (sig * (1.0 + gate * (1.0 - sig)))).astype(bf16)
        norm_grad = grad * gate * sig
        partial_gain = partial_gain + jnp.sum(norm_grad * unit, axis=0, keepdims=True)
        norm_grad = norm_grad * gain
        scales.append(scale)
        pulled.append(norm_grad)
        inner.append(dot((norm_grad * unit).astype(bf16), ones) * (1.0 / HEAD_DIM))
    dmisc_ref[2:3, :] = dmisc_ref[2:3, :] + partial_gain
    dout = [(scale * (grad - one * scale * mean)).astype(bf16) for scale, grad, one, mean in zip(scales, pulled, mixed, inner)]

    def silu_parts(ref, t, h):
        conv = ref[spans[t], lanes_of(h)].astype(f32)
        sig = jax.nn.sigmoid(conv)
        return conv * sig, sig * (1.0 + conv * (1.0 - sig))

    raw_q = [silu_parts(cq_ref, t, h) for t, h in pairs]
    raw_k = [silu_parts(ck_ref, t, h) for t, h in pairs]
    norm_q = [lax.rsqrt(dot((one[0] * one[0]).astype(bf16), ones) + epsilon) for one in raw_q]
    norm_k = [lax.rsqrt(dot((one[0] * one[0]).astype(bf16), ones) + epsilon) for one in raw_k]
    decays = [decay_parts(sp_ref[span, :], rate_ref[...], bias_ref[...]) for span in spans]
    writes = [jax.nn.sigmoid(sp_ref[span, :]) for span in spans]
    queries, keys, fadings, growns, tails, spread_writes, write_packs, ends = [], [], [], [], [], [], [], []
    for n, (t, h) in enumerate(pairs):
        _, total, total_rows = decays[t]
        queries.append(raw_q[n][0] * (norm_q[n] * HEAD_DIM ** -0.5))
        keys.append(raw_k[n][0] * norm_k[n])
        write = jnp.broadcast_to(writes[t][:, heads + h:heads + h + 1], (TILE, HEAD_DIM))
        column = jnp.broadcast_to(total[:, h:h + 1], (TILE, HEAD_DIM))
        gaps = jnp.where(left, column[:SPAN], column[SPAN:]) - total_rows[h:h + 1, :]
        fadings.append(jnp.where(row >= col, jnp.exp(jnp.where(row >= col, gaps, 0.0)), 0.0))
        growns.append(jnp.exp(column))
        tails.append(jnp.exp(last_rows(total, h) - column))
        spread_writes.append(write)
        write_packs.append(jnp.where(left, write[:SPAN], write[SPAN:]))
        ends.append([jnp.exp(total[SPAN * i + SPAN - 1:SPAN * (i + 1), h:h + 1]) for i in range(2)])
    qk = [qk_ref[packs[t], lanes_of(h)].astype(f32) for t, h in pairs]
    score_grads = [dot(spread((qk[n] * fadings[n]).astype(bf16)), dout[n], ((0,), (0,))) for n in range(len(pairs))]
    q_grown = [(queries[n] * growns[n]).astype(bf16) for n in range(len(pairs))]
    k_tail = [(keys[n] * tails[n]).astype(bf16) for n in range(len(pairs))]
    parts = [slice(0, SPAN), slice(SPAN, TILE)]
    q_outs = [[dot(q_grown[n][part], dout[n][part], ((0,), (0,))) for part in parts] for n in range(len(pairs))]

    states = [state_ref[h] for h in range(heads)]
    change_grads = [[None, None] for _ in pairs]
    tail_grads = [[None, None] for _ in pairs]
    end_grads = [[None, None] for _ in pairs]
    for t in reversed(range(tiles)):
        for i in (1, 0):
            part = parts[i]
            here = slice(t * TILE + i * SPAN, t * TILE + (i + 1) * SPAN)
            at = slice((t * 2 + i) * HEAD_DIM, (t * 2 + i + 1) * HEAD_DIM)
            flag = carry_flag(step * rows + t * TILE + i * SPAN, starts_ref)
            lows = [one.astype(bf16) for one in states]
            news = []
            for h in range(heads):
                n = t * heads + h
                news.append((score_grads[n][part] + dot(k_tail[n][part], lows[h])).astype(bf16))
            for h in range(heads):
                n = t * heads + h
                change_grads[n][i] = news[h]
                tail_grads[n][i] = dot(u_ref[here, lanes_of(h)], lows[h], ((1,), (1,)))
                held = jnp.sum(states[h] * s_ref[at, lanes_of(h)].astype(f32), axis=0, keepdims=True)
                end_grads[n][i] = ends[n][i] * jnp.sum(held, axis=1, keepdims=True)
            states = [
                flag * (ends[t * heads + h][i] * states[h] + q_outs[t * heads + h][i] - dot(w_ref[here, lanes_of(h)], news[h], ((0,), (0,))))
                for h in range(heads)
            ]
    for h in range(heads):
        state_ref[h] = states[h]

    change_grads = [jnp.concatenate(one, axis=0) for one in change_grads]
    side_grads = [dot(spread(inv_ref[packs[t], lanes_of(h)]), change_grads[n], ((0,), (0,))) for n, (t, h) in enumerate(pairs)]
    side_low = [one.astype(bf16) for one in side_grads]
    crossed = []
    for n, (t, h) in enumerate(pairs):
        through = []
        for i, part in enumerate(parts):
            at = slice((t * 2 + i) * HEAD_DIM, (t * 2 + i + 1) * HEAD_DIM)
            through.append(dot(jnp.concatenate([side_low[n][part], dout[n][part]], axis=0), s_ref[at, lanes_of(h)], ((1,), (1,))))
        grams = dot(jnp.concatenate([dout[n], side_low[n]], axis=0), u_ref[spans[t], lanes_of(h)], ((1,), (1,)))
        crossed.append((through, grams))
    query_grads, key_grads = [], []
    flat_q = [one.astype(bf16) for one in queries]
    flat_k = [one.astype(bf16) for one in keys]
    products = []
    for n, (t, h) in enumerate(pairs):
        through, grams = crossed[n]
        weighted_grad = -jnp.concatenate([one[:SPAN] for one in through], axis=0)
        grown_grad = jnp.concatenate([one[SPAN:] for one in through], axis=0)
        gram = gram_ref[packs[t], lanes_of(h)].astype(f32)
        pair_grad = halves(grams[:TILE]) * fadings[n]
        strict_grad = jnp.where(row > col, -halves(grams[TILE:]), 0.0) * fadings[n]
        gram_grad = strict_grad * write_packs[n]
        matrix = jnp.concatenate([spread(pair_grad.astype(bf16)), spread(gram_grad.astype(bf16))], axis=0)
        forward = dot(matrix, flat_k[n])
        backward = dot(matrix, jnp.concatenate([flat_q[n], flat_k[n]], axis=0), ((0,), (0,)))
        tail_grad = jnp.concatenate(tail_grads[n], axis=0)
        grown_key = growns[n] * keys[n]
        write = spread_writes[n]
        query_grads.append(forward[:TILE] + grown_grad * growns[n])
        key_grads.append(forward[TILE:] + backward + tail_grad * tails[n] + weighted_grad * write * growns[n])
        value = cv_ref[spans[t], lanes_of(h)].astype(f32)
        value = value * jax.nn.sigmoid(value)
        moving = pair_grad * qk[n] + gram_grad * gram
        inner_key = weighted_grad * grown_key
        products.append((
            spread(strict_grad * gram) + inner_key + side_grads[n] * value,
            spread(moving) + grown_grad * growns[n] * queries[n] + inner_key * write,
            tail_grad * tails[n] * keys[n],
            jnp.sum(moving, axis=0, keepdims=True),
        ))
    sums = [[row_sums(one, ones_tall) for one in three[:3]] for three in products]
    upper = jnp.where((full_row <= full_col) & same, 1.0, 0.0)
    lower = jnp.where((full_row > full_col) & same, 1.0, 0.0)
    for t in range(tiles):
        gap_grad = jnp.zeros((TILE, HEAD_DIM), f32)
        tail_sum = jnp.zeros((TILE, HEAD_DIM), f32)
        write_grad = jnp.zeros((TILE, HEAD_DIM), f32)
        ends_grad = jnp.zeros((TILE, HEAD_DIM), f32)
        across = jnp.zeros((TILE, HEAD_DIM), f32)
        for h in range(heads):
            n = t * heads + h
            mine = full_col == h
            gap_grad = jnp.where(mine, sums[n][1], gap_grad)
            tail_sum = jnp.where(mine, sums[n][2], tail_sum)
            write_grad = jnp.where(full_col == heads + h, sums[n][0], write_grad)
            across = jnp.where(full_row == h, products[n][3], across)
            ends_grad = jnp.where(mine, jnp.where(full_row < SPAN, end_grads[n][0], end_grads[n][1]), ends_grad)
        log_grad = dot(upper, gap_grad - across.T, precise=True) + dot(lower, tail_sum, precise=True) + ends_grad
        scalars = sp_ref[spans[t], :]
        rate = -jnp.exp(rate_ref[...])
        inside = log_grad * rate * jax.nn.sigmoid(scalars + bias_ref[...])
        write = writes[t]
        out = jnp.where(full_col < heads, inside, write_grad * write * (1.0 - write))
        dsp_ref[spans[t], :] = jnp.where(full_col < 2 * heads, out, 0.0).astype(bf16)
        dmisc_ref[0:1, :] = dmisc_ref[0:1, :] + jnp.sum(log_grad * decays[t][0], axis=0, keepdims=True)
        dmisc_ref[1:2, :] = dmisc_ref[1:2, :] + jnp.sum(inside, axis=0, keepdims=True)

    inner_q = [dot((query_grads[n] * raw_q[n][0]).astype(bf16), ones) for n in range(len(pairs))]
    inner_k = [dot((key_grads[n] * raw_k[n][0]).astype(bf16), ones) for n in range(len(pairs))]
    for n, (t, h) in enumerate(pairs):
        scale = norm_q[n]
        grad = (query_grads[n] - raw_q[n][0] * (scale * scale * inner_q[n])) * (scale * HEAD_DIM ** -0.5)
        ext_ref[0, spans[t], lanes_of(h)] = grad * raw_q[n][1]
        scale = norm_k[n]
        grad = (key_grads[n] - raw_k[n][0] * (scale * scale * inner_k[n])) * scale
        ext_ref[1, spans[t], lanes_of(h)] = grad * raw_k[n][1]
        ext_ref[2, spans[t], lanes_of(h)] = side_grads[n] * spread_writes[n] * silu_parts(cv_ref, t, h)[1]
    place, _, end = row_places(step * rows, rows, starts_ref)
    masks = [None] + [jnp.where(place + j < end, 1.0, 0.0) for j in range(1, CONV)]
    for which, source in enumerate((q_ref, k_ref, v_ref)):
        for h in range(heads):
            lanes = lanes_of(h)
            proj = source[:, lanes].astype(f32)
            total = None
            for j in range(CONV):
                moved = ext_ref[which, j:j + rows, lanes]
                if j:
                    moved = moved * masks[j]
                at = which * CONV + j
                dtaps_ref[at:at + 1, lanes] = dtaps_ref[at:at + 1, lanes] + jnp.sum(proj * moved, axis=0, keepdims=True)
                term = moved * taps_ref[at:at + 1, lanes]
                total = term if total is None else total + term
            flat_ref[:, lanes_of(which * heads + h)] = total.astype(bf16)
        ext_ref[which, rows:, :] = ext_ref[which, :8, :]


def mixer_backward(count, starts, gg, gate, q, k, v, sp, kept, taps, rate, bias, gain):
    mixed, cq, ck, cv, inv, qk, gram, w, u, s = kept
    rows, width = q.shape
    heads = width // HEAD_DIM
    block = rows // count
    tiles = block // TILE
    spec = lambda r, w: blocked(r, w, lambda i: count - 1 - i)
    wide, half, state, scal = spec(block, width), spec(block // 2, width), spec(block * 2, width), spec(block, HEAD_DIM)
    shape = lambda r: jax.ShapeDtypeStruct((r, width), bf16)
    return pl.pallas_call(
        partial(backward_kernel, tiles, heads),
        grid_spec=pltpu.PrefetchScalarGridSpec(
            num_scalar_prefetch=1,
            grid=(count,),
            in_specs=[wide] * 9 + [scal] + [half] * 3 + [wide] * 2 + [state] + [constant(a.shape) for a in (taps, rate, bias, gain)],
            out_specs=[spec(block, 4 * width), scal, constant((3 * CONV, width)), constant((8, HEAD_DIM))],
            scratch_shapes=[pltpu.VMEM((3, block + 8, width), f32), pltpu.VMEM((heads, HEAD_DIM, HEAD_DIM), f32)],
        ),
        out_shape=[
            jax.ShapeDtypeStruct((rows, 4 * width), bf16),
            jax.ShapeDtypeStruct((rows, HEAD_DIM), bf16),
            jax.ShapeDtypeStruct((3 * CONV, width), f32),
            jax.ShapeDtypeStruct((8, HEAD_DIM), f32),
        ],
        compiler_params=pltpu.CompilerParams(dimension_semantics=("arbitrary",), vmem_limit_bytes=VMEM_BYTES),
        cost_estimate=SMALL,
    )(starts, gg, mixed, gate, cq, ck, cv, q, k, v, sp, inv, qk, gram, w, u, s, taps, rate, bias, gain)


def after(values, *others):
    single = not isinstance(values, (list, tuple))
    values = [values] if single else list(values)
    others = [one for one in others if one is not None]
    out = pl.pallas_call(
        lambda *refs: None,
        out_shape=[jax.ShapeDtypeStruct(one.shape, one.dtype) for one in values],
        in_specs=[pl.BlockSpec(memory_space=pl.ANY)] * (len(values) + len(others)),
        out_specs=[pl.BlockSpec(memory_space=pl.ANY)] * len(values),
        input_output_aliases={i: i for i in range(len(values))},
    )(*values, *others)
    return out[0] if single else list(out)


def once(shape):
    return pl.BlockSpec(shape, lambda *_: (0,) * len(shape), pipeline_mode=pl.Buffered(1))


def params():
    return pltpu.CompilerParams(dimension_semantics=("arbitrary",), vmem_limit_bytes=VMEM_BYTES)


def project_kernel(pieces, *refs):
    gain_ref, weights, outs = refs[pieces], refs[pieces + 1:pieces + 6], refs[-6:]
    x = whole(refs[:pieces]).astype(f32)
    scale = lax.rsqrt(jnp.mean(x * x, axis=-1, keepdims=True) + epsilon)
    normed = (x * scale * gain_ref[...]).astype(bf16)
    outs[5][...] = normed
    for weight, out in zip(weights, outs[:5]):
        out[...] = dot(normed, weight[...]).astype(out.dtype)


def project(pieces, at, total, gain, weights, held):
    rows, depth = sum(one.shape[0] for one in pieces), pieces[0].shape[1]
    first, count = at // rows, len(pieces)
    shapes = [jax.ShapeDtypeStruct((total, w.shape[1]), f32 if i == 4 else bf16) for i, w in enumerate(weights)]
    shapes.append(jax.ShapeDtypeStruct((total, depth), bf16))
    return pl.pallas_call(
        partial(project_kernel, count),
        grid=(1,),
        in_specs=[once(one.shape) for one in pieces]
        + [once(gain.shape)]
        + [once(w.shape) for w in weights]
        + [pl.BlockSpec(memory_space=pl.ANY)] * len(held),
        out_specs=[pl.BlockSpec((rows, s.shape[1]), lambda i: (first, 0)) for s in shapes],
        out_shape=shapes,
        input_output_aliases={count + 6 + i: i for i in range(len(held))},
        compiler_params=params(),
        cost_estimate=SMALL,
    )(*pieces, gain, *weights, *held)


def pick(count, refs, held):
    step = pl.program_id(0)
    for which in range(count):
        @pl.when(step == which)
        def _():
            held[...] = whole(refs[which]) if isinstance(refs[which], (list, tuple)) else refs[which][...]


def middle_kernel(sizes, rank_ref, *refs):
    count = len(sizes)
    x_refs, refs = split_pieces(refs, sizes)
    g_refs = refs[:count]
    weight_ref, gain_ref, normed_ref, own_ref, scr, x_scr = refs[count:]
    pick(count, x_refs, x_scr)
    gated = jnp.concatenate([one[...] for one in g_refs], axis=1)
    width = gated.shape[1] // count
    for a, b in column_cuts(scr.shape[1]):
        weight = [weight_ref[:, rank_ref[0] ^ m, :, a:b].reshape(width, b - a) for m in range(count)]
        scr[:, a:b] = dot(gated, jnp.concatenate(weight, axis=0)) + x_scr[:, a:b].astype(f32)
    middle = scr[...]
    scale = lax.rsqrt(jnp.mean(middle * middle, axis=-1, keepdims=True) + epsilon)
    normed_ref[...] = (middle * scale * gain_ref[...]).astype(bf16)

    @pl.when(pl.program_id(0) == 0)
    def _():
        own_ref[...] = middle


def middle_rows(rank, x_parts, gated_parts, weight, gain):
    count = len(x_parts)
    rows, depth = x_parts[0][0].shape
    width = gated_parts[0].shape[1]
    flat = [one for part in x_parts for one in part]
    return pl.pallas_call(
        partial(middle_kernel, [len(part) for part in x_parts]),
        grid_spec=pltpu.PrefetchScalarGridSpec(
            num_scalar_prefetch=1,
            grid=(count,),
            in_specs=[once(one.shape) for one in flat]
            + [pl.BlockSpec((rows, width), lambda i, s, at=at: (i ^ at, 0)) for at in range(count)]
            + [once(weight.shape), once(gain.shape)],
            out_specs=[pl.BlockSpec((rows, depth), lambda i, s: (i, 0)), once((rows, depth))],
            scratch_shapes=[pltpu.VMEM((rows, depth), f32), pltpu.VMEM((rows, depth), bf16)],
        ),
        out_shape=[jax.ShapeDtypeStruct((count * rows, depth), bf16), jax.ShapeDtypeStruct((rows, depth), f32)],
        compiler_params=params(),
        cost_estimate=SMALL,
    )(rank, *flat, *gated_parts, weight, gain)


def gated_grad_kernel(rank_ref, rows_ref, weight_ref, *refs):
    refs[-1][...] = dot(rows_ref[...], weight_ref[...], ((1,), (1,))).astype(bf16)


def gated_grads(count, rank, gathered, weight, *others):
    rows, depth = gathered.shape[0] // count, gathered.shape[1]
    width = weight.shape[0]
    return pl.pallas_call(
        gated_grad_kernel,
        grid_spec=pltpu.PrefetchScalarGridSpec(
            num_scalar_prefetch=1,
            grid=(count,),
            in_specs=[pl.BlockSpec((rows, depth), lambda i, s: (i ^ s[0], 0)), once(weight.shape)]
            + [pl.BlockSpec(memory_space=pl.ANY)] * len(others),
            out_specs=pl.BlockSpec((rows, width), lambda i, s: (i, 0)),
        ),
        out_shape=jax.ShapeDtypeStruct((count * rows, width), bf16),
        compiler_params=params(),
        cost_estimate=SMALL,
    )(rank, gathered, weight, *others)


def column_cuts(width, chunk=512):
    return [(lo, min(lo + chunk, width)) for lo in range(0, width, chunk)]


def hidden_kernel(x_ref, wg_ref, wu_ref, *refs):
    gate_ref, up_ref, hidden_ref = refs[-3:]
    x = x_ref[...]
    for a, b in column_cuts(wg_ref.shape[1]):
        gate, up = dot(x, wg_ref[:, a:b]), dot(x, wu_ref[:, a:b])
        gate_ref[:, a:b] = gate.astype(bf16)
        up_ref[:, a:b] = up.astype(bf16)
        hidden_ref[:, a:b] = (gate * jax.nn.sigmoid(gate) * up).astype(bf16)


def hidden_units(x, gate_weight, up_weight, *others):
    rows, depth = x.shape
    width = gate_weight.shape[1]
    block = rows // 4
    out = pl.BlockSpec((block, width), lambda i: (i, 0))
    return pl.pallas_call(
        hidden_kernel,
        grid=(4,),
        in_specs=[pl.BlockSpec((block, depth), lambda i: (i, 0)), once(gate_weight.shape), once(up_weight.shape)]
        + [pl.BlockSpec(memory_space=pl.ANY)] * len(others),
        out_specs=[out] * 3,
        out_shape=[jax.ShapeDtypeStruct((rows, width), bf16)] * 3,
        compiler_params=params(),
        cost_estimate=SMALL,
    )(x, gate_weight, up_weight, *others)


def whole(refs):
    values = [one[...] for one in refs]
    return values[0] if len(values) == 1 else jnp.concatenate(values, axis=0)


def outer_kernel(parts, info_ref, *refs):
    total, at = None, 0
    for count in parts:
        term = dot(whole(refs[at:at + count]), refs[at + count][...], ((0,), (0,)))
        total = term if total is None else total + term
        at += count + 1
    refs[-1][...] = total.astype(bf16)


def half_column(count, own):
    return lambda i, s: (s[0] if own else 1 - s[0]) * count + i


def outer_half(info, own, sides, *others):
    lefts, right = sides[0]
    half, block = lefts[0].shape[1] // 2, 2 * TILE
    count, units = half // block, right.shape[1]
    column = half_column(count, own)
    in_specs, values = [], []
    for lefts, right in sides:
        in_specs += [pl.BlockSpec((one.shape[0], block), lambda i, s: (0, column(i, s))) for one in lefts] + [once(right.shape)]
        values += list(lefts) + [right]
    return pl.pallas_call(
        partial(outer_kernel, [len(lefts) for lefts, _ in sides]),
        grid_spec=pltpu.PrefetchScalarGridSpec(
            num_scalar_prefetch=1,
            grid=(count,),
            in_specs=in_specs + [pl.BlockSpec(memory_space=pl.ANY)] * len(others),
            out_specs=pl.BlockSpec((block, units), lambda i, s: (i, 0)),
        ),
        out_shape=jax.ShapeDtypeStruct((half, units), bf16),
        compiler_params=params(),
        cost_estimate=SMALL,
    )(info, *values, *others)


def split_pieces(refs, sizes):
    pieces, at = [], 0
    for size in sizes:
        pieces.append(refs[at:at + size])
        at += size
    return pieces, refs[at:]


def hidden_grad_kernel(sizes, rank_ref, *refs):
    c_refs, refs = split_pieces(refs, sizes)
    gate_ref, up_ref, wg_ref, wu_ref, wd_ref = refs[:5]
    gg_ref, ug_ref, mid_ref, held = refs[-4:]
    pick(len(sizes), c_refs, held)
    grad_rows = held[...]
    nt = ((1,), (1,))
    for a, b in column_cuts(wg_ref.shape[1]):
        grad = dot(grad_rows, wd_ref[a:b, :], nt)
        gate, up = gate_ref[:, a:b].astype(f32), up_ref[:, a:b].astype(f32)
        sig = jax.nn.sigmoid(gate)
        gg_ref[:, a:b] = (grad * up * sig * (1.0 + gate * (1.0 - sig))).astype(bf16)
        ug_ref[:, a:b] = (grad * gate * sig).astype(bf16)
    gate_grad, up_grad = gg_ref[...], ug_ref[...]
    for a, b in column_cuts(wg_ref.shape[0]):
        mid_ref[:, a:b] = (dot(gate_grad, wg_ref[a:b, :], nt) + dot(up_grad, wu_ref[a:b, :], nt)).astype(bf16)


def hidden_grads(rank, cot_parts, gates, ups, gate_weight, up_weight, down_weight, *others):
    count = len(cot_parts)
    rows, depth = cot_parts[0][0].shape
    width = gate_weight.shape[1]
    spec = pl.BlockSpec((rows, width), lambda i, s: (i, 0))
    flat = [one for part in cot_parts for one in part]
    return pl.pallas_call(
        partial(hidden_grad_kernel, [len(part) for part in cot_parts]),
        grid_spec=pltpu.PrefetchScalarGridSpec(
            num_scalar_prefetch=1,
            grid=(count,),
            in_specs=[once(one.shape) for one in flat]
            + [spec] * 2
            + [once(gate_weight.shape), once(up_weight.shape), once(down_weight.shape)]
            + [pl.BlockSpec(memory_space=pl.ANY)] * len(others),
            out_specs=[spec, spec, pl.BlockSpec((rows, depth), lambda i, s: (i ^ s[0], 0))],
            scratch_shapes=[pltpu.VMEM((rows, depth), bf16)],
        ),
        out_shape=[jax.ShapeDtypeStruct((count * rows, width), bf16)] * 2 + [jax.ShapeDtypeStruct((count * rows, depth), bf16)],
        compiler_params=params(),
        cost_estimate=SMALL,
    )(rank, *flat, gates, ups, gate_weight, up_weight, down_weight, *others)


def input_grad_kernel(rank_ref, grad_ref, scalar_ref, *refs):
    weights, out = refs[:5], refs[-1]
    grad = jnp.concatenate([grad_ref[...], scalar_ref[...]], axis=1)
    for a, b in column_cuts(out.shape[1]):
        weight = jnp.concatenate([one[a:b, :] for one in weights], axis=1)
        out[:, a:b] = dot(grad, weight, ((1,), (1,))).astype(bf16)


def input_grads(count, rank, grad, scalar_grad, weights, *others):
    rows, depth = grad.shape[0] // count, weights[0].shape[0]
    return pl.pallas_call(
        input_grad_kernel,
        grid_spec=pltpu.PrefetchScalarGridSpec(
            num_scalar_prefetch=1,
            grid=(count,),
            in_specs=[pl.BlockSpec((rows, one.shape[1]), lambda i, s: (i, 0)) for one in (grad, scalar_grad)]
            + [once(one.shape) for one in weights]
            + [pl.BlockSpec(memory_space=pl.ANY)] * len(others),
            out_specs=pl.BlockSpec((rows, depth), lambda i, s: (i ^ s[0], 0)),
        ),
        out_shape=jax.ShapeDtypeStruct((count * rows, depth), bf16),
        compiler_params=params(),
        cost_estimate=SMALL,
    )(rank, grad, scalar_grad, *weights, *others)


def result_kernel(rank_ref, hidden_ref, weight_ref, *refs):
    out = refs[-1]
    for a, b in column_cuts(out.shape[1]):
        out[:, a:b] = dot(hidden_ref[...], weight_ref[:, a:b]).astype(bf16)


def result_rows(count, rank, hidden, weight, *others):
    rows, depth = hidden.shape[0] // count, weight.shape[1]
    return pl.pallas_call(
        result_kernel,
        grid_spec=pltpu.PrefetchScalarGridSpec(
            num_scalar_prefetch=1,
            grid=(count,),
            in_specs=[pl.BlockSpec((rows, hidden.shape[1]), lambda i, s: (i, 0)), once(weight.shape)]
            + [pl.BlockSpec(memory_space=pl.ANY)] * len(others),
            out_specs=pl.BlockSpec((rows, depth), lambda i, s: (i ^ s[0], 0)),
        ),
        out_shape=jax.ShapeDtypeStruct((count * rows, depth), bf16),
        compiler_params=params(),
        cost_estimate=SMALL,
    )(rank, hidden, weight, *others)


def small_call(kernel, outs, *values):
    return pl.pallas_call(
        kernel,
        out_shape=outs,
        compiler_params=pltpu.CompilerParams(vmem_limit_bytes=VMEM_BYTES),
        cost_estimate=SMALL,
    )(*values)


def merge_kernel(across_ref, down_ref, top_ref, low_ref, *refs):
    half = top_ref.shape[0]
    across_out, down_out = refs[-2:]
    down_out[:half] = (down_ref[:half].astype(f32) + top_ref[...].astype(f32)).astype(bf16)
    down_out[half:] = down_ref[half:]
    across_out[:half] = across_ref[:half]
    across_out[half:] = (across_ref[half:].astype(f32) + low_ref[...].astype(f32)).astype(bf16)


def halves_kernel(across_ref, down_ref, top_out, low_out):
    top_out[...] = down_ref[...]
    low_out[...] = across_ref[...]


def far_halves(across, down):
    rows, columns = across.shape[0] // 2, across.shape[1]
    top, low = pl.BlockSpec((rows, columns), lambda i: (0, 0)), pl.BlockSpec((rows, columns), lambda i: (1, 0))
    return pl.pallas_call(
        halves_kernel,
        grid=(1,),
        in_specs=[low, top],
        out_specs=[top, top],
        out_shape=[jax.ShapeDtypeStruct((rows, columns), across.dtype)] * 2,
        compiler_params=params(),
        cost_estimate=SMALL,
    )(across, down)


def norm_grad_kernel(count, *refs):
    terms, (x_ref, cot_ref, gain_ref, grad_out, low_out, gain_out) = refs[:count], refs[count:]
    grad = terms[0][...].astype(f32)
    for one in terms[1:]:
        grad = grad + one[...].astype(f32)
    x = x_ref[...].astype(f32)
    scale = lax.rsqrt(jnp.mean(x * x, axis=-1, keepdims=True) + epsilon)
    unit = x * scale
    gain_out[...] = jnp.sum(grad * unit, axis=0, keepdims=True)
    inner = grad * gain_ref[...]
    total = cot_ref[...].astype(f32) + scale * (inner - unit * jnp.mean(inner * unit, axis=-1, keepdims=True))
    if grad_out is not None:
        grad_out[...] = total
    low_out[...] = total.astype(bf16)


def norm_grad(terms, x, cot, gain):
    rows, depth = x.shape
    return small_call(
        partial(norm_grad_kernel, len(terms)),
        [jax.ShapeDtypeStruct((rows, depth), f32), jax.ShapeDtypeStruct((rows, depth), bf16), jax.ShapeDtypeStruct((1, depth), f32)],
        *terms, x, cot, gain,
    )


def total_kernel(*refs):
    refs[-1][...] = (refs[0][...] + refs[1][...].astype(f32)).astype(bf16)


def wide_call(kernel, out_dtype, values, *others):
    rows, columns = values[0].shape
    block = next(size for size in (256, 128, 64, 32, 16) if rows % size == 0)
    spec = pl.BlockSpec((block, columns), lambda i, *_: (i, 0))
    return pl.pallas_call(
        kernel,
        grid=(rows // block,),
        in_specs=[spec] * len(values) + [pl.BlockSpec(memory_space=pl.ANY)] * len(others),
        out_specs=spec,
        out_shape=jax.ShapeDtypeStruct((rows, columns), out_dtype),
        compiler_params=params(),
        cost_estimate=SMALL,
    )(*values, *others)


def add_kernel(left, right, *refs):
    refs[-1][...] = (left[...].astype(f32) + right[...].astype(f32)).astype(bf16)


def cast_kernel(value, *refs):
    refs[-1][...] = value[...].astype(f32)


def choose_kernel(flag_ref, left, right, *refs):
    refs[-1][...] = jnp.where(flag_ref[0] == 1, left[...], right[...])


def choose(flag, left, right, *others):
    rows, columns = left.shape
    block = next(size for size in (256, 128, 64, 32, 16) if rows % size == 0)
    spec = pl.BlockSpec((block, columns), lambda i, s: (i, 0))
    return pl.pallas_call(
        choose_kernel,
        grid_spec=pltpu.PrefetchScalarGridSpec(
            num_scalar_prefetch=1,
            grid=(rows // block,),
            in_specs=[spec, spec] + [pl.BlockSpec(memory_space=pl.ANY)] * len(others),
            out_specs=spec,
        ),
        out_shape=jax.ShapeDtypeStruct((rows, columns), left.dtype),
        compiler_params=params(),
        cost_estimate=SMALL,
    )(flag, left, right, *others)


def head_outer_kernel(parts, info_ref, *refs):
    attn, (gated_ref, in_ref, flat_ref, scalar_ref) = refs[:parts], refs[parts:parts + 4]
    one, two = refs[-2:]
    units = one.shape[1]
    tn = ((0,), (0,))
    left = in_ref[...]
    columns = [dot(whole(attn), gated_ref[...], tn), dot(left, flat_ref[...], tn), dot(left, scalar_ref[...], tn)]
    joined = jnp.concatenate([one.astype(bf16) for one in columns], axis=1)
    spare = 2 * units - joined.shape[1]
    if spare:
        joined = jnp.concatenate([joined, jnp.zeros((joined.shape[0], spare), bf16)], axis=1)
    one[...] = joined[:, :units]
    two[...] = joined[:, units:]


def head_outer(info, own, parts, attn, gated, normed, flat, scalar, units, *others):
    tokens, width = normed.shape
    half, block = width // 2, 2 * TILE
    count, rows = half // block, tokens // parts
    column = half_column(count, own)
    attn_specs = [pl.BlockSpec((rows, block), lambda i, s, m=m: (s[2] ^ m, column(i, s))) for m in range(parts)]
    out = pl.BlockSpec((block, units), lambda i, s: (i, 0))
    return pl.pallas_call(
        partial(head_outer_kernel, parts),
        grid_spec=pltpu.PrefetchScalarGridSpec(
            num_scalar_prefetch=1,
            grid=(count,),
            in_specs=attn_specs
            + [once(gated.shape), pl.BlockSpec((tokens, block), lambda i, s: (0, column(i, s))), once(flat.shape), once(scalar.shape)]
            + [pl.BlockSpec(memory_space=pl.ANY)] * len(others),
            out_specs=[out, out],
        ),
        out_shape=[jax.ShapeDtypeStruct((half, units), bf16)] * 2,
        compiler_params=params(),
        cost_estimate=SMALL,
    )(info, *[attn] * parts, gated, normed, flat, scalar, *others)


SLAB = 128


def summed(refs):
    total = refs[0][...].astype(f32)
    for one in refs[1:]:
        total = total + one[...].astype(f32)
    return total


def line_start_kernel(count, info_ref, *refs):
    refs[-1][...] = summed(refs[:count]).astype(bf16)


def line_step_kernel(now_count, later_count, info_ref, *refs):
    now, later, refs = refs[:now_count], refs[now_count:now_count + later_count], refs[now_count + later_count:]
    right_sent, left_sent, right_came, left_came = refs[:4]
    result_ref, right_ref, left_ref = refs[-3:]
    center, upper = info_ref[1] == 1, info_ref[3] == 1
    add = lambda one, two: one[...].astype(f32) + two[...].astype(f32)

    @pl.when(jnp.logical_not(center))
    def _():
        value = summed(later or now).astype(bf16)
        right_ref[...] = value
        left_ref[...] = value
        result_ref[...] = jnp.where(upper, right_came[...], left_came[...])

    @pl.when(center & upper)
    def _():
        result_ref[...] = right_sent[...]
        right_ref[...] = add(left_sent, right_came).astype(bf16)
        left_ref[...] = (summed(now) + left_came[...].astype(f32)).astype(bf16)

    @pl.when(center & jnp.logical_not(upper))
    def _():
        result_ref[...] = left_sent[...]
        left_ref[...] = add(right_sent, left_came).astype(bf16)
        right_ref[...] = (summed(now) + right_came[...].astype(f32)).astype(bf16)


class Line:
    def __init__(self, info, rows, chunks):
        self.info, self.rows, self.chunks, self.step = info, rows, chunks, 0
        size = lax.axis_size("dp")
        self.stride = size // 4
        self.sent = self.came = None
        self.results = []

    def send(self, right, left):
        count, step = len(self.chunks), self.step
        inner, middle, outer_hop = step < count, 1 <= step <= count, step >= 2
        hops = lambda pairs: [(j + a * self.stride, j + b * self.stride) for a, b in pairs for j in range(self.stride)]
        rightward = [(0, 1)] * inner + [(1, 2)] * middle + [(2, 3)] * outer_hop
        leftward = [(3, 2)] * inner + [(2, 1)] * middle + [(1, 0)] * outer_hop
        self.sent = (right, left)
        self.came = (lax.ppermute(right, "dp", hops(rightward)), lax.ppermute(left, "dp", hops(leftward)))

    def land(self, *others):
        self.came = tuple(after(list(self.came), *others))
        return self.came[0]

    def begin(self, *others):
        *sources, row = self.chunks[0]()
        units = sources[0].shape[1]
        spec = pl.BlockSpec((SLAB, units), lambda i, s: (row * (self.rows // SLAB) + i, 0))
        value = pl.pallas_call(
            partial(line_start_kernel, len(sources)),
            grid_spec=pltpu.PrefetchScalarGridSpec(
                num_scalar_prefetch=1,
                grid=(self.rows // SLAB,),
                in_specs=[spec] * len(sources) + [pl.BlockSpec(memory_space=pl.ANY)] * len(others),
                out_specs=pl.BlockSpec((SLAB, units), lambda i, s: (i, 0)),
            ),
            out_shape=jax.ShapeDtypeStruct((self.rows, units), bf16),
            compiler_params=params(),
            cost_estimate=SMALL,
        )(self.info, *sources, *others)
        self.send(value, value)
        return value

    def advance(self, *others):
        count, step = len(self.chunks), self.step
        *now, first = self.chunks[min(step, count - 1)]()
        *later, second = self.chunks[min(step + 1, count - 1)]()
        per = self.rows // SLAB
        units = now[0].shape[1]
        if now[0] is later[0]:
            later = []
            specs = [pl.BlockSpec((SLAB, units), lambda i, s: (jnp.where(s[1] == 1, first, second) * per + i, 0))] * len(now)
        else:
            specs = [pl.BlockSpec((SLAB, units), lambda i, s: (first * per + i, 0))] * len(now)
            specs += [pl.BlockSpec((SLAB, units), lambda i, s: (second * per + i, 0))] * len(later)
        slab = pl.BlockSpec((SLAB, units), lambda i, s: (i, 0))
        result, right, left = pl.pallas_call(
            partial(line_step_kernel, len(now), len(later)),
            grid_spec=pltpu.PrefetchScalarGridSpec(
                num_scalar_prefetch=1,
                grid=(per,),
                in_specs=specs + [slab] * 4 + [pl.BlockSpec(memory_space=pl.ANY)] * len(others),
                out_specs=[slab] * 3,
            ),
            out_shape=[jax.ShapeDtypeStruct((self.rows, units), bf16)] * 3,
            compiler_params=params(),
            cost_estimate=SMALL,
        )(self.info, *now, *later, *self.sent, *self.came, *others)
        self.step += 1
        if step >= 2:
            self.results.append(result)
        if self.step < count + 2:
            self.send(right, left)
        return result


def place_kernel(turned, info_ref, mine_ref, other_ref, *refs):
    value = jnp.where(pl.program_id(0) == info_ref[0], mine_ref[...], other_ref[...]).astype(f32)
    refs[-2][...] = value.T if turned else value
    refs[-1][...] = jnp.zeros(refs[-1].shape, f32)


def place(info, held, shape, mine, other, row, turned, *others):
    rows, units = mine.shape
    block = 2 * TILE
    per, inner = (shape[1] if turned else shape[0]) // 2 // block, rows // block
    both = pl.BlockSpec((block, units), lambda i, j, s: (j, 0))
    if turned:
        out = pl.BlockSpec((units, block), lambda i, j, s: (0, i * per + row * inner + j))
    else:
        out = pl.BlockSpec((block, units), lambda i, j, s: (i * per + row * inner + j, 0))
    extra = ([] if held is None else [held]) + list(others)
    return pl.pallas_call(
        partial(place_kernel, turned),
        grid_spec=pltpu.PrefetchScalarGridSpec(
            num_scalar_prefetch=1,
            grid=(2, inner),
            in_specs=[both, both] + [pl.BlockSpec(memory_space=pl.ANY)] * len(extra),
            out_specs=[out, pl.BlockSpec((8, HEAD_DIM), lambda i, j, s: (0, 0))],
        ),
        out_shape=[jax.ShapeDtypeStruct(shape, f32), jax.ShapeDtypeStruct((8, HEAD_DIM), f32)],
        input_output_aliases={} if held is None else {3: 0},
        compiler_params=pltpu.CompilerParams(dimension_semantics=("arbitrary", "arbitrary"), vmem_limit_bytes=VMEM_BYTES),
        cost_estimate=SMALL,
    )(info, mine, other, *extra)


def place_heads_kernel(info_ref, *refs):
    own = pl.program_id(0) == info_ref[0]
    one = jnp.where(own, refs[0][...], refs[2][...]).astype(f32)
    two = jnp.where(own, refs[1][...], refs[3][...]).astype(f32)
    out, query, key, value, gate, scalars, token = refs[-7:]
    token[...] = jnp.zeros(token.shape, f32)
    local, units = query.shape[1], one.shape[1]
    out[...] = one[:, :local].T
    query[...] = one[:, local:2 * local]
    cut = units - 2 * local
    key[:, :cut] = one[:, 2 * local:]
    key[:, cut:] = two[:, :local - cut]
    at = local - cut
    value[...] = two[:, at:at + local]
    gate[...] = two[:, at + local:at + 2 * local]
    scalars[...] = two[:, at + 2 * local:at + 2 * local + HEAD_DIM]


def place_heads(info, held, width, local, mine, other, row):
    rows, units = mine[0].shape
    block = 2 * TILE
    per, inner = width // 2 // block, rows // block
    both = pl.BlockSpec((block, units), lambda i, j, s: (j, 0))
    tall = lambda columns: pl.BlockSpec((block, columns), lambda i, j, s: (i * per + row * inner + j, 0))
    return pl.pallas_call(
        place_heads_kernel,
        grid_spec=pltpu.PrefetchScalarGridSpec(
            num_scalar_prefetch=1,
            grid=(2, inner),
            in_specs=[both] * 4 + [pl.BlockSpec(memory_space=pl.ANY)] * len(held),
            out_specs=[pl.BlockSpec((local, block), lambda i, j, s: (0, i * per + row * inner + j))] + [tall(local)] * 4 + [tall(HEAD_DIM), pl.BlockSpec((8, HEAD_DIM), lambda i, j, s: (0, 0))],
        ),
        out_shape=[jax.ShapeDtypeStruct((local, width), f32)]
        + [jax.ShapeDtypeStruct((width, local), f32)] * 4
        + [jax.ShapeDtypeStruct((width, HEAD_DIM), f32), jax.ShapeDtypeStruct((8, HEAD_DIM), f32)],
        input_output_aliases={5 + i: i for i in range(len(held))},
        compiler_params=pltpu.CompilerParams(dimension_semantics=("arbitrary", "arbitrary"), vmem_limit_bytes=VMEM_BYTES),
        cost_estimate=SMALL,
    )(info, *mine, *other, *held)


def xor_pairs(size, mask):
    return [(i, i ^ mask) for i in range(size)]


def swap(values, axis, mask):
    return lax.ppermute(values, axis, xor_pairs(lax.axis_size(axis), mask))


def gather_rows(mine, *others):
    size = lax.axis_size("tp")
    if size != 4:
        parts, mask = [mine], 1
        while mask < size:
            parts = parts + [swap(one, "tp", mask) for one in parts]
            mask *= 2
        return [[one] for one in parts]
    across, down = after([swap(mine, "tp", 1), swap(mine, "tp", 2)], *others)
    top, low = far_halves(across, down)
    return [[mine], [across], [down], [swap(top, "tp", 1), swap(low, "tp", 2)]]


def joined(part):
    return part[0] if len(part) == 1 else jnp.concatenate(part, axis=0)


def gather_weight(weight):
    places, count = lax.axis_size("dp"), lax.axis_size("tp")
    rows = weight.shape[0] // places
    piece = lax.dynamic_slice_in_dim(weight, lax.axis_index("dp") * rows, rows, axis=0)
    return lax.all_gather(piece, ("dp", "tp"), axis=0, tiled=True).reshape(places, count, rows, weight.shape[1])


def sum_over(values, axis):
    for i in range(lax.axis_size(axis).bit_length() - 1):
        values = values + swap(values, axis, 1 << i)
    return values


def body(
    tokens,
    seq_lengths,
    out_cotangent,
    attn_norm_gain,
    query_weight,
    key_weight,
    value_weight,
    out_gate_weight,
    head_scalar_weight,
    conv_weight,
    decay_log,
    decay_bias,
    head_norm_gain,
    output_weight,
    mlp_norm_gain,
    mlp_gate_weight,
    mlp_up_weight,
    mlp_down_weight,
):
    rows, width = tokens.shape[1:]
    half = width // 2
    heads = decay_log.shape[0]
    local = output_weight.shape[0]
    units = mlp_gate_weight.shape[1]
    place_at = lax.axis_index("dp") // (lax.axis_size("dp") // 4)
    core = (lax.axis_index("dp") % 2).astype(jnp.int32)
    rank = lax.axis_index("tp").astype(jnp.int32)
    lengths = seq_lengths[0]
    center = (place_at == 1) | (place_at == 2)
    info = jnp.stack([core, center.astype(jnp.int32), rank, (place_at >= 2).astype(jnp.int32)])
    lines = lax.axis_size("dp") == 8 and units % HEAD_DIM == 0
    starts = jnp.stack([rank, lengths[0], lengths[0] + lengths[1]])

    count = lax.axis_size("tp")
    total = count * rows
    scalar_weight = jnp.pad(
        jnp.transpose(head_scalar_weight, (0, 2, 1)).reshape(width, 2 * heads), ((0, 0), (0, HEAD_DIM - 2 * heads))
    )
    pad_row = lambda row: jnp.pad(row, (0, HEAD_DIM - heads))[None]
    rates, biases = pad_row(decay_log), pad_row(decay_bias)
    taps = conv_weight.reshape(3 * CONV, -1)
    in_weights = (query_weight, key_weight, value_weight, out_gate_weight, scalar_weight)
    in_gain, mid_gain = attn_norm_gain[None], mlp_norm_gain[None]
    across = lambda one: swap(one, "dp", 1)
    weight_full = gather_weight(output_weight)
    held = project([tokens[0]], 0, total, in_gain, in_weights, [])
    token_parts = gather_rows(tokens[0], held[-1])
    for which in range(1, count):
        if len(token_parts[which]) > 1:
            token_parts[which] = after(token_parts[which], held[-1])
        held = project(token_parts[which], which * rows, total, in_gain, in_weights, held)
    query_proj, key_proj, value_proj, gate_proj, scalar_proj, normed_in = held
    gated, *kept = mixer_forward(
        count, starts, query_proj, key_proj, value_proj, gate_proj, scalar_proj, taps, rates, biases, head_norm_gain[None]
    )
    gated_parts = [joined(one) for one in gather_rows(gated)]
    cot_mine = after(out_cotangent[0], gated_parts[-1])
    normed_mid, middle = middle_rows(rank[None], token_parts, gated_parts, weight_full, mid_gain)

    cot_parts = [[cot_mine]] + [[swap(cot_mine, "tp", mask)] for mask in range(1, count)]
    gates, ups, hidden = hidden_units(normed_mid, mlp_gate_weight, mlp_up_weight)
    mid_other = after(across(normed_mid), hidden)
    cot_parts[-1] = after(cot_parts[-1], hidden)
    cot_flat = [one for part in cot_parts for one in part]
    if lines:
        sources = {}
        chunk = lambda name, row: lambda: (*sources[name], row)
        names = ["down", "gate", "up"]
        even = Line(info, half // 4, [chunk(name, row) for name in names for row in (0, 2)] + [chunk("one", row) for row in range(4)])
        odd = Line(info, half // 4, [chunk(name, row) for name in names for row in (1, 3)] + [chunk("two", row) for row in range(4)])
        placed, waiting = {}, []

        def settle(step):
            if not waiting:
                return step
            name, row, mine, other = waiting.pop(0)
            if name in names:
                shape = (units, width) if name == "down" else (width, units)
                placed[name], step = place(info, placed.get(name), shape, mine, other, row, name == "down", step)
                return step
            *placed["heads"], step = place_heads(
                info, placed.get("heads", []), width, local, mine, [after(one, step) for one in other], row
            )
            return step

        order = {
            id(even): [(name, row) for name in names for row in (0, 2)] + [("one", row) for row in range(4)],
            id(odd): [(name, row) for name in names for row in (1, 3)] + [("two", row) for row in range(4)],
        }
        firsts = {}

        def tick(line, *others):
            before = len(line.results)
            step = line.advance(*others)
            if len(line.results) > before:
                name, row = order[id(line)][before]
                value = line.results[-1]
                other = across(value)
                if name == "one":
                    firsts[row] = (value, other)
                elif name == "two":
                    waiting.append((name, row, [firsts[row][0], value], [firsts[row][1], other]))
                else:
                    waiting.append((name, row, value, other))
            return step

        def land(step, lines=(even, odd)):
            for line in lines:
                step = line.land(step)
            return step

        def ticks(step, lines=(even, odd)):
            for line in lines:
                step = tick(line, step)
            return step

        send = outer_half(info, False, [(cot_flat, hidden)])
        sources["down"] = outer_half(info, True, [(cot_flat, hidden)], send), across(send)
        step = even.begin()
        step = odd.begin(step)

        gate_grad, up_grad, mid_partial = hidden_grads(
            rank[None], cot_parts, gates, ups, mlp_gate_weight, mlp_up_weight, mlp_down_weight, step
        )
        step = land(mid_partial)
        mid_normed_grad = lax.psum_scatter(after(mid_partial, step), "tp", scatter_dimension=0, tiled=True)
        gate_other = across(gate_grad)
        step = ticks(step)
        gate_other = after(gate_other, step)
        up_other = across(after(up_grad, gate_other))
        sources["gate"] = (outer_half(info, True, [([normed_mid], gate_grad), ([mid_other], gate_other)], up_other),)
        step = ticks(sources["gate"][0])
        sources["up"] = (outer_half(info, True, [([normed_mid], up_grad), ([mid_other], up_other)], step),)
        mid_normed_grad = after(mid_normed_grad, sources["up"][0])
        middle_grad, attn_low, gain_mid = norm_grad([mid_normed_grad], middle, out_cotangent[0], mid_gain)
        attn_all = lax.all_gather(attn_low, "tp", axis=0, tiled=True)
        step = ticks(attn_low)
        step = settle(step)
        step = ticks(step)
        gated_grad = gated_grads(count, rank[None], attn_all, output_weight, step)
        grads = mixer_backward(
            count, starts, gated_grad, gate_proj, query_proj, key_proj, value_proj, scalar_proj, kept, taps, rates, biases, head_norm_gain[None]
        )
        flat_low, scalar_low, grad_taps, misc = grads
        step = land(flat_low)
        step = ticks(step)
        one_send, two_send = head_outer(info, False, count, attn_all, gated, normed_in, flat_low, scalar_low, units, step)
        one_other = across(one_send)
        one_keep, two_keep = head_outer(info, True, count, attn_all, gated, normed_in, flat_low, scalar_low, units, one_send)
        one_other = after(one_other, one_keep)
        two_other = across(after(two_send, one_other))
        step = settle(one_other)
        sources["one"], sources["two"] = (one_keep, one_other), (two_keep, after(two_other, step))
        step = tick(even, step)
        in_partial = input_grads(count, rank[None], flat_low, scalar_low, in_weights, step)
        step = tick(odd, in_partial)
        in_normed_grad = lax.psum_scatter(after(in_partial, step), "tp", scatter_dimension=0, tiled=True)
        step = settle(step)
        hops = [("tp", 1 << i) for i in range(count.bit_length() - 1)] + [("dp", 1 << i) for i in range(lax.axis_size("dp").bit_length() - 1)]
        small = None
        while len(odd.results) < len(odd.chunks):
            for line in (even, odd):
                step = settle(step)
                step = tick(line, step)
                if line is even and even.step == 8:
                    in_normed_grad = after(in_normed_grad, step)
                    _, input_grad, gain_in = norm_grad([in_normed_grad], tokens[0], middle_grad, in_gain)
                    small = jnp.concatenate([gain_in[0], gain_mid[0], misc[2]])
                    result_partial = result_rows(count, rank[None], hidden, mlp_down_weight, input_grad)
                    result_sum = lax.psum_scatter(result_partial, "tp", scatter_dimension=0, tiled=True)
                elif small is not None and hops:
                    axis, mask = hops.pop(0)
                    small = small + after(swap(small, axis, mask), step)
                    if hops and hops[0] == ("dp", 1):
                        small = jnp.concatenate([small, grad_taps.reshape(-1), misc[0, :heads], misc[1, :heads]])
        while waiting:
            step = settle(step)
        result = small_call(total_kernel, jax.ShapeDtypeStruct((rows, width), bf16), middle, result_sum)
        grad_output, grad_query, grad_key, grad_value, grad_gate, scalar_sum = placed["heads"]
        scalar_sum = scalar_sum[:, :2 * heads]
        grad_down, grad_mlp_gate, grad_mlp_up = placed["down"], placed["gate"], placed["up"]
    else:
        over = lambda left, right: lax.psum(jnp.einsum("ta,tb->ab", left, right, preferred_element_type=f32).astype(bf16), "dp").astype(f32)
        gate_grad, up_grad, mid_partial = hidden_grads(
            rank[None], cot_parts, gates, ups, mlp_gate_weight, mlp_up_weight, mlp_down_weight
        )
        mid_normed_grad = lax.psum_scatter(mid_partial, "tp", scatter_dimension=0, tiled=True)
        middle_grad, attn_low, gain_mid = norm_grad([mid_normed_grad], middle, out_cotangent[0], mid_gain)
        attn_all = lax.all_gather(attn_low, "tp", axis=0, tiled=True)
        gated_grad = gated_grads(count, rank[None], attn_all, output_weight)
        flat_low, scalar_low, grad_taps, misc = mixer_backward(
            count, starts, gated_grad, gate_proj, query_proj, key_proj, value_proj, scalar_proj, kept, taps, rates, biases, head_norm_gain[None]
        )
        in_partial = input_grads(count, rank[None], flat_low, scalar_low, in_weights)
        in_normed_grad = lax.psum_scatter(in_partial, "tp", scatter_dimension=0, tiled=True)
        _, input_grad, gain_in = norm_grad([in_normed_grad], tokens[0], middle_grad, in_gain)
        result_partial = result_rows(count, rank[None], hidden, mlp_down_weight)
        result_sum = lax.psum_scatter(result_partial, "tp", scatter_dimension=0, tiled=True)
        result = small_call(total_kernel, jax.ShapeDtypeStruct((rows, width), bf16), middle, result_sum)
        grad_down = over(hidden, jnp.concatenate([one for part in cot_parts for one in part], axis=0))
        grad_mlp_gate, grad_mlp_up = over(normed_mid, gate_grad), over(normed_mid, up_grad)
        blocks = attn_all.reshape(count, rows, width)
        attn_rows = jnp.concatenate([lax.dynamic_index_in_dim(blocks, rank ^ m, 0, keepdims=False) for m in range(count)], axis=0)
        grad_output = over(gated, attn_rows)
        grad_query, grad_key, grad_value, grad_gate = [
            over(normed_in, flat_low[:, i * local:(i + 1) * local]) for i in range(4)
        ]
        scalar_sum = over(normed_in, scalar_low[:, :2 * heads])
        small = sum_over(jnp.concatenate([gain_in[0], gain_mid[0], misc[2]]), "tp")
        small = jnp.concatenate([small, grad_taps.reshape(-1), misc[0, :heads], misc[1, :heads]])
        hops = [("dp", 1 << i) for i in range(lax.axis_size("dp").bit_length() - 1)]
    for axis, mask in hops:
        small = small + swap(small, axis, mask)
    pieces = []
    at = 0
    for size in (width, width, HEAD_DIM, grad_taps.size, heads, heads):
        pieces.append(small[at:at + size])
        at += size
    gain_in, gain_mid, gain_head, taps_sum, log_sum, bias_sum = pieces
    return (
        result[None],
        input_grad[None],
        gain_in,
        grad_query,
        grad_key,
        grad_value,
        grad_gate,
        jnp.transpose(scalar_sum.reshape(width, 2, heads), (0, 2, 1)),
        taps_sum.reshape(conv_weight.shape),
        log_sum,
        bias_sum,
        gain_head,
        grad_output,
        gain_mid,
        grad_mlp_gate,
        grad_mlp_up,
        grad_down,
    )


def solution(mesh):
    return jax.shard_map(
        body,
        mesh=mesh,
        in_specs=(
            P("dp", "tp", None),
            P("dp", None),
            P("dp", "tp", None),
            P(),
            P(None, "tp"),
            P(None, "tp"),
            P(None, "tp"),
            P(None, "tp"),
            P(None, "tp", None),
            P(None, None, "tp"),
            P("tp"),
            P("tp"),
            P(),
            P("tp", None),
            P(),
            P(None, "tp"),
            P(None, "tp"),
            P("tp", None),
        ),
        out_specs=(
            P("dp", "tp", None),
            P("dp", "tp", None),
            P(),
            P(None, "tp"),
            P(None, "tp"),
            P(None, "tp"),
            P(None, "tp"),
            P(None, "tp", None),
            P(None, None, "tp"),
            P("tp"),
            P("tp"),
            P(),
            P("tp", None),
            P(),
            P(None, "tp"),
            P(None, "tp"),
            P("tp", None),
        ),
        check_vma=False,
    )
```

```python
import math
from functools import partial

import jax
import jax.numpy as jnp
from jax import lax
from jax.experimental import pallas as pl
from jax.experimental.pallas import tpu as pltpu
from jax.sharding import PartitionSpec as P

HEAD_DIM = 128
CONV = 4
SPAN = 64
TILE = 2 * SPAN
VMEM_BYTES = 60 * 1024 * 1024
SMALL = pl.CostEstimate(flops=0, bytes_accessed=0, transcendentals=0)
epsilon = 1e-06
head_epsilon = 0.001
f32 = jnp.float32
bf16 = jnp.bfloat16


def dot(left, right, dims=((1,), (0,)), precise=False):
    return lax.dot_general(
        left, right, (dims, ((), ())), preferred_element_type=f32,
        precision=lax.Precision.HIGHEST if precise else None,
    )


def iota(shape, axis):
    return lax.broadcasted_iota(jnp.int32, shape, axis)


def spread(packed):
    left = iota(packed.shape, 1) < SPAN
    none = jnp.zeros_like(packed)
    return jnp.concatenate([jnp.where(left, packed, none), jnp.where(left, none, packed)], axis=0)


def halves(full):
    left = iota((SPAN, TILE), 1) < SPAN
    return jnp.where(left, full[:SPAN], full[SPAN:])


def packed_masks():
    row, col = iota((SPAN, TILE), 0), iota((SPAN, TILE), 1) % SPAN
    return row, col


def unit_inverse(stricts):
    row, col = packed_masks()
    near = (row // 2) == (col // 2)
    eye = jnp.where(row == col, 1.0, 0.0)
    results = [eye - jnp.where(near, strict, 0.0) for strict in stricts]
    width = 2
    while width < SPAN:
        inside = ((row // (2 * width)) == (col // (2 * width))) & ((row // width) != (col // width))
        pieces = [jnp.where(inside, strict, 0.0).astype(bf16) for strict in stricts]
        kept = [result.astype(bf16) for result in results]
        moved = [dot(piece, spread(keep)) for piece, keep in zip(pieces, kept)]
        results = [result - dot(keep, spread(move.astype(bf16))) for result, keep, move in zip(results, kept, moved)]
        width *= 2
    return results


def softplus(value):
    return jnp.maximum(value, 0.0) + jnp.log1p(jnp.exp(-jnp.abs(value)))


def row_places(first, rows, starts_ref):
    place = iota((rows, HEAD_DIM), 0) + first
    one, two = starts_ref[1], starts_ref[2]
    start = jnp.where(place >= two, two, jnp.where(place >= one, one, 0))
    end = jnp.where(place >= two, 1 << 30, jnp.where(place >= one, two, one))
    return place, start, end


def carry_flag(first, starts_ref):
    fresh = (first == 0) | (first == starts_ref[1]) | (first == starts_ref[2])
    return jnp.where(fresh, 0.0, 1.0).astype(f32)


def decay_parts(scalars, rates, biases):
    row, col = iota((TILE, TILE), 0), iota((TILE, TILE), 1)
    running = jnp.where((row >= col) & ((row // SPAN) == (col // SPAN)), 1.0, 0.0)
    log_decay = -jnp.exp(rates) * softplus(scalars + biases)
    total = dot(running, log_decay, precise=True)
    return log_decay, total, total.T


def fading_of(total, total_rows, head):
    row, col = packed_masks()
    left = iota((SPAN, TILE), 1) < SPAN
    column = jnp.broadcast_to(total[:, head:head + 1], (TILE, TILE))
    gaps = jnp.where(left, column[:SPAN], column[SPAN:]) - total_rows[head:head + 1, :]
    incl = row >= col
    return jnp.where(incl, jnp.exp(jnp.where(incl, gaps, 0.0)), 0.0)


def last_rows(total, head):
    ends = [jnp.broadcast_to(total[SPAN * i + SPAN - 1:SPAN * (i + 1), head:head + 1], (SPAN, TILE)) for i in range(2)]
    return jnp.concatenate(ends, axis=0)


def forward_kernel(tiles, heads, starts_ref, q_ref, k_ref, v_ref, gate_ref, sp_ref, taps_ref, rate_ref, bias_ref, gain_ref,
                   gated_ref, mixed_ref, cq_ref, ck_ref, cv_ref, inv_ref, qk_ref, gram_ref, w_ref, u_ref, s_ref,
                   ext_ref, state_ref):
    step = pl.program_id(0)
    rows = tiles * TILE

    @pl.when(step == 0)
    def _():
        ext_ref[:, :8, :] = jnp.zeros((3, 8, heads * HEAD_DIM), f32)
        state_ref[...] = jnp.zeros(state_ref.shape, f32)

    ones = jnp.ones((HEAD_DIM, HEAD_DIM), bf16)
    place, start, _ = row_places(step * rows, rows, starts_ref)
    position = place - start
    masks = [jnp.where(position >= j, 1.0, 0.0) for j in range(1, CONV)]
    for which, source in enumerate((q_ref, k_ref, v_ref)):
        ext_ref[which, 8:8 + rows, :] = source[...].astype(f32)

    def activated(which, head, out):
        lanes = slice(head * HEAD_DIM, (head + 1) * HEAD_DIM)
        conv = ext_ref[which, 8:8 + rows, lanes] * taps_ref[which * CONV:which * CONV + 1, lanes]
        for j in range(1, CONV):
            conv = conv + ext_ref[which, 8 - j:8 - j + rows, lanes] * masks[j - 1] * taps_ref[which * CONV + j:which * CONV + j + 1, lanes]
        low = conv.astype(bf16)
        out[:, lanes] = low
        conv = low.astype(f32)
        return conv * jax.nn.sigmoid(conv)

    active = [[activated(which, h, out) for h in range(heads)] for which, out in enumerate((cq_ref, ck_ref, cv_ref))]
    norms = [[dot((one * one).astype(bf16), ones) for one in active[which]] for which in range(2)]
    queries = [one * (lax.rsqrt(norm + epsilon) * HEAD_DIM ** -0.5) for one, norm in zip(active[0], norms[0])]
    keys = [one * lax.rsqrt(norm + epsilon) for one, norm in zip(active[1], norms[1])]
    values = active[2]
    for which in range(3):
        ext_ref[which, :8, :] = ext_ref[which, rows:rows + 8, :]

    lanes_of = lambda head: slice(head * HEAD_DIM, (head + 1) * HEAD_DIM)
    row, col = packed_masks()
    left = iota((SPAN, TILE), 1) < SPAN
    pairs = [(tile, head) for tile in range(tiles) for head in range(heads)]
    spans = [slice(tile * TILE, (tile + 1) * TILE) for tile in range(tiles)]
    packs = [slice(tile * SPAN, (tile + 1) * SPAN) for tile in range(tiles)]
    scalars = [sp_ref[span, :] for span in spans]
    decays = [decay_parts(one, rate_ref[...], bias_ref[...]) for one in scalars]
    writes = [jax.nn.sigmoid(one) for one in scalars]
    grams = []
    for tile, head in pairs:
        k_low = keys[head][spans[tile]].astype(bf16)
        grams.append(dot(jnp.concatenate([queries[head][spans[tile]].astype(bf16), k_low], axis=0), k_low, ((1,), (1,))))
    stricts, scores, spread_writes, columns = [], [], [], []
    for (tile, head), both in zip(pairs, grams):
        _, total, total_rows = decays[tile]
        write = jnp.broadcast_to(writes[tile][:, heads + head:heads + head + 1], (TILE, HEAD_DIM))
        column = jnp.broadcast_to(total[:, head:head + 1], (TILE, HEAD_DIM))
        gaps = jnp.where(left, column[:SPAN], column[SPAN:]) - total_rows[head:head + 1, :]
        fading = jnp.where(row >= col, jnp.exp(jnp.where(row >= col, gaps, 0.0)), 0.0)
        qk, gram = halves(both[:TILE]), halves(both[TILE:])
        qk_ref[packs[tile], lanes_of(head)] = qk.astype(bf16)
        gram_ref[packs[tile], lanes_of(head)] = gram.astype(bf16)
        write_pack = jnp.where(left, write[:SPAN], write[SPAN:])
        stricts.append(jnp.where(row > col, write_pack * gram * fading, 0.0))
        scores.append(spread((qk * fading).astype(bf16)))
        spread_writes.append(write)
        columns.append(column)
    inverses = [one.astype(bf16) for one in unit_inverse(stricts)]
    weighted, free, q_grown, k_tail, ends = [], [], [], [], []
    for (tile, head), inverse, write, column in zip(pairs, inverses, spread_writes, columns):
        total = decays[tile][1]
        q, k, v = queries[head][spans[tile]], keys[head][spans[tile]], values[head][spans[tile]]
        grown = jnp.exp(column)
        tails = jnp.exp(last_rows(total, head) - column)
        inv_ref[packs[tile], lanes_of(head)] = inverse
        sides = jnp.concatenate([(write * grown * k).astype(bf16), (write * v).astype(bf16)], axis=1)
        solved = dot(spread(inverse), sides)
        low = solved[:, :HEAD_DIM].astype(bf16)
        w_ref[spans[tile], lanes_of(head)] = low
        weighted.append(low)
        free.append(solved[:, HEAD_DIM:])
        q_grown.append((q * grown).astype(bf16))
        k_tail.append((k * tails).astype(bf16))
        ends.append([jnp.exp(total[SPAN * i + SPAN - 1:SPAN * (i + 1), head:head + 1]) for i in range(2)])

    states = [state_ref[head] for head in range(heads)]
    for tile in range(tiles):
        at = tile * heads
        seen, changes = [[] for _ in range(heads)], [[] for _ in range(heads)]
        for i in range(2):
            flag = carry_flag(step * rows + tile * TILE + i * SPAN, starts_ref)
            states = [state * flag for state in states]
            lows = [state.astype(bf16) for state in states]
            base = (tile * 2 + i) * HEAD_DIM
            part = slice(i * SPAN, (i + 1) * SPAN)
            both = [dot(jnp.concatenate([weighted[at + h][part], q_grown[at + h][part]], axis=0), lows[h]) for h in range(heads)]
            new = [(free[at + h][part] - both[h][:SPAN]).astype(bf16) for h in range(heads)]
            states = [ends[at + h][i] * states[h] + dot(k_tail[at + h][part], new[h], ((0,), (0,))) for h in range(heads)]
            for h in range(heads):
                s_ref[base:base + HEAD_DIM, lanes_of(h)] = lows[h]
                seen[h].append(both[h][SPAN:])
                changes[h].append(new[h])
        change = [jnp.concatenate(parts, axis=0) for parts in changes]
        mixed = [jnp.concatenate(seen[h], axis=0) + dot(scores[at + h], change[h]) for h in range(heads)]
        squares = [dot((one * one).astype(bf16), ones) * (1.0 / HEAD_DIM) for one in mixed]
        for h in range(heads):
            u_ref[spans[tile], lanes_of(h)] = change[h]
            mixed_ref[spans[tile], lanes_of(h)] = mixed[h].astype(bf16)
            normed = mixed[h] * lax.rsqrt(squares[h] + head_epsilon) * gain_ref[...]
            gate = gate_ref[spans[tile], lanes_of(h)].astype(f32)
            gated_ref[spans[tile], lanes_of(h)] = (normed * gate * jax.nn.sigmoid(gate)).astype(bf16)
    for h in range(heads):
        state_ref[h] = states[h]


def blocked(rows, width, place):
    return pl.BlockSpec((rows, width), lambda i, s: (place(i) ^ s[0], 0))


def constant(shape):
    return pl.BlockSpec(shape, lambda i, s: (0,) * len(shape))


def mixer_forward(count, starts, q, k, v, gate, sp, taps, rate, bias, gain):
    rows, width = q.shape
    heads = width // HEAD_DIM
    block = rows // count
    tiles = block // TILE
    spec = lambda r, w: blocked(r, w, lambda i: i)
    wide, half, state = spec(block, width), spec(block // 2, width), spec(block * 2, width)
    shape = lambda r: jax.ShapeDtypeStruct((r, width), bf16)
    return pl.pallas_call(
        partial(forward_kernel, tiles, heads),
        grid_spec=pltpu.PrefetchScalarGridSpec(
            num_scalar_prefetch=1,
            grid=(count,),
            in_specs=[wide] * 4 + [spec(block, HEAD_DIM)] + [constant(a.shape) for a in (taps, rate, bias, gain)],
            out_specs=[wide] * 5 + [half] * 3 + [wide] * 2 + [state],
            scratch_shapes=[pltpu.VMEM((3, block + 8, width), f32), pltpu.VMEM((heads, HEAD_DIM, HEAD_DIM), f32)],
        ),
        out_shape=[shape(rows)] * 5 + [shape(rows // 2)] * 3 + [shape(rows)] * 2 + [shape(rows * 2)],
        compiler_params=pltpu.CompilerParams(dimension_semantics=("arbitrary",), vmem_limit_bytes=VMEM_BYTES),
        cost_estimate=SMALL,
    )(starts, q, k, v, gate, sp, taps, rate, bias, gain)


def row_sums(product, ones_tall):
    high = product.astype(bf16)
    low = (product - high.astype(f32)).astype(bf16)
    return dot(jnp.concatenate([high, low], axis=1), ones_tall)


def backward_kernel(tiles, heads, starts_ref, gg_ref, mixed_ref, gate_ref, cq_ref, ck_ref, cv_ref, q_ref, k_ref, v_ref, sp_ref,
                    inv_ref, qk_ref, gram_ref, w_ref, u_ref, s_ref, taps_ref, rate_ref, bias_ref, gain_ref,
                    flat_ref, dsp_ref, dtaps_ref, dmisc_ref, ext_ref, state_ref):
    step = pl.num_programs(0) - 1 - pl.program_id(0)
    rows = tiles * TILE

    @pl.when(pl.program_id(0) == 0)
    def _():
        ext_ref[:, rows:, :] = jnp.zeros((3, 8, heads * HEAD_DIM), f32)
        state_ref[...] = jnp.zeros(state_ref.shape, f32)
        dtaps_ref[...] = jnp.zeros(dtaps_ref.shape, f32)
        dmisc_ref[...] = jnp.zeros(dmisc_ref.shape, f32)

    ones = jnp.ones((HEAD_DIM, HEAD_DIM), bf16)
    ones_tall = jnp.ones((2 * HEAD_DIM, HEAD_DIM), bf16)
    lanes_of = lambda head: slice(head * HEAD_DIM, (head + 1) * HEAD_DIM)
    row, col = packed_masks()
    left = iota((SPAN, TILE), 1) < SPAN
    full_row, full_col = iota((TILE, TILE), 0), iota((TILE, TILE), 1)
    same = (full_row // SPAN) == (full_col // SPAN)
    pairs = [(tile, head) for tile in range(tiles) for head in range(heads)]
    spans = [slice(tile * TILE, (tile + 1) * TILE) for tile in range(tiles)]
    packs = [slice(tile * SPAN, (tile + 1) * SPAN) for tile in range(tiles)]
    gain = gain_ref[...]

    mixed = [mixed_ref[spans[t], lanes_of(h)].astype(f32) for t, h in pairs]
    squares = [dot((one * one).astype(bf16), ones) * (1.0 / HEAD_DIM) for one in mixed]
    partial_gain = jnp.zeros((1, HEAD_DIM), f32)
    scales, pulled, inner = [], [], []
    for (t, h), one, square in zip(pairs, mixed, squares):
        scale = lax.rsqrt(square + head_epsilon)
        gate = gate_ref[spans[t], lanes_of(h)].astype(f32)
        grad = gg_ref[spans[t], lanes_of(h)].astype(f32)
        sig = jax.nn.sigmoid(gate)
        unit = one * scale
        flat_ref[spans[t], lanes_of(3 * heads + h)] = (grad * unit * gain * (sig * (1.0 + gate * (1.0 - sig)))).astype(bf16)
        norm_grad = grad * gate * sig
        partial_gain = partial_gain + jnp.sum(norm_grad * unit, axis=0, keepdims=True)
        norm_grad = norm_grad * gain
        scales.append(scale)
        pulled.append(norm_grad)
        inner.append(dot((norm_grad * unit).astype(bf16), ones) * (1.0 / HEAD_DIM))
    dmisc_ref[2:3, :] = dmisc_ref[2:3, :] + partial_gain
    dout = [(scale * (grad - one * scale * mean)).astype(bf16) for scale, grad, one, mean in zip(scales, pulled, mixed, inner)]

    def silu_parts(ref, t, h):
        conv = ref[spans[t], lanes_of(h)].astype(f32)
        sig = jax.nn.sigmoid(conv)
        return conv * sig, sig * (1.0 + conv * (1.0 - sig))

    raw_q = [silu_parts(cq_ref, t, h) for t, h in pairs]
    raw_k = [silu_parts(ck_ref, t, h) for t, h in pairs]
    norm_q = [lax.rsqrt(dot((one[0] * one[0]).astype(bf16), ones) + epsilon) for one in raw_q]
    norm_k = [lax.rsqrt(dot((one[0] * one[0]).astype(bf16), ones) + epsilon) for one in raw_k]
    decays = [decay_parts(sp_ref[span, :], rate_ref[...], bias_ref[...]) for span in spans]
    writes = [jax.nn.sigmoid(sp_ref[span, :]) for span in spans]
    queries, keys, fadings, growns, tails, spread_writes, write_packs, ends = [], [], [], [], [], [], [], []
    for n, (t, h) in enumerate(pairs):
        _, total, total_rows = decays[t]
        queries.append(raw_q[n][0] * (norm_q[n] * HEAD_DIM ** -0.5))
        keys.append(raw_k[n][0] * norm_k[n])
        write = jnp.broadcast_to(writes[t][:, heads + h:heads + h + 1], (TILE, HEAD_DIM))
        column = jnp.broadcast_to(total[:, h:h + 1], (TILE, HEAD_DIM))
        gaps = jnp.where(left, column[:SPAN], column[SPAN:]) - total_rows[h:h + 1, :]
        fadings.append(jnp.where(row >= col, jnp.exp(jnp.where(row >= col, gaps, 0.0)), 0.0))
        growns.append(jnp.exp(column))
        tails.append(jnp.exp(last_rows(total, h) - column))
        spread_writes.append(write)
        write_packs.append(jnp.where(left, write[:SPAN], write[SPAN:]))
        ends.append([jnp.exp(total[SPAN * i + SPAN - 1:SPAN * (i + 1), h:h + 1]) for i in range(2)])
    qk = [qk_ref[packs[t], lanes_of(h)].astype(f32) for t, h in pairs]
    score_grads = [dot(spread((qk[n] * fadings[n]).astype(bf16)), dout[n], ((0,), (0,))) for n in range(len(pairs))]
    q_grown = [(queries[n] * growns[n]).astype(bf16) for n in range(len(pairs))]
    k_tail = [(keys[n] * tails[n]).astype(bf16) for n in range(len(pairs))]
    parts = [slice(0, SPAN), slice(SPAN, TILE)]
    q_outs = [[dot(q_grown[n][part], dout[n][part], ((0,), (0,))) for part in parts] for n in range(len(pairs))]

    states = [state_ref[h] for h in range(heads)]
    change_grads = [[None, None] for _ in pairs]
    tail_grads = [[None, None] for _ in pairs]
    end_grads = [[None, None] for _ in pairs]
    for t in reversed(range(tiles)):
        for i in (1, 0):
            part = parts[i]
            here = slice(t * TILE + i * SPAN, t * TILE + (i + 1) * SPAN)
            at = slice((t * 2 + i) * HEAD_DIM, (t * 2 + i + 1) * HEAD_DIM)
            flag = carry_flag(step * rows + t * TILE + i * SPAN, starts_ref)
            lows = [one.astype(bf16) for one in states]
            news = []
            for h in range(heads):
                n = t * heads + h
                news.append((score_grads[n][part] + dot(k_tail[n][part], lows[h])).astype(bf16))
            for h in range(heads):
                n = t * heads + h
                change_grads[n][i] = news[h]
                tail_grads[n][i] = dot(u_ref[here, lanes_of(h)], lows[h], ((1,), (1,)))
                held = jnp.sum(states[h] * s_ref[at, lanes_of(h)].astype(f32), axis=0, keepdims=True)
                end_grads[n][i] = ends[n][i] * jnp.sum(held, axis=1, keepdims=True)
            states = [
                flag * (ends[t * heads + h][i] * states[h] + q_outs[t * heads + h][i] - dot(w_ref[here, lanes_of(h)], news[h], ((0,), (0,))))
                for h in range(heads)
            ]
    for h in range(heads):
        state_ref[h] = states[h]

    change_grads = [jnp.concatenate(one, axis=0) for one in change_grads]
    side_grads = [dot(spread(inv_ref[packs[t], lanes_of(h)]), change_grads[n], ((0,), (0,))) for n, (t, h) in enumerate(pairs)]
    side_low = [one.astype(bf16) for one in side_grads]
    crossed = []
    for n, (t, h) in enumerate(pairs):
        through = []
        for i, part in enumerate(parts):
            at = slice((t * 2 + i) * HEAD_DIM, (t * 2 + i + 1) * HEAD_DIM)
            through.append(dot(jnp.concatenate([side_low[n][part], dout[n][part]], axis=0), s_ref[at, lanes_of(h)], ((1,), (1,))))
        grams = dot(jnp.concatenate([dout[n], side_low[n]], axis=0), u_ref[spans[t], lanes_of(h)], ((1,), (1,)))
        crossed.append((through, grams))
    query_grads, key_grads = [], []
    flat_q = [one.astype(bf16) for one in queries]
    flat_k = [one.astype(bf16) for one in keys]
    products = []
    for n, (t, h) in enumerate(pairs):
        through, grams = crossed[n]
        weighted_grad = -jnp.concatenate([one[:SPAN] for one in through], axis=0)
        grown_grad = jnp.concatenate([one[SPAN:] for one in through], axis=0)
        gram = gram_ref[packs[t], lanes_of(h)].astype(f32)
        pair_grad = halves(grams[:TILE]) * fadings[n]
        strict_grad = jnp.where(row > col, -halves(grams[TILE:]), 0.0) * fadings[n]
        gram_grad = strict_grad * write_packs[n]
        matrix = jnp.concatenate([spread(pair_grad.astype(bf16)), spread(gram_grad.astype(bf16))], axis=0)
        forward = dot(matrix, flat_k[n])
        backward = dot(matrix, jnp.concatenate([flat_q[n], flat_k[n]], axis=0), ((0,), (0,)))
        tail_grad = jnp.concatenate(tail_grads[n], axis=0)
        grown_key = growns[n] * keys[n]
        write = spread_writes[n]
        query_grads.append(forward[:TILE] + grown_grad * growns[n])
        key_grads.append(forward[TILE:] + backward + tail_grad * tails[n] + weighted_grad * write * growns[n])
        value = cv_ref[spans[t], lanes_of(h)].astype(f32)
        value = value * jax.nn.sigmoid(value)
        moving = pair_grad * qk[n] + gram_grad * gram
        inner_key = weighted_grad * grown_key
        products.append((
            spread(strict_grad * gram) + inner_key + side_grads[n] * value,
            spread(moving) + grown_grad * growns[n] * queries[n] + inner_key * write,
            tail_grad * tails[n] * keys[n],
            jnp.sum(moving, axis=0, keepdims=True),
        ))
    sums = [[row_sums(one, ones_tall) for one in three[:3]] for three in products]
    upper = jnp.where((full_row <= full_col) & same, 1.0, 0.0)
    lower = jnp.where((full_row > full_col) & same, 1.0, 0.0)
    for t in range(tiles):
        gap_grad = jnp.zeros((TILE, HEAD_DIM), f32)
        tail_sum = jnp.zeros((TILE, HEAD_DIM), f32)
        write_grad = jnp.zeros((TILE, HEAD_DIM), f32)
        ends_grad = jnp.zeros((TILE, HEAD_DIM), f32)
        across = jnp.zeros((TILE, HEAD_DIM), f32)
        for h in range(heads):
            n = t * heads + h
            mine = full_col == h
            gap_grad = jnp.where(mine, sums[n][1], gap_grad)
            tail_sum = jnp.where(mine, sums[n][2], tail_sum)
            write_grad = jnp.where(full_col == heads + h, sums[n][0], write_grad)
            across = jnp.where(full_row == h, products[n][3], across)
            ends_grad = jnp.where(mine, jnp.where(full_row < SPAN, end_grads[n][0], end_grads[n][1]), ends_grad)
        log_grad = dot(upper, gap_grad - across.T, precise=True) + dot(lower, tail_sum, precise=True) + ends_grad
        scalars = sp_ref[spans[t], :]
        rate = -jnp.exp(rate_ref[...])
        inside = log_grad * rate * jax.nn.sigmoid(scalars + bias_ref[...])
        write = writes[t]
        out = jnp.where(full_col < heads, inside, write_grad * write * (1.0 - write))
        dsp_ref[spans[t], :] = jnp.where(full_col < 2 * heads, out, 0.0).astype(bf16)
        dmisc_ref[0:1, :] = dmisc_ref[0:1, :] + jnp.sum(log_grad * decays[t][0], axis=0, keepdims=True)
        dmisc_ref[1:2, :] = dmisc_ref[1:2, :] + jnp.sum(inside, axis=0, keepdims=True)

    inner_q = [dot((query_grads[n] * raw_q[n][0]).astype(bf16), ones) for n in range(len(pairs))]
    inner_k = [dot((key_grads[n] * raw_k[n][0]).astype(bf16), ones) for n in range(len(pairs))]
    for n, (t, h) in enumerate(pairs):
        scale = norm_q[n]
        grad = (query_grads[n] - raw_q[n][0] * (scale * scale * inner_q[n])) * (scale * HEAD_DIM ** -0.5)
        ext_ref[0, spans[t], lanes_of(h)] = grad * raw_q[n][1]
        scale = norm_k[n]
        grad = (key_grads[n] - raw_k[n][0] * (scale * scale * inner_k[n])) * scale
        ext_ref[1, spans[t], lanes_of(h)] = grad * raw_k[n][1]
        ext_ref[2, spans[t], lanes_of(h)] = side_grads[n] * spread_writes[n] * silu_parts(cv_ref, t, h)[1]
    place, _, end = row_places(step * rows, rows, starts_ref)
    masks = [None] + [jnp.where(place + j < end, 1.0, 0.0) for j in range(1, CONV)]
    for which, source in enumerate((q_ref, k_ref, v_ref)):
        for h in range(heads):
            lanes = lanes_of(h)
            proj = source[:, lanes].astype(f32)
            total = None
            for j in range(CONV):
                moved = ext_ref[which, j:j + rows, lanes]
                if j:
                    moved = moved * masks[j]
                at = which * CONV + j
                dtaps_ref[at:at + 1, lanes] = dtaps_ref[at:at + 1, lanes] + jnp.sum(proj * moved, axis=0, keepdims=True)
                term = moved * taps_ref[at:at + 1, lanes]
                total = term if total is None else total + term
            flat_ref[:, lanes_of(which * heads + h)] = total.astype(bf16)
        ext_ref[which, rows:, :] = ext_ref[which, :8, :]


def mixer_backward(count, starts, gg, gate, q, k, v, sp, kept, taps, rate, bias, gain):
    mixed, cq, ck, cv, inv, qk, gram, w, u, s = kept
    rows, width = q.shape
    heads = width // HEAD_DIM
    block = rows // count
    tiles = block // TILE
    spec = lambda r, w: blocked(r, w, lambda i: count - 1 - i)
    wide, half, state, scal = spec(block, width), spec(block // 2, width), spec(block * 2, width), spec(block, HEAD_DIM)
    shape = lambda r: jax.ShapeDtypeStruct((r, width), bf16)
    return pl.pallas_call(
        partial(backward_kernel, tiles, heads),
        grid_spec=pltpu.PrefetchScalarGridSpec(
            num_scalar_prefetch=1,
            grid=(count,),
            in_specs=[wide] * 9 + [scal] + [half] * 3 + [wide] * 2 + [state] + [constant(a.shape) for a in (taps, rate, bias, gain)],
            out_specs=[spec(block, 4 * width), scal, constant((3 * CONV, width)), constant((8, HEAD_DIM))],
            scratch_shapes=[pltpu.VMEM((3, block + 8, width), f32), pltpu.VMEM((heads, HEAD_DIM, HEAD_DIM), f32)],
        ),
        out_shape=[
            jax.ShapeDtypeStruct((rows, 4 * width), bf16),
            jax.ShapeDtypeStruct((rows, HEAD_DIM), bf16),
            jax.ShapeDtypeStruct((3 * CONV, width), f32),
            jax.ShapeDtypeStruct((8, HEAD_DIM), f32),
        ],
        compiler_params=pltpu.CompilerParams(dimension_semantics=("arbitrary",), vmem_limit_bytes=VMEM_BYTES),
        cost_estimate=SMALL,
    )(starts, gg, mixed, gate, cq, ck, cv, q, k, v, sp, inv, qk, gram, w, u, s, taps, rate, bias, gain)


def after(values, *others):
    single = not isinstance(values, (list, tuple))
    values = [values] if single else list(values)
    others = [one for one in others if one is not None]
    out = pl.pallas_call(
        lambda *refs: None,
        out_shape=[jax.ShapeDtypeStruct(one.shape, one.dtype) for one in values],
        in_specs=[pl.BlockSpec(memory_space=pl.ANY)] * (len(values) + len(others)),
        out_specs=[pl.BlockSpec(memory_space=pl.ANY)] * len(values),
        input_output_aliases={i: i for i in range(len(values))},
    )(*values, *others)
    return out[0] if single else list(out)


def once(shape):
    return pl.BlockSpec(shape, lambda *_: (0,) * len(shape), pipeline_mode=pl.Buffered(1))


def params():
    return pltpu.CompilerParams(dimension_semantics=("arbitrary",), vmem_limit_bytes=VMEM_BYTES)


def project_kernel(sizes, *refs):
    parts, refs = split_pieces(refs, sizes)
    gain_ref, weights, outs, held = refs[0], refs[1:6], refs[-7:-1], refs[-1]
    if len(sizes) > 1:
        pick(len(sizes), parts, held)
        x = held[...].astype(f32)
    else:
        x = whole(parts[0]).astype(f32)
    scale = lax.rsqrt(jnp.mean(x * x, axis=-1, keepdims=True) + epsilon)
    normed = (x * scale * gain_ref[...]).astype(bf16)
    outs[5][...] = normed
    for weight, out in zip(weights, outs[:5]):
        out[...] = dot(normed, weight[...]).astype(out.dtype)


def project(parts, first, total, gain, weights, held, *others):
    rows, depth = sum(one.shape[0] for one in parts[0]), parts[0][0].shape[1]
    flat, sizes = [one for part in parts for one in part], [len(part) for part in parts]
    shapes = [jax.ShapeDtypeStruct((total, w.shape[1]), f32 if i == 4 else bf16) for i, w in enumerate(weights)]
    shapes.append(jax.ShapeDtypeStruct((total, depth), bf16))
    return pl.pallas_call(
        partial(project_kernel, sizes),
        grid=(len(parts),),
        in_specs=[once(one.shape) for one in flat]
        + [once(gain.shape)]
        + [once(w.shape) for w in weights]
        + [pl.BlockSpec(memory_space=pl.ANY)] * (len(held) + len(others)),
        out_specs=[pl.BlockSpec((rows, s.shape[1]), lambda i: (first + i, 0)) for s in shapes],
        out_shape=shapes,
        scratch_shapes=[pltpu.VMEM((rows, depth), bf16)],
        input_output_aliases={len(flat) + 6 + i: i for i in range(len(held))},
        compiler_params=params(),
        cost_estimate=SMALL,
    )(*flat, gain, *weights, *held, *others)


def pick(count, refs, held):
    step = pl.program_id(0)
    for which in range(count):
        @pl.when(step == which)
        def _():
            held[...] = whole(refs[which]) if isinstance(refs[which], (list, tuple)) else refs[which][...]


def middle_kernel(sizes, *refs):
    count = len(sizes)
    x_refs, refs = split_pieces(refs, sizes)
    g_refs = refs[:count]
    own_weight, far_weight, gain_ref, normed_ref, own_ref, scr, x_scr = refs[count:]
    pick(count, x_refs, x_scr)
    gated = jnp.concatenate([one[...] for one in g_refs], axis=1)
    width = gated.shape[1] // count
    for a, b in column_cuts(scr.shape[1]):
        weight = [own_weight[:, a:b]] + [far_weight[:, m, :, a:b].reshape(width, b - a) for m in range(count - 1)]
        scr[:, a:b] = dot(gated, jnp.concatenate(weight, axis=0)) + x_scr[:, a:b].astype(f32)
    middle = scr[...]
    scale = lax.rsqrt(jnp.mean(middle * middle, axis=-1, keepdims=True) + epsilon)
    normed_ref[...] = (middle * scale * gain_ref[...]).astype(bf16)

    @pl.when(pl.program_id(0) == 0)
    def _():
        own_ref[...] = middle


def middle_rows(x_parts, gated_parts, own_weight, far_weight, gain):
    count = len(x_parts)
    rows, depth = x_parts[0][0].shape
    width = gated_parts[0].shape[1]
    flat = [one for part in x_parts for one in part]
    return pl.pallas_call(
        partial(middle_kernel, [len(part) for part in x_parts]),
        grid=(count,),
        in_specs=[once(one.shape) for one in flat]
        + [pl.BlockSpec((rows, width), lambda i, at=at: (i ^ at, 0)) for at in range(count)]
        + [once(own_weight.shape), once(far_weight.shape), once(gain.shape)],
        out_specs=[pl.BlockSpec((rows, depth), lambda i: (i, 0)), once((rows, depth))],
        out_shape=[jax.ShapeDtypeStruct((count * rows, depth), bf16), jax.ShapeDtypeStruct((rows, depth), f32)],
        scratch_shapes=[pltpu.VMEM((rows, depth), f32), pltpu.VMEM((rows, depth), bf16)],
        compiler_params=params(),
        cost_estimate=SMALL,
    )(*flat, *gated_parts, own_weight, far_weight, gain)


def gated_grad_kernel(rank_ref, rows_ref, weight_ref, *refs):
    refs[-1][...] = dot(rows_ref[...], weight_ref[...], ((1,), (1,))).astype(bf16)


def gated_grads(count, rank, gathered, weight, *others):
    rows, depth = gathered.shape[0] // count, gathered.shape[1]
    width = weight.shape[0]
    return pl.pallas_call(
        gated_grad_kernel,
        grid_spec=pltpu.PrefetchScalarGridSpec(
            num_scalar_prefetch=1,
            grid=(count,),
            in_specs=[pl.BlockSpec((rows, depth), lambda i, s: (i ^ s[0], 0)), once(weight.shape)]
            + [pl.BlockSpec(memory_space=pl.ANY)] * len(others),
            out_specs=pl.BlockSpec((rows, width), lambda i, s: (i, 0)),
        ),
        out_shape=jax.ShapeDtypeStruct((count * rows, width), bf16),
        compiler_params=params(),
        cost_estimate=SMALL,
    )(rank, gathered, weight, *others)


def column_cuts(width, chunk=512):
    return [(lo, min(lo + chunk, width)) for lo in range(0, width, chunk)]


def hidden_kernel(x_ref, wg_ref, wu_ref, *refs):
    gate_ref, up_ref, hidden_ref = refs[-3:]
    x = x_ref[...]
    for a, b in column_cuts(wg_ref.shape[1]):
        gate, up = dot(x, wg_ref[:, a:b]), dot(x, wu_ref[:, a:b])
        gate_ref[:, a:b] = gate.astype(bf16)
        up_ref[:, a:b] = up.astype(bf16)
        hidden_ref[:, a:b] = (gate * jax.nn.sigmoid(gate) * up).astype(bf16)


def hidden_units(x, gate_weight, up_weight, *others):
    rows, depth = x.shape
    width = gate_weight.shape[1]
    block = rows // 4
    out = pl.BlockSpec((block, width), lambda i: (i, 0))
    return pl.pallas_call(
        hidden_kernel,
        grid=(4,),
        in_specs=[pl.BlockSpec((block, depth), lambda i: (i, 0)), once(gate_weight.shape), once(up_weight.shape)]
        + [pl.BlockSpec(memory_space=pl.ANY)] * len(others),
        out_specs=[out] * 3,
        out_shape=[jax.ShapeDtypeStruct((rows, width), bf16)] * 3,
        compiler_params=params(),
        cost_estimate=SMALL,
    )(x, gate_weight, up_weight, *others)


def whole(refs):
    values = [one[...] for one in refs]
    return values[0] if len(values) == 1 else jnp.concatenate(values, axis=0)


def outer_kernel(parts, info_ref, *refs):
    total, at = None, 0
    for count in parts:
        term = dot(whole(refs[at:at + count]), refs[at + count][...], ((0,), (0,)))
        total = term if total is None else total + term
        at += count + 1
    refs[-1][...] = total.astype(bf16)


def half_column(count, own):
    return lambda i, s: (s[0] if own else 1 - s[0]) * count + i


def outer_half(info, own, sides, *others):
    lefts, right = sides[0]
    half, block = lefts[0].shape[1] // 2, 2 * TILE
    count, units = half // block, right.shape[1]
    column = half_column(count, own)
    in_specs, values = [], []
    for lefts, right in sides:
        in_specs += [pl.BlockSpec((one.shape[0], block), lambda i, s: (0, column(i, s))) for one in lefts] + [once(right.shape)]
        values += list(lefts) + [right]
    return pl.pallas_call(
        partial(outer_kernel, [len(lefts) for lefts, _ in sides]),
        grid_spec=pltpu.PrefetchScalarGridSpec(
            num_scalar_prefetch=1,
            grid=(count,),
            in_specs=in_specs + [pl.BlockSpec(memory_space=pl.ANY)] * len(others),
            out_specs=pl.BlockSpec((block, units), lambda i, s: (i, 0)),
        ),
        out_shape=jax.ShapeDtypeStruct((half, units), bf16),
        compiler_params=params(),
        cost_estimate=SMALL,
    )(info, *values, *others)


def split_pieces(refs, sizes):
    pieces, at = [], 0
    for size in sizes:
        pieces.append(refs[at:at + size])
        at += size
    return pieces, refs[at:]


def hidden_grad_kernel(sizes, rank_ref, *refs):
    c_refs, refs = split_pieces(refs, sizes)
    gate_ref, up_ref, wg_ref, wu_ref, wd_ref = refs[:5]
    gg_ref, ug_ref, mid_ref, held = refs[-4:]
    pick(len(sizes), c_refs, held)
    grad_rows = held[...]
    nt = ((1,), (1,))
    for a, b in column_cuts(wg_ref.shape[1]):
        grad = dot(grad_rows, wd_ref[a:b, :], nt)
        gate, up = gate_ref[:, a:b].astype(f32), up_ref[:, a:b].astype(f32)
        sig = jax.nn.sigmoid(gate)
        gg_ref[:, a:b] = (grad * up * sig * (1.0 + gate * (1.0 - sig))).astype(bf16)
        ug_ref[:, a:b] = (grad * gate * sig).astype(bf16)
    gate_grad, up_grad = gg_ref[...], ug_ref[...]
    for a, b in column_cuts(wg_ref.shape[0]):
        mid_ref[:, a:b] = (dot(gate_grad, wg_ref[a:b, :], nt) + dot(up_grad, wu_ref[a:b, :], nt)).astype(bf16)


def hidden_grads(rank, cot_parts, gates, ups, gate_weight, up_weight, down_weight, *others):
    count = len(cot_parts)
    rows, depth = cot_parts[0][0].shape
    width = gate_weight.shape[1]
    spec = pl.BlockSpec((rows, width), lambda i, s: (i, 0))
    flat = [one for part in cot_parts for one in part]
    return pl.pallas_call(
        partial(hidden_grad_kernel, [len(part) for part in cot_parts]),
        grid_spec=pltpu.PrefetchScalarGridSpec(
            num_scalar_prefetch=1,
            grid=(count,),
            in_specs=[once(one.shape) for one in flat]
            + [spec] * 2
            + [once(gate_weight.shape), once(up_weight.shape), once(down_weight.shape)]
            + [pl.BlockSpec(memory_space=pl.ANY)] * len(others),
            out_specs=[spec, spec, pl.BlockSpec((rows, depth), lambda i, s: (i ^ s[0], 0))],
            scratch_shapes=[pltpu.VMEM((rows, depth), bf16)],
        ),
        out_shape=[jax.ShapeDtypeStruct((count * rows, width), bf16)] * 2 + [jax.ShapeDtypeStruct((count * rows, depth), bf16)],
        compiler_params=params(),
        cost_estimate=SMALL,
    )(rank, *flat, gates, ups, gate_weight, up_weight, down_weight, *others)


def input_grad_kernel(rank_ref, grad_ref, scalar_ref, *refs):
    weights, out = refs[:5], refs[-1]
    grad = jnp.concatenate([grad_ref[...], scalar_ref[...]], axis=1)
    for a, b in column_cuts(out.shape[1]):
        weight = jnp.concatenate([one[a:b, :] for one in weights], axis=1)
        out[:, a:b] = dot(grad, weight, ((1,), (1,))).astype(bf16)


def input_grads(count, rank, grad, scalar_grad, weights, *others):
    rows, depth = grad.shape[0] // count, weights[0].shape[0]
    return pl.pallas_call(
        input_grad_kernel,
        grid_spec=pltpu.PrefetchScalarGridSpec(
            num_scalar_prefetch=1,
            grid=(count,),
            in_specs=[pl.BlockSpec((rows, one.shape[1]), lambda i, s: (i, 0)) for one in (grad, scalar_grad)]
            + [once(one.shape) for one in weights]
            + [pl.BlockSpec(memory_space=pl.ANY)] * len(others),
            out_specs=pl.BlockSpec((rows, depth), lambda i, s: (i ^ s[0], 0)),
        ),
        out_shape=jax.ShapeDtypeStruct((count * rows, depth), bf16),
        compiler_params=params(),
        cost_estimate=SMALL,
    )(rank, grad, scalar_grad, *weights, *others)


def result_kernel(rank_ref, hidden_ref, weight_ref, *refs):
    out = refs[-1]
    for a, b in column_cuts(out.shape[1]):
        out[:, a:b] = dot(hidden_ref[...], weight_ref[:, a:b]).astype(bf16)


def result_rows(count, rank, hidden, weight, *others):
    rows, depth = hidden.shape[0] // count, weight.shape[1]
    return pl.pallas_call(
        result_kernel,
        grid_spec=pltpu.PrefetchScalarGridSpec(
            num_scalar_prefetch=1,
            grid=(count,),
            in_specs=[pl.BlockSpec((rows, hidden.shape[1]), lambda i, s: (i, 0)), once(weight.shape)]
            + [pl.BlockSpec(memory_space=pl.ANY)] * len(others),
            out_specs=pl.BlockSpec((rows, depth), lambda i, s: (i ^ s[0], 0)),
        ),
        out_shape=jax.ShapeDtypeStruct((count * rows, depth), bf16),
        compiler_params=params(),
        cost_estimate=SMALL,
    )(rank, hidden, weight, *others)


def small_call(kernel, outs, *values):
    return pl.pallas_call(
        kernel,
        out_shape=outs,
        compiler_params=pltpu.CompilerParams(vmem_limit_bytes=VMEM_BYTES),
        cost_estimate=SMALL,
    )(*values)


def merge_kernel(across_ref, down_ref, top_ref, low_ref, *refs):
    half = top_ref.shape[0]
    across_out, down_out = refs[-2:]
    down_out[:half] = (down_ref[:half].astype(f32) + top_ref[...].astype(f32)).astype(bf16)
    down_out[half:] = down_ref[half:]
    across_out[:half] = across_ref[:half]
    across_out[half:] = (across_ref[half:].astype(f32) + low_ref[...].astype(f32)).astype(bf16)


def halves_kernel(across_ref, down_ref, top_out, low_out):
    top_out[...] = down_ref[...]
    low_out[...] = across_ref[...]


def far_halves(across, down):
    rows, columns = across.shape[0] // 2, across.shape[1]
    top, low = pl.BlockSpec((rows, columns), lambda i: (0, 0)), pl.BlockSpec((rows, columns), lambda i: (1, 0))
    return pl.pallas_call(
        halves_kernel,
        grid=(1,),
        in_specs=[low, top],
        out_specs=[top, top],
        out_shape=[jax.ShapeDtypeStruct((rows, columns), across.dtype)] * 2,
        compiler_params=params(),
        cost_estimate=SMALL,
    )(across, down)


def norm_grad_kernel(count, *refs):
    terms, (x_ref, cot_ref, gain_ref, grad_out, low_out, gain_out) = refs[:count], refs[count:]
    grad = terms[0][...].astype(f32)
    for one in terms[1:]:
        grad = grad + one[...].astype(f32)
    x = x_ref[...].astype(f32)
    scale = lax.rsqrt(jnp.mean(x * x, axis=-1, keepdims=True) + epsilon)
    unit = x * scale
    gain_out[...] = jnp.sum(grad * unit, axis=0, keepdims=True)
    inner = grad * gain_ref[...]
    total = cot_ref[...].astype(f32) + scale * (inner - unit * jnp.mean(inner * unit, axis=-1, keepdims=True))
    if grad_out is not None:
        grad_out[...] = total
    low_out[...] = total.astype(bf16)


def norm_grad(terms, x, cot, gain):
    rows, depth = x.shape
    return small_call(
        partial(norm_grad_kernel, len(terms)),
        [jax.ShapeDtypeStruct((rows, depth), f32), jax.ShapeDtypeStruct((rows, depth), bf16), jax.ShapeDtypeStruct((1, depth), f32)],
        *terms, x, cot, gain,
    )


def total_kernel(*refs):
    refs[-1][...] = (refs[0][...] + refs[1][...].astype(f32)).astype(bf16)


def wide_call(kernel, out_dtype, values, *others):
    rows, columns = values[0].shape
    block = next(size for size in (256, 128, 64, 32, 16) if rows % size == 0)
    spec = pl.BlockSpec((block, columns), lambda i, *_: (i, 0))
    return pl.pallas_call(
        kernel,
        grid=(rows // block,),
        in_specs=[spec] * len(values) + [pl.BlockSpec(memory_space=pl.ANY)] * len(others),
        out_specs=spec,
        out_shape=jax.ShapeDtypeStruct((rows, columns), out_dtype),
        compiler_params=params(),
        cost_estimate=SMALL,
    )(*values, *others)


def add_kernel(left, right, *refs):
    refs[-1][...] = (left[...].astype(f32) + right[...].astype(f32)).astype(bf16)


def cast_kernel(value, *refs):
    refs[-1][...] = value[...].astype(f32)


def choose_kernel(flag_ref, left, right, *refs):
    refs[-1][...] = jnp.where(flag_ref[0] == 1, left[...], right[...])


def choose(flag, left, right, *others):
    rows, columns = left.shape
    block = next(size for size in (256, 128, 64, 32, 16) if rows % size == 0)
    spec = pl.BlockSpec((block, columns), lambda i, s: (i, 0))
    return pl.pallas_call(
        choose_kernel,
        grid_spec=pltpu.PrefetchScalarGridSpec(
            num_scalar_prefetch=1,
            grid=(rows // block,),
            in_specs=[spec, spec] + [pl.BlockSpec(memory_space=pl.ANY)] * len(others),
            out_specs=spec,
        ),
        out_shape=jax.ShapeDtypeStruct((rows, columns), left.dtype),
        compiler_params=params(),
        cost_estimate=SMALL,
    )(flag, left, right, *others)


def head_outer_kernel(parts, info_ref, *refs):
    attn, (gated_ref, in_ref, flat_ref, scalar_ref) = refs[:parts], refs[parts:parts + 4]
    one, two = refs[-2:]
    units = one.shape[1]
    tn = ((0,), (0,))
    left = in_ref[...]
    columns = [dot(whole(attn), gated_ref[...], tn), dot(left, flat_ref[...], tn), dot(left, scalar_ref[...], tn)]
    joined = jnp.concatenate([one.astype(bf16) for one in columns], axis=1)
    spare = 2 * units - joined.shape[1]
    if spare:
        joined = jnp.concatenate([joined, jnp.zeros((joined.shape[0], spare), bf16)], axis=1)
    one[...] = joined[:, :units]
    two[...] = joined[:, units:]


def head_outer(info, own, parts, attn, gated, normed, flat, scalar, units, *others):
    tokens, width = normed.shape
    half, block = width // 2, 2 * TILE
    count, rows = half // block, tokens // parts
    column = half_column(count, own)
    attn_specs = [pl.BlockSpec((rows, block), lambda i, s, m=m: (s[2] ^ m, column(i, s))) for m in range(parts)]
    out = pl.BlockSpec((block, units), lambda i, s: (i, 0))
    return pl.pallas_call(
        partial(head_outer_kernel, parts),
        grid_spec=pltpu.PrefetchScalarGridSpec(
            num_scalar_prefetch=1,
            grid=(count,),
            in_specs=attn_specs
            + [once(gated.shape), pl.BlockSpec((tokens, block), lambda i, s: (0, column(i, s))), once(flat.shape), once(scalar.shape)]
            + [pl.BlockSpec(memory_space=pl.ANY)] * len(others),
            out_specs=[out, out],
        ),
        out_shape=[jax.ShapeDtypeStruct((half, units), bf16)] * 2,
        compiler_params=params(),
        cost_estimate=SMALL,
    )(info, *[attn] * parts, gated, normed, flat, scalar, *others)


SLAB = 128


def summed(refs):
    total = refs[0][...].astype(f32)
    for one in refs[1:]:
        total = total + one[...].astype(f32)
    return total


def line_start_kernel(count, info_ref, *refs):
    refs[-1][...] = summed(refs[:count]).astype(bf16)


def line_step_kernel(now_count, later_count, info_ref, *refs):
    now, later, refs = refs[:now_count], refs[now_count:now_count + later_count], refs[now_count + later_count:]
    right_sent, left_sent, right_came, left_came = refs[:4]
    result_ref, right_ref, left_ref = refs[-3:]
    center, upper = info_ref[1] == 1, info_ref[3] == 1
    add = lambda one, two: one[...].astype(f32) + two[...].astype(f32)

    @pl.when(jnp.logical_not(center))
    def _():
        value = summed(later or now).astype(bf16)
        right_ref[...] = value
        left_ref[...] = value
        result_ref[...] = jnp.where(upper, right_came[...], left_came[...])

    @pl.when(center & upper)
    def _():
        result_ref[...] = right_sent[...]
        right_ref[...] = add(left_sent, right_came).astype(bf16)
        left_ref[...] = (summed(now) + left_came[...].astype(f32)).astype(bf16)

    @pl.when(center & jnp.logical_not(upper))
    def _():
        result_ref[...] = left_sent[...]
        left_ref[...] = add(right_sent, left_came).astype(bf16)
        right_ref[...] = (summed(now) + right_came[...].astype(f32)).astype(bf16)


class Line:
    def __init__(self, info, rows, chunks):
        self.info, self.rows, self.chunks, self.step = info, rows, chunks, 0
        size = lax.axis_size("dp")
        self.stride = size // 4
        self.sent = self.came = None
        self.results = []

    def send(self, right, left):
        count, step = len(self.chunks), self.step
        inner, middle, outer_hop = step < count, 1 <= step <= count, step >= 2
        hops = lambda pairs: [(j + a * self.stride, j + b * self.stride) for a, b in pairs for j in range(self.stride)]
        rightward = [(0, 1)] * inner + [(1, 2)] * middle + [(2, 3)] * outer_hop
        leftward = [(3, 2)] * inner + [(2, 1)] * middle + [(1, 0)] * outer_hop
        self.sent = (right, left)
        self.came = (lax.ppermute(right, "dp", hops(rightward)), lax.ppermute(left, "dp", hops(leftward)))

    def land(self, *others):
        self.came = tuple(after(list(self.came), *others))
        return self.came[0]

    def begin(self, *others):
        *sources, row = self.chunks[0]()
        units = sources[0].shape[1]
        spec = pl.BlockSpec((SLAB, units), lambda i, s: (row * (self.rows // SLAB) + i, 0))
        value = pl.pallas_call(
            partial(line_start_kernel, len(sources)),
            grid_spec=pltpu.PrefetchScalarGridSpec(
                num_scalar_prefetch=1,
                grid=(self.rows // SLAB,),
                in_specs=[spec] * len(sources) + [pl.BlockSpec(memory_space=pl.ANY)] * len(others),
                out_specs=pl.BlockSpec((SLAB, units), lambda i, s: (i, 0)),
            ),
            out_shape=jax.ShapeDtypeStruct((self.rows, units), bf16),
            compiler_params=params(),
            cost_estimate=SMALL,
        )(self.info, *sources, *others)
        self.send(value, value)
        return value

    def advance(self, *others):
        count, step = len(self.chunks), self.step
        *now, first = self.chunks[min(step, count - 1)]()
        *later, second = self.chunks[min(step + 1, count - 1)]()
        per = self.rows // SLAB
        units = now[0].shape[1]
        if now[0] is later[0]:
            later = []
            specs = [pl.BlockSpec((SLAB, units), lambda i, s: (jnp.where(s[1] == 1, first, second) * per + i, 0))] * len(now)
        else:
            specs = [pl.BlockSpec((SLAB, units), lambda i, s: (first * per + i, 0))] * len(now)
            specs += [pl.BlockSpec((SLAB, units), lambda i, s: (second * per + i, 0))] * len(later)
        slab = pl.BlockSpec((SLAB, units), lambda i, s: (i, 0))
        result, right, left = pl.pallas_call(
            partial(line_step_kernel, len(now), len(later)),
            grid_spec=pltpu.PrefetchScalarGridSpec(
                num_scalar_prefetch=1,
                grid=(per,),
                in_specs=specs + [slab] * 4 + [pl.BlockSpec(memory_space=pl.ANY)] * len(others),
                out_specs=[slab] * 3,
            ),
            out_shape=[jax.ShapeDtypeStruct((self.rows, units), bf16)] * 3,
            compiler_params=params(),
            cost_estimate=SMALL,
        )(self.info, *now, *later, *self.sent, *self.came, *others)
        self.step += 1
        if step >= 2:
            self.results.append(result)
        if self.step < count + 2:
            self.send(right, left)
        return result


def place_kernel(turned, info_ref, mine_ref, other_ref, *refs):
    value = jnp.where(pl.program_id(0) == info_ref[0], mine_ref[...], other_ref[...]).astype(f32)
    refs[-2][...] = value.T if turned else value
    refs[-1][...] = jnp.zeros(refs[-1].shape, f32)


def place(info, held, shape, mine, other, row, turned, *others):
    rows, units = mine.shape
    block = 2 * TILE
    per, inner = (shape[1] if turned else shape[0]) // 2 // block, rows // block
    both = pl.BlockSpec((block, units), lambda i, j, s: (j, 0))
    if turned:
        out = pl.BlockSpec((units, block), lambda i, j, s: (0, i * per + row * inner + j))
    else:
        out = pl.BlockSpec((block, units), lambda i, j, s: (i * per + row * inner + j, 0))
    extra = ([] if held is None else [held]) + list(others)
    return pl.pallas_call(
        partial(place_kernel, turned),
        grid_spec=pltpu.PrefetchScalarGridSpec(
            num_scalar_prefetch=1,
            grid=(2, inner),
            in_specs=[both, both] + [pl.BlockSpec(memory_space=pl.ANY)] * len(extra),
            out_specs=[out, pl.BlockSpec((8, HEAD_DIM), lambda i, j, s: (0, 0))],
        ),
        out_shape=[jax.ShapeDtypeStruct(shape, f32), jax.ShapeDtypeStruct((8, HEAD_DIM), f32)],
        input_output_aliases={} if held is None else {3: 0},
        compiler_params=pltpu.CompilerParams(dimension_semantics=("arbitrary", "arbitrary"), vmem_limit_bytes=VMEM_BYTES),
        cost_estimate=SMALL,
    )(info, mine, other, *extra)


def place_heads_kernel(info_ref, *refs):
    own = pl.program_id(0) == info_ref[0]
    one = jnp.where(own, refs[0][...], refs[2][...]).astype(f32)
    two = jnp.where(own, refs[1][...], refs[3][...]).astype(f32)
    out, query, key, value, gate, scalars, token = refs[-7:]
    token[...] = jnp.zeros(token.shape, f32)
    local, units = query.shape[1], one.shape[1]
    out[...] = one[:, :local].T
    query[...] = one[:, local:2 * local]
    cut = units - 2 * local
    key[:, :cut] = one[:, 2 * local:]
    key[:, cut:] = two[:, :local - cut]
    at = local - cut
    value[...] = two[:, at:at + local]
    gate[...] = two[:, at + local:at + 2 * local]
    scalars[...] = two[:, at + 2 * local:at + 2 * local + HEAD_DIM]


def place_heads(info, held, width, local, mine, other, row):
    rows, units = mine[0].shape
    block = 2 * TILE
    per, inner = width // 2 // block, rows // block
    both = pl.BlockSpec((block, units), lambda i, j, s: (j, 0))
    tall = lambda columns: pl.BlockSpec((block, columns), lambda i, j, s: (i * per + row * inner + j, 0))
    return pl.pallas_call(
        place_heads_kernel,
        grid_spec=pltpu.PrefetchScalarGridSpec(
            num_scalar_prefetch=1,
            grid=(2, inner),
            in_specs=[both] * 4 + [pl.BlockSpec(memory_space=pl.ANY)] * len(held),
            out_specs=[pl.BlockSpec((local, block), lambda i, j, s: (0, i * per + row * inner + j))] + [tall(local)] * 4 + [tall(HEAD_DIM), pl.BlockSpec((8, HEAD_DIM), lambda i, j, s: (0, 0))],
        ),
        out_shape=[jax.ShapeDtypeStruct((local, width), f32)]
        + [jax.ShapeDtypeStruct((width, local), f32)] * 4
        + [jax.ShapeDtypeStruct((width, HEAD_DIM), f32), jax.ShapeDtypeStruct((8, HEAD_DIM), f32)],
        input_output_aliases={5 + i: i for i in range(len(held))},
        compiler_params=pltpu.CompilerParams(dimension_semantics=("arbitrary", "arbitrary"), vmem_limit_bytes=VMEM_BYTES),
        cost_estimate=SMALL,
    )(info, *mine, *other, *held)


def xor_pairs(size, mask):
    return [(i, i ^ mask) for i in range(size)]


def swap(values, axis, mask):
    return lax.ppermute(values, axis, xor_pairs(lax.axis_size(axis), mask))


def gather_rows(mine, *others):
    size = lax.axis_size("tp")
    if size != 4:
        parts, mask = [mine], 1
        while mask < size:
            parts = parts + [swap(one, "tp", mask) for one in parts]
            mask *= 2
        return [[one] for one in parts]
    across, down = after([swap(mine, "tp", 1), swap(mine, "tp", 2)], *others)
    top, low = far_halves(across, down)
    return [[mine], [across], [down], [swap(top, "tp", 1), swap(low, "tp", 2)]]


def joined(part):
    return part[0] if len(part) == 1 else jnp.concatenate(part, axis=0)


def gather_weight(weight, before, last):
    places = lax.axis_size("dp")
    rows = weight.shape[0] // places
    piece = lax.dynamic_slice_in_dim(weight, lax.axis_index("dp") * rows, rows, axis=0)
    piece = after(piece, before)
    parts = after([swap(piece, "tp", mask) for mask in range(1, lax.axis_size("tp"))], last)
    return lax.all_gather(jnp.stack(parts, axis=0), "dp", axis=0)


def sum_over(values, axis):
    for i in range(lax.axis_size(axis).bit_length() - 1):
        values = values + swap(values, axis, 1 << i)
    return values


def body(
    tokens,
    seq_lengths,
    out_cotangent,
    attn_norm_gain,
    query_weight,
    key_weight,
    value_weight,
    out_gate_weight,
    head_scalar_weight,
    conv_weight,
    decay_log,
    decay_bias,
    head_norm_gain,
    output_weight,
    mlp_norm_gain,
    mlp_gate_weight,
    mlp_up_weight,
    mlp_down_weight,
):
    rows, width = tokens.shape[1:]
    half = width // 2
    heads = decay_log.shape[0]
    local = output_weight.shape[0]
    units = mlp_gate_weight.shape[1]
    place_at = lax.axis_index("dp") // (lax.axis_size("dp") // 4)
    core = (lax.axis_index("dp") % 2).astype(jnp.int32)
    rank = lax.axis_index("tp").astype(jnp.int32)
    lengths = seq_lengths[0]
    center = (place_at == 1) | (place_at == 2)
    info = jnp.stack([core, center.astype(jnp.int32), rank, (place_at >= 2).astype(jnp.int32)])
    lines = lax.axis_size("dp") == 8 and units % HEAD_DIM == 0
    starts = jnp.stack([rank, lengths[0], lengths[0] + lengths[1]])

    count = lax.axis_size("tp")
    total = count * rows
    scalar_weight = jnp.pad(
        jnp.transpose(head_scalar_weight, (0, 2, 1)).reshape(width, 2 * heads), ((0, 0), (0, HEAD_DIM - 2 * heads))
    )
    pad_row = lambda row: jnp.pad(row, (0, HEAD_DIM - heads))[None]
    rates, biases = pad_row(decay_log), pad_row(decay_bias)
    taps = conv_weight.reshape(3 * CONV, -1)
    in_weights = (query_weight, key_weight, value_weight, out_gate_weight, scalar_weight)
    in_gain, mid_gain = attn_norm_gain[None], mlp_norm_gain[None]
    across = lambda one: swap(one, "dp", 1)
    early = [taps, rates, biases, starts, info]
    held = project([[tokens[0]]], 0, total, in_gain, in_weights, [], *early)
    token_parts = gather_rows(tokens[0], held[-1])
    held = project(token_parts[1:3], 1, total, in_gain, in_weights, held)
    if count == 4:
        token_parts[-1] = after(token_parts[-1], held[-1])
    held = project(token_parts[3:], 3, total, in_gain, in_weights, held)
    far_weight = gather_weight(output_weight, token_parts[-1][-1], held[-1])
    query_proj, key_proj, value_proj, gate_proj, scalar_proj, normed_in = held
    gated, *kept = mixer_forward(
        count, starts, query_proj, key_proj, value_proj, gate_proj, scalar_proj, taps, rates, biases, head_norm_gain[None]
    )
    gated_parts = [joined(one) for one in gather_rows(gated)]
    cot_mine = after(out_cotangent[0], gated_parts[-1])
    normed_mid, middle = middle_rows(token_parts, gated_parts, output_weight, far_weight, mid_gain)

    cot_parts = [[cot_mine]] + [[swap(cot_mine, "tp", mask)] for mask in range(1, count)]
    gates, ups, hidden = hidden_units(normed_mid, mlp_gate_weight, mlp_up_weight)
    mid_other = after(across(normed_mid), hidden)
    cot_parts[-1] = after(cot_parts[-1], hidden)
    cot_flat = [one for part in cot_parts for one in part]
    if lines:
        sources = {}
        chunk = lambda name, row: lambda: (*sources[name], row)
        names = ["down", "gate", "up"]
        even = Line(info, half // 4, [chunk(name, row) for name in names for row in (0, 2)] + [chunk("one", row) for row in range(4)])
        odd = Line(info, half // 4, [chunk(name, row) for name in names for row in (1, 3)] + [chunk("two", row) for row in range(4)])
        placed, waiting = {}, []

        def settle(step):
            if not waiting:
                return step
            name, row, mine, other = waiting.pop(0)
            if name in names:
                shape = (units, width) if name == "down" else (width, units)
                placed[name], step = place(info, placed.get(name), shape, mine, other, row, name == "down", step)
                return step
            *placed["heads"], step = place_heads(
                info, placed.get("heads", []), width, local, mine, [after(one, step) for one in other], row
            )
            return step

        order = {
            id(even): [(name, row) for name in names for row in (0, 2)] + [("one", row) for row in range(4)],
            id(odd): [(name, row) for name in names for row in (1, 3)] + [("two", row) for row in range(4)],
        }
        firsts = {}

        def tick(line, *others):
            before = len(line.results)
            step = line.advance(*others)
            if len(line.results) > before:
                name, row = order[id(line)][before]
                value = line.results[-1]
                other = across(value)
                if name == "one":
                    firsts[row] = (value, other)
                elif name == "two":
                    waiting.append((name, row, [firsts[row][0], value], [firsts[row][1], other]))
                else:
                    waiting.append((name, row, value, other))
            return step

        def land(step, lines=(even, odd)):
            for line in lines:
                step = line.land(step)
            return step

        def ticks(step, lines=(even, odd)):
            for line in lines:
                step = tick(line, step)
            return step

        send = outer_half(info, False, [(cot_flat, hidden)])
        sources["down"] = outer_half(info, True, [(cot_flat, hidden)], send), across(send)
        step = even.begin()
        step = odd.begin(step)

        gate_grad, up_grad, mid_partial = hidden_grads(
            rank[None], cot_parts, gates, ups, mlp_gate_weight, mlp_up_weight, mlp_down_weight, step
        )
        step = land(mid_partial)
        mid_normed_grad = lax.psum_scatter(after(mid_partial, step), "tp", scatter_dimension=0, tiled=True)
        gate_other = across(gate_grad)
        step = ticks(step)
        gate_other = after(gate_other, step)
        up_other = across(after(up_grad, gate_other))
        sources["gate"] = (outer_half(info, True, [([normed_mid], gate_grad), ([mid_other], gate_other)], up_other),)
        step = ticks(sources["gate"][0])
        mid_normed_grad = after(mid_normed_grad, step)
        middle_grad, attn_low, gain_mid = norm_grad([mid_normed_grad], middle, out_cotangent[0], mid_gain)
        attn_all = lax.all_gather(attn_low, "tp", axis=0, tiled=True)
        sources["up"] = (outer_half(info, True, [([normed_mid], up_grad), ([mid_other], up_other)], attn_low),)
        result_partial = result_rows(count, rank[None], hidden, mlp_down_weight, sources["up"][0])
        result_sum = lax.psum_scatter(result_partial, "tp", scatter_dimension=0, tiled=True)
        step = ticks(result_partial)
        step = settle(step)
        step = ticks(step)
        gated_grad = gated_grads(count, rank[None], attn_all, output_weight, step)
        grads = mixer_backward(
            count, starts, gated_grad, gate_proj, query_proj, key_proj, value_proj, scalar_proj, kept, taps, rates, biases, head_norm_gain[None]
        )
        flat_low, scalar_low, grad_taps, misc = grads
        step = land(flat_low)
        step = ticks(step)
        one_send, two_send = head_outer(info, False, count, attn_all, gated, normed_in, flat_low, scalar_low, units, step)
        one_keep, two_keep = head_outer(info, True, count, attn_all, gated, normed_in, flat_low, scalar_low, units, one_send)
        step = land(one_keep)
        one_other = across(after(one_send, step))
        step = settle(step)
        sources["one"] = one_keep, after(one_other, step)
        two_other = across(after(two_send, sources["one"][1]))
        step = tick(even, sources["one"][1])
        sources["two"] = two_keep, after(two_other, step)
        step = tick(odd, step)
        in_partial = input_grads(count, rank[None], flat_low, scalar_low, in_weights, step, result_sum)
        step = land(in_partial)
        in_normed_grad = lax.psum_scatter(after(in_partial, step), "tp", scatter_dimension=0, tiled=True)
        step = settle(step)
        hops = [("tp", 1 << i) for i in range(count.bit_length() - 1)] + [("dp", 1 << i) for i in range(lax.axis_size("dp").bit_length() - 1)]
        small = None
        while len(odd.results) < len(odd.chunks):
            for line in (even, odd):
                step = settle(step)
                step = tick(line, step) if small is None else tick(line, step, small)
                if line is even and even.step == 8:
                    in_normed_grad = after(in_normed_grad, step)
                    _, input_grad, gain_in = norm_grad([in_normed_grad], tokens[0], middle_grad, in_gain)
                    result = small_call(total_kernel, jax.ShapeDtypeStruct((rows, width), bf16), middle, result_sum)
                    small = jnp.concatenate([gain_in[0], gain_mid[0], misc[2]])
                elif small is not None and hops:
                    axis, mask = hops.pop(0)
                    small = small + after(swap(small, axis, mask), step)
                    if hops and hops[0] == ("dp", 1):
                        small = jnp.concatenate([small, grad_taps.reshape(-1), misc[0, :heads], misc[1, :heads]])
        while waiting:
            step = settle(step)
        grad_output, grad_query, grad_key, grad_value, grad_gate, scalar_sum = placed["heads"]
        scalar_sum = scalar_sum[:, :2 * heads]
        grad_down, grad_mlp_gate, grad_mlp_up = placed["down"], placed["gate"], placed["up"]
    else:
        over = lambda left, right: lax.psum(jnp.einsum("ta,tb->ab", left, right, preferred_element_type=f32).astype(bf16), "dp").astype(f32)
        gate_grad, up_grad, mid_partial = hidden_grads(
            rank[None], cot_parts, gates, ups, mlp_gate_weight, mlp_up_weight, mlp_down_weight
        )
        mid_normed_grad = lax.psum_scatter(mid_partial, "tp", scatter_dimension=0, tiled=True)
        middle_grad, attn_low, gain_mid = norm_grad([mid_normed_grad], middle, out_cotangent[0], mid_gain)
        attn_all = lax.all_gather(attn_low, "tp", axis=0, tiled=True)
        gated_grad = gated_grads(count, rank[None], attn_all, output_weight)
        flat_low, scalar_low, grad_taps, misc = mixer_backward(
            count, starts, gated_grad, gate_proj, query_proj, key_proj, value_proj, scalar_proj, kept, taps, rates, biases, head_norm_gain[None]
        )
        in_partial = input_grads(count, rank[None], flat_low, scalar_low, in_weights)
        in_normed_grad = lax.psum_scatter(in_partial, "tp", scatter_dimension=0, tiled=True)
        _, input_grad, gain_in = norm_grad([in_normed_grad], tokens[0], middle_grad, in_gain)
        result_partial = result_rows(count, rank[None], hidden, mlp_down_weight)
        result_sum = lax.psum_scatter(result_partial, "tp", scatter_dimension=0, tiled=True)
        result = small_call(total_kernel, jax.ShapeDtypeStruct((rows, width), bf16), middle, result_sum)
        grad_down = over(hidden, jnp.concatenate([one for part in cot_parts for one in part], axis=0))
        grad_mlp_gate, grad_mlp_up = over(normed_mid, gate_grad), over(normed_mid, up_grad)
        blocks = attn_all.reshape(count, rows, width)
        attn_rows = jnp.concatenate([lax.dynamic_index_in_dim(blocks, rank ^ m, 0, keepdims=False) for m in range(count)], axis=0)
        grad_output = over(gated, attn_rows)
        grad_query, grad_key, grad_value, grad_gate = [
            over(normed_in, flat_low[:, i * local:(i + 1) * local]) for i in range(4)
        ]
        scalar_sum = over(normed_in, scalar_low[:, :2 * heads])
        small = sum_over(jnp.concatenate([gain_in[0], gain_mid[0], misc[2]]), "tp")
        small = jnp.concatenate([small, grad_taps.reshape(-1), misc[0, :heads], misc[1, :heads]])
        hops = [("dp", 1 << i) for i in range(lax.axis_size("dp").bit_length() - 1)]
    for axis, mask in hops:
        small = small + swap(small, axis, mask)
    pieces = []
    at = 0
    for size in (width, width, HEAD_DIM, grad_taps.size, heads, heads):
        pieces.append(small[at:at + size])
        at += size
    gain_in, gain_mid, gain_head, taps_sum, log_sum, bias_sum = pieces
    return (
        result[None],
        input_grad[None],
        gain_in,
        grad_query,
        grad_key,
        grad_value,
        grad_gate,
        jnp.transpose(scalar_sum.reshape(width, 2, heads), (0, 2, 1)),
        taps_sum.reshape(conv_weight.shape),
        log_sum,
        bias_sum,
        gain_head,
        grad_output,
        gain_mid,
        grad_mlp_gate,
        grad_mlp_up,
        grad_down,
    )


def solution(mesh):
    return jax.shard_map(
        body,
        mesh=mesh,
        in_specs=(
            P("dp", "tp", None),
            P("dp", None),
            P("dp", "tp", None),
            P(),
            P(None, "tp"),
            P(None, "tp"),
            P(None, "tp"),
            P(None, "tp"),
            P(None, "tp", None),
            P(None, None, "tp"),
            P("tp"),
            P("tp"),
            P(),
            P("tp", None),
            P(),
            P(None, "tp"),
            P(None, "tp"),
            P("tp", None),
        ),
        out_specs=(
            P("dp", "tp", None),
            P("dp", "tp", None),
            P(),
            P(None, "tp"),
            P(None, "tp"),
            P(None, "tp"),
            P(None, "tp"),
            P(None, "tp", None),
            P(None, None, "tp"),
            P("tp"),
            P("tp"),
            P(),
            P("tp", None),
            P(),
            P(None, "tp"),
            P(None, "tp"),
            P("tp", None),
        ),
        check_vma=False,
    )
```

```python
import math
from functools import partial

import jax
import jax.numpy as jnp
from jax import lax
from jax.experimental import pallas as pl
from jax.experimental.pallas import tpu as pltpu
from jax.sharding import PartitionSpec as P

HEAD_DIM = 128
CONV = 4
SPAN = 64
TILE = 2 * SPAN
VMEM_BYTES = 60 * 1024 * 1024
SMALL = pl.CostEstimate(flops=0, bytes_accessed=0, transcendentals=0)
epsilon = 1e-06
head_epsilon = 0.001
f32 = jnp.float32
bf16 = jnp.bfloat16


def dot(left, right, dims=((1,), (0,)), precise=False):
    return lax.dot_general(
        left, right, (dims, ((), ())), preferred_element_type=f32,
        precision=lax.Precision.HIGHEST if precise else None,
    )


def iota(shape, axis):
    return lax.broadcasted_iota(jnp.int32, shape, axis)


def spread(packed):
    left = iota(packed.shape, 1) < SPAN
    none = jnp.zeros_like(packed)
    return jnp.concatenate([jnp.where(left, packed, none), jnp.where(left, none, packed)], axis=0)


def halves(full):
    left = iota((SPAN, TILE), 1) < SPAN
    return jnp.where(left, full[:SPAN], full[SPAN:])


def packed_masks():
    row, col = iota((SPAN, TILE), 0), iota((SPAN, TILE), 1) % SPAN
    return row, col


def unit_inverse(stricts):
    row, col = packed_masks()
    near = (row // 2) == (col // 2)
    eye = jnp.where(row == col, 1.0, 0.0)
    results = [eye - jnp.where(near, strict, 0.0) for strict in stricts]
    width = 2
    while width < SPAN:
        inside = ((row // (2 * width)) == (col // (2 * width))) & ((row // width) != (col // width))
        pieces = [jnp.where(inside, strict, 0.0).astype(bf16) for strict in stricts]
        kept = [result.astype(bf16) for result in results]
        moved = [dot(piece, spread(keep)) for piece, keep in zip(pieces, kept)]
        results = [result - dot(keep, spread(move.astype(bf16))) for result, keep, move in zip(results, kept, moved)]
        width *= 2
    return results


def softplus(value):
    return jnp.maximum(value, 0.0) + jnp.log1p(jnp.exp(-jnp.abs(value)))


def row_places(first, rows, starts_ref):
    place = iota((rows, HEAD_DIM), 0) + first
    one, two = starts_ref[1], starts_ref[2]
    start = jnp.where(place >= two, two, jnp.where(place >= one, one, 0))
    end = jnp.where(place >= two, 1 << 30, jnp.where(place >= one, two, one))
    return place, start, end


def carry_flag(first, starts_ref):
    fresh = (first == 0) | (first == starts_ref[1]) | (first == starts_ref[2])
    return jnp.where(fresh, 0.0, 1.0).astype(f32)


def decay_parts(scalars, rates, biases):
    row, col = iota((TILE, TILE), 0), iota((TILE, TILE), 1)
    running = jnp.where((row >= col) & ((row // SPAN) == (col // SPAN)), 1.0, 0.0)
    log_decay = -jnp.exp(rates) * softplus(scalars + biases)
    total = dot(running, log_decay, precise=True)
    return log_decay, total, total.T


def fading_of(total, total_rows, head):
    row, col = packed_masks()
    left = iota((SPAN, TILE), 1) < SPAN
    column = jnp.broadcast_to(total[:, head:head + 1], (TILE, TILE))
    gaps = jnp.where(left, column[:SPAN], column[SPAN:]) - total_rows[head:head + 1, :]
    incl = row >= col
    return jnp.where(incl, jnp.exp(jnp.where(incl, gaps, 0.0)), 0.0)


def last_rows(total, head):
    ends = [jnp.broadcast_to(total[SPAN * i + SPAN - 1:SPAN * (i + 1), head:head + 1], (SPAN, TILE)) for i in range(2)]
    return jnp.concatenate(ends, axis=0)


def forward_kernel(tiles, heads, starts_ref, q_ref, k_ref, v_ref, gate_ref, sp_ref, taps_ref, rate_ref, bias_ref, gain_ref,
                   gated_ref, mixed_ref, cq_ref, ck_ref, cv_ref, inv_ref, qk_ref, gram_ref, w_ref, u_ref, s_ref,
                   ext_ref, state_ref):
    step = pl.program_id(0)
    rows = tiles * TILE

    @pl.when(step == 0)
    def _():
        ext_ref[:, :8, :] = jnp.zeros((3, 8, heads * HEAD_DIM), f32)
        state_ref[...] = jnp.zeros(state_ref.shape, f32)

    ones = jnp.ones((HEAD_DIM, HEAD_DIM), bf16)
    place, start, _ = row_places(step * rows, rows, starts_ref)
    position = place - start
    masks = [jnp.where(position >= j, 1.0, 0.0) for j in range(1, CONV)]
    for which, source in enumerate((q_ref, k_ref, v_ref)):
        ext_ref[which, 8:8 + rows, :] = source[...].astype(f32)

    def activated(which, head, out):
        lanes = slice(head * HEAD_DIM, (head + 1) * HEAD_DIM)
        conv = ext_ref[which, 8:8 + rows, lanes] * taps_ref[which * CONV:which * CONV + 1, lanes]
        for j in range(1, CONV):
            conv = conv + ext_ref[which, 8 - j:8 - j + rows, lanes] * masks[j - 1] * taps_ref[which * CONV + j:which * CONV + j + 1, lanes]
        low = conv.astype(bf16)
        out[:, lanes] = low
        conv = low.astype(f32)
        return conv * jax.nn.sigmoid(conv)

    active = [[activated(which, h, out) for h in range(heads)] for which, out in enumerate((cq_ref, ck_ref, cv_ref))]
    norms = [[dot((one * one).astype(bf16), ones) for one in active[which]] for which in range(2)]
    queries = [one * (lax.rsqrt(norm + epsilon) * HEAD_DIM ** -0.5) for one, norm in zip(active[0], norms[0])]
    keys = [one * lax.rsqrt(norm + epsilon) for one, norm in zip(active[1], norms[1])]
    values = active[2]
    for which in range(3):
        ext_ref[which, :8, :] = ext_ref[which, rows:rows + 8, :]

    lanes_of = lambda head: slice(head * HEAD_DIM, (head + 1) * HEAD_DIM)
    row, col = packed_masks()
    left = iota((SPAN, TILE), 1) < SPAN
    pairs = [(tile, head) for tile in range(tiles) for head in range(heads)]
    spans = [slice(tile * TILE, (tile + 1) * TILE) for tile in range(tiles)]
    packs = [slice(tile * SPAN, (tile + 1) * SPAN) for tile in range(tiles)]
    scalars = [sp_ref[span, :] for span in spans]
    decays = [decay_parts(one, rate_ref[...], bias_ref[...]) for one in scalars]
    writes = [jax.nn.sigmoid(one) for one in scalars]
    grams = []
    for tile, head in pairs:
        k_low = keys[head][spans[tile]].astype(bf16)
        grams.append(dot(jnp.concatenate([queries[head][spans[tile]].astype(bf16), k_low], axis=0), k_low, ((1,), (1,))))
    stricts, scores, spread_writes, columns = [], [], [], []
    for (tile, head), both in zip(pairs, grams):
        _, total, total_rows = decays[tile]
        write = jnp.broadcast_to(writes[tile][:, heads + head:heads + head + 1], (TILE, HEAD_DIM))
        column = jnp.broadcast_to(total[:, head:head + 1], (TILE, HEAD_DIM))
        gaps = jnp.where(left, column[:SPAN], column[SPAN:]) - total_rows[head:head + 1, :]
        fading = jnp.where(row >= col, jnp.exp(jnp.where(row >= col, gaps, 0.0)), 0.0)
        qk, gram = halves(both[:TILE]), halves(both[TILE:])
        qk_ref[packs[tile], lanes_of(head)] = qk.astype(bf16)
        gram_ref[packs[tile], lanes_of(head)] = gram.astype(bf16)
        write_pack = jnp.where(left, write[:SPAN], write[SPAN:])
        stricts.append(jnp.where(row > col, write_pack * gram * fading, 0.0))
        scores.append(spread((qk * fading).astype(bf16)))
        spread_writes.append(write)
        columns.append(column)
    inverses = [one.astype(bf16) for one in unit_inverse(stricts)]
    weighted, free, q_grown, k_tail, ends = [], [], [], [], []
    for (tile, head), inverse, write, column in zip(pairs, inverses, spread_writes, columns):
        total = decays[tile][1]
        q, k, v = queries[head][spans[tile]], keys[head][spans[tile]], values[head][spans[tile]]
        grown = jnp.exp(column)
        tails = jnp.exp(last_rows(total, head) - column)
        inv_ref[packs[tile], lanes_of(head)] = inverse
        sides = jnp.concatenate([(write * grown * k).astype(bf16), (write * v).astype(bf16)], axis=1)
        solved = dot(spread(inverse), sides)
        low = solved[:, :HEAD_DIM].astype(bf16)
        w_ref[spans[tile], lanes_of(head)] = low
        weighted.append(low)
        free.append(solved[:, HEAD_DIM:])
        q_grown.append((q * grown).astype(bf16))
        k_tail.append((k * tails).astype(bf16))
        ends.append([jnp.exp(total[SPAN * i + SPAN - 1:SPAN * (i + 1), head:head + 1]) for i in range(2)])

    states = [state_ref[head] for head in range(heads)]
    for tile in range(tiles):
        at = tile * heads
        seen, changes = [[] for _ in range(heads)], [[] for _ in range(heads)]
        for i in range(2):
            flag = carry_flag(step * rows + tile * TILE + i * SPAN, starts_ref)
            states = [state * flag for state in states]
            lows = [state.astype(bf16) for state in states]
            base = (tile * 2 + i) * HEAD_DIM
            part = slice(i * SPAN, (i + 1) * SPAN)
            both = [dot(jnp.concatenate([weighted[at + h][part], q_grown[at + h][part]], axis=0), lows[h]) for h in range(heads)]
            new = [(free[at + h][part] - both[h][:SPAN]).astype(bf16) for h in range(heads)]
            states = [ends[at + h][i] * states[h] + dot(k_tail[at + h][part], new[h], ((0,), (0,))) for h in range(heads)]
            for h in range(heads):
                s_ref[base:base + HEAD_DIM, lanes_of(h)] = lows[h]
                seen[h].append(both[h][SPAN:])
                changes[h].append(new[h])
        change = [jnp.concatenate(parts, axis=0) for parts in changes]
        mixed = [jnp.concatenate(seen[h], axis=0) + dot(scores[at + h], change[h]) for h in range(heads)]
        squares = [dot((one * one).astype(bf16), ones) * (1.0 / HEAD_DIM) for one in mixed]
        for h in range(heads):
            u_ref[spans[tile], lanes_of(h)] = change[h]
            mixed_ref[spans[tile], lanes_of(h)] = mixed[h].astype(bf16)
            normed = mixed[h] * lax.rsqrt(squares[h] + head_epsilon) * gain_ref[...]
            gate = gate_ref[spans[tile], lanes_of(h)].astype(f32)
            gated_ref[spans[tile], lanes_of(h)] = (normed * gate * jax.nn.sigmoid(gate)).astype(bf16)
    for h in range(heads):
        state_ref[h] = states[h]


def blocked(rows, width, place):
    return pl.BlockSpec((rows, width), lambda i, s: (place(i) ^ s[0], 0))


def constant(shape):
    return pl.BlockSpec(shape, lambda i, s: (0,) * len(shape))


def mixer_forward(count, starts, q, k, v, gate, sp, taps, rate, bias, gain):
    rows, width = q.shape
    heads = width // HEAD_DIM
    block = rows // count
    tiles = block // TILE
    spec = lambda r, w: blocked(r, w, lambda i: i)
    wide, half, state = spec(block, width), spec(block // 2, width), spec(block * 2, width)
    shape = lambda r: jax.ShapeDtypeStruct((r, width), bf16)
    return pl.pallas_call(
        partial(forward_kernel, tiles, heads),
        grid_spec=pltpu.PrefetchScalarGridSpec(
            num_scalar_prefetch=1,
            grid=(count,),
            in_specs=[wide] * 4 + [spec(block, HEAD_DIM)] + [constant(a.shape) for a in (taps, rate, bias, gain)],
            out_specs=[wide] * 5 + [half] * 3 + [wide] * 2 + [state],
            scratch_shapes=[pltpu.VMEM((3, block + 8, width), f32), pltpu.VMEM((heads, HEAD_DIM, HEAD_DIM), f32)],
        ),
        out_shape=[shape(rows)] * 5 + [shape(rows // 2)] * 3 + [shape(rows)] * 2 + [shape(rows * 2)],
        compiler_params=pltpu.CompilerParams(dimension_semantics=("arbitrary",), vmem_limit_bytes=VMEM_BYTES),
        cost_estimate=SMALL,
    )(starts, q, k, v, gate, sp, taps, rate, bias, gain)


def row_sums(product, ones_tall):
    high = product.astype(bf16)
    low = (product - high.astype(f32)).astype(bf16)
    return dot(jnp.concatenate([high, low], axis=1), ones_tall)


def backward_kernel(tiles, heads, starts_ref, gg_ref, mixed_ref, gate_ref, cq_ref, ck_ref, cv_ref, q_ref, k_ref, v_ref, sp_ref,
                    inv_ref, qk_ref, gram_ref, w_ref, u_ref, s_ref, taps_ref, rate_ref, bias_ref, gain_ref,
                    flat_ref, dsp_ref, dtaps_ref, dmisc_ref, ext_ref, state_ref):
    step = pl.num_programs(0) - 1 - pl.program_id(0)
    rows = tiles * TILE

    @pl.when(pl.program_id(0) == 0)
    def _():
        ext_ref[:, rows:, :] = jnp.zeros((3, 8, heads * HEAD_DIM), f32)
        state_ref[...] = jnp.zeros(state_ref.shape, f32)
        dtaps_ref[...] = jnp.zeros(dtaps_ref.shape, f32)
        dmisc_ref[...] = jnp.zeros(dmisc_ref.shape, f32)

    ones = jnp.ones((HEAD_DIM, HEAD_DIM), bf16)
    ones_tall = jnp.ones((2 * HEAD_DIM, HEAD_DIM), bf16)
    lanes_of = lambda head: slice(head * HEAD_DIM, (head + 1) * HEAD_DIM)
    row, col = packed_masks()
    left = iota((SPAN, TILE), 1) < SPAN
    full_row, full_col = iota((TILE, TILE), 0), iota((TILE, TILE), 1)
    same = (full_row // SPAN) == (full_col // SPAN)
    pairs = [(tile, head) for tile in range(tiles) for head in range(heads)]
    spans = [slice(tile * TILE, (tile + 1) * TILE) for tile in range(tiles)]
    packs = [slice(tile * SPAN, (tile + 1) * SPAN) for tile in range(tiles)]
    gain = gain_ref[...]

    mixed = [mixed_ref[spans[t], lanes_of(h)].astype(f32) for t, h in pairs]
    squares = [dot((one * one).astype(bf16), ones) * (1.0 / HEAD_DIM) for one in mixed]
    partial_gain = jnp.zeros((1, HEAD_DIM), f32)
    scales, pulled, inner = [], [], []
    for (t, h), one, square in zip(pairs, mixed, squares):
        scale = lax.rsqrt(square + head_epsilon)
        gate = gate_ref[spans[t], lanes_of(h)].astype(f32)
        grad = gg_ref[spans[t], lanes_of(h)].astype(f32)
        sig = jax.nn.sigmoid(gate)
        unit = one * scale
        flat_ref[spans[t], lanes_of(3 * heads + h)] = (grad * unit * gain * (sig * (1.0 + gate * (1.0 - sig)))).astype(bf16)
        norm_grad = grad * gate * sig
        partial_gain = partial_gain + jnp.sum(norm_grad * unit, axis=0, keepdims=True)
        norm_grad = norm_grad * gain
        scales.append(scale)
        pulled.append(norm_grad)
        inner.append(dot((norm_grad * unit).astype(bf16), ones) * (1.0 / HEAD_DIM))
    dmisc_ref[2:3, :] = dmisc_ref[2:3, :] + partial_gain
    dout = [(scale * (grad - one * scale * mean)).astype(bf16) for scale, grad, one, mean in zip(scales, pulled, mixed, inner)]

    def silu_parts(ref, t, h):
        conv = ref[spans[t], lanes_of(h)].astype(f32)
        sig = jax.nn.sigmoid(conv)
        return conv * sig, sig * (1.0 + conv * (1.0 - sig))

    raw_q = [silu_parts(cq_ref, t, h) for t, h in pairs]
    raw_k = [silu_parts(ck_ref, t, h) for t, h in pairs]
    norm_q = [lax.rsqrt(dot((one[0] * one[0]).astype(bf16), ones) + epsilon) for one in raw_q]
    norm_k = [lax.rsqrt(dot((one[0] * one[0]).astype(bf16), ones) + epsilon) for one in raw_k]
    decays = [decay_parts(sp_ref[span, :], rate_ref[...], bias_ref[...]) for span in spans]
    writes = [jax.nn.sigmoid(sp_ref[span, :]) for span in spans]
    queries, keys, fadings, growns, tails, spread_writes, write_packs, ends = [], [], [], [], [], [], [], []
    for n, (t, h) in enumerate(pairs):
        _, total, total_rows = decays[t]
        queries.append(raw_q[n][0] * (norm_q[n] * HEAD_DIM ** -0.5))
        keys.append(raw_k[n][0] * norm_k[n])
        write = jnp.broadcast_to(writes[t][:, heads + h:heads + h + 1], (TILE, HEAD_DIM))
        column = jnp.broadcast_to(total[:, h:h + 1], (TILE, HEAD_DIM))
        gaps = jnp.where(left, column[:SPAN], column[SPAN:]) - total_rows[h:h + 1, :]
        fadings.append(jnp.where(row >= col, jnp.exp(jnp.where(row >= col, gaps, 0.0)), 0.0))
        growns.append(jnp.exp(column))
        tails.append(jnp.exp(last_rows(total, h) - column))
        spread_writes.append(write)
        write_packs.append(jnp.where(left, write[:SPAN], write[SPAN:]))
        ends.append([jnp.exp(total[SPAN * i + SPAN - 1:SPAN * (i + 1), h:h + 1]) for i in range(2)])
    qk = [qk_ref[packs[t], lanes_of(h)].astype(f32) for t, h in pairs]
    score_grads = [dot(spread((qk[n] * fadings[n]).astype(bf16)), dout[n], ((0,), (0,))) for n in range(len(pairs))]
    q_grown = [(queries[n] * growns[n]).astype(bf16) for n in range(len(pairs))]
    k_tail = [(keys[n] * tails[n]).astype(bf16) for n in range(len(pairs))]
    parts = [slice(0, SPAN), slice(SPAN, TILE)]
    q_outs = [[dot(q_grown[n][part], dout[n][part], ((0,), (0,))) for part in parts] for n in range(len(pairs))]

    states = [state_ref[h] for h in range(heads)]
    change_grads = [[None, None] for _ in pairs]
    tail_grads = [[None, None] for _ in pairs]
    end_grads = [[None, None] for _ in pairs]
    for t in reversed(range(tiles)):
        for i in (1, 0):
            part = parts[i]
            here = slice(t * TILE + i * SPAN, t * TILE + (i + 1) * SPAN)
            at = slice((t * 2 + i) * HEAD_DIM, (t * 2 + i + 1) * HEAD_DIM)
            flag = carry_flag(step * rows + t * TILE + i * SPAN, starts_ref)
            lows = [one.astype(bf16) for one in states]
            news = []
            for h in range(heads):
                n = t * heads + h
                news.append((score_grads[n][part] + dot(k_tail[n][part], lows[h])).astype(bf16))
            for h in range(heads):
                n = t * heads + h
                change_grads[n][i] = news[h]
                tail_grads[n][i] = dot(u_ref[here, lanes_of(h)], lows[h], ((1,), (1,)))
                held = jnp.sum(states[h] * s_ref[at, lanes_of(h)].astype(f32), axis=0, keepdims=True)
                end_grads[n][i] = ends[n][i] * jnp.sum(held, axis=1, keepdims=True)
            states = [
                flag * (ends[t * heads + h][i] * states[h] + q_outs[t * heads + h][i] - dot(w_ref[here, lanes_of(h)], news[h], ((0,), (0,))))
                for h in range(heads)
            ]
    for h in range(heads):
        state_ref[h] = states[h]

    change_grads = [jnp.concatenate(one, axis=0) for one in change_grads]
    side_grads = [dot(spread(inv_ref[packs[t], lanes_of(h)]), change_grads[n], ((0,), (0,))) for n, (t, h) in enumerate(pairs)]
    side_low = [one.astype(bf16) for one in side_grads]
    crossed = []
    for n, (t, h) in enumerate(pairs):
        through = []
        for i, part in enumerate(parts):
            at = slice((t * 2 + i) * HEAD_DIM, (t * 2 + i + 1) * HEAD_DIM)
            through.append(dot(jnp.concatenate([side_low[n][part], dout[n][part]], axis=0), s_ref[at, lanes_of(h)], ((1,), (1,))))
        grams = dot(jnp.concatenate([dout[n], side_low[n]], axis=0), u_ref[spans[t], lanes_of(h)], ((1,), (1,)))
        crossed.append((through, grams))
    query_grads, key_grads = [], []
    flat_q = [one.astype(bf16) for one in queries]
    flat_k = [one.astype(bf16) for one in keys]
    products = []
    for n, (t, h) in enumerate(pairs):
        through, grams = crossed[n]
        weighted_grad = -jnp.concatenate([one[:SPAN] for one in through], axis=0)
        grown_grad = jnp.concatenate([one[SPAN:] for one in through], axis=0)
        gram = gram_ref[packs[t], lanes_of(h)].astype(f32)
        pair_grad = halves(grams[:TILE]) * fadings[n]
        strict_grad = jnp.where(row > col, -halves(grams[TILE:]), 0.0) * fadings[n]
        gram_grad = strict_grad * write_packs[n]
        matrix = jnp.concatenate([spread(pair_grad.astype(bf16)), spread(gram_grad.astype(bf16))], axis=0)
        forward = dot(matrix, flat_k[n])
        backward = dot(matrix, jnp.concatenate([flat_q[n], flat_k[n]], axis=0), ((0,), (0,)))
        tail_grad = jnp.concatenate(tail_grads[n], axis=0)
        grown_key = growns[n] * keys[n]
        write = spread_writes[n]
        query_grads.append(forward[:TILE] + grown_grad * growns[n])
        key_grads.append(forward[TILE:] + backward + tail_grad * tails[n] + weighted_grad * write * growns[n])
        value = cv_ref[spans[t], lanes_of(h)].astype(f32)
        value = value * jax.nn.sigmoid(value)
        moving = pair_grad * qk[n] + gram_grad * gram
        inner_key = weighted_grad * grown_key
        products.append((
            spread(strict_grad * gram) + inner_key + side_grads[n] * value,
            spread(moving) + grown_grad * growns[n] * queries[n] + inner_key * write,
            tail_grad * tails[n] * keys[n],
            jnp.sum(moving, axis=0, keepdims=True),
        ))
    sums = [[row_sums(one, ones_tall) for one in three[:3]] for three in products]
    upper = jnp.where((full_row <= full_col) & same, 1.0, 0.0)
    lower = jnp.where((full_row > full_col) & same, 1.0, 0.0)
    for t in range(tiles):
        gap_grad = jnp.zeros((TILE, HEAD_DIM), f32)
        tail_sum = jnp.zeros((TILE, HEAD_DIM), f32)
        write_grad = jnp.zeros((TILE, HEAD_DIM), f32)
        ends_grad = jnp.zeros((TILE, HEAD_DIM), f32)
        across = jnp.zeros((TILE, HEAD_DIM), f32)
        for h in range(heads):
            n = t * heads + h
            mine = full_col == h
            gap_grad = jnp.where(mine, sums[n][1], gap_grad)
            tail_sum = jnp.where(mine, sums[n][2], tail_sum)
            write_grad = jnp.where(full_col == heads + h, sums[n][0], write_grad)
            across = jnp.where(full_row == h, products[n][3], across)
            ends_grad = jnp.where(mine, jnp.where(full_row < SPAN, end_grads[n][0], end_grads[n][1]), ends_grad)
        log_grad = dot(upper, gap_grad - across.T, precise=True) + dot(lower, tail_sum, precise=True) + ends_grad
        scalars = sp_ref[spans[t], :]
        rate = -jnp.exp(rate_ref[...])
        inside = log_grad * rate * jax.nn.sigmoid(scalars + bias_ref[...])
        write = writes[t]
        out = jnp.where(full_col < heads, inside, write_grad * write * (1.0 - write))
        dsp_ref[spans[t], :] = jnp.where(full_col < 2 * heads, out, 0.0).astype(bf16)
        dmisc_ref[0:1, :] = dmisc_ref[0:1, :] + jnp.sum(log_grad * decays[t][0], axis=0, keepdims=True)
        dmisc_ref[1:2, :] = dmisc_ref[1:2, :] + jnp.sum(inside, axis=0, keepdims=True)

    inner_q = [dot((query_grads[n] * raw_q[n][0]).astype(bf16), ones) for n in range(len(pairs))]
    inner_k = [dot((key_grads[n] * raw_k[n][0]).astype(bf16), ones) for n in range(len(pairs))]
    for n, (t, h) in enumerate(pairs):
        scale = norm_q[n]
        grad = (query_grads[n] - raw_q[n][0] * (scale * scale * inner_q[n])) * (scale * HEAD_DIM ** -0.5)
        ext_ref[0, spans[t], lanes_of(h)] = grad * raw_q[n][1]
        scale = norm_k[n]
        grad = (key_grads[n] - raw_k[n][0] * (scale * scale * inner_k[n])) * scale
        ext_ref[1, spans[t], lanes_of(h)] = grad * raw_k[n][1]
        ext_ref[2, spans[t], lanes_of(h)] = side_grads[n] * spread_writes[n] * silu_parts(cv_ref, t, h)[1]
    place, _, end = row_places(step * rows, rows, starts_ref)
    masks = [None] + [jnp.where(place + j < end, 1.0, 0.0) for j in range(1, CONV)]
    for which, source in enumerate((q_ref, k_ref, v_ref)):
        for h in range(heads):
            lanes = lanes_of(h)
            proj = source[:, lanes].astype(f32)
            total = None
            for j in range(CONV):
                moved = ext_ref[which, j:j + rows, lanes]
                if j:
                    moved = moved * masks[j]
                at = which * CONV + j
                dtaps_ref[at:at + 1, lanes] = dtaps_ref[at:at + 1, lanes] + jnp.sum(proj * moved, axis=0, keepdims=True)
                term = moved * taps_ref[at:at + 1, lanes]
                total = term if total is None else total + term
            flat_ref[:, lanes_of(which * heads + h)] = total.astype(bf16)
        ext_ref[which, rows:, :] = ext_ref[which, :8, :]


def mixer_backward(count, starts, gg, gate, q, k, v, sp, kept, taps, rate, bias, gain):
    mixed, cq, ck, cv, inv, qk, gram, w, u, s = kept
    rows, width = q.shape
    heads = width // HEAD_DIM
    block = rows // count
    tiles = block // TILE
    spec = lambda r, w: blocked(r, w, lambda i: count - 1 - i)
    wide, half, state, scal = spec(block, width), spec(block // 2, width), spec(block * 2, width), spec(block, HEAD_DIM)
    shape = lambda r: jax.ShapeDtypeStruct((r, width), bf16)
    return pl.pallas_call(
        partial(backward_kernel, tiles, heads),
        grid_spec=pltpu.PrefetchScalarGridSpec(
            num_scalar_prefetch=1,
            grid=(count,),
            in_specs=[wide] * 9 + [scal] + [half] * 3 + [wide] * 2 + [state] + [constant(a.shape) for a in (taps, rate, bias, gain)],
            out_specs=[spec(block, 4 * width), scal, constant((3 * CONV, width)), constant((8, HEAD_DIM))],
            scratch_shapes=[pltpu.VMEM((3, block + 8, width), f32), pltpu.VMEM((heads, HEAD_DIM, HEAD_DIM), f32)],
        ),
        out_shape=[
            jax.ShapeDtypeStruct((rows, 4 * width), bf16),
            jax.ShapeDtypeStruct((rows, HEAD_DIM), bf16),
            jax.ShapeDtypeStruct((3 * CONV, width), f32),
            jax.ShapeDtypeStruct((8, HEAD_DIM), f32),
        ],
        compiler_params=pltpu.CompilerParams(dimension_semantics=("arbitrary",), vmem_limit_bytes=VMEM_BYTES),
        cost_estimate=SMALL,
    )(starts, gg, mixed, gate, cq, ck, cv, q, k, v, sp, inv, qk, gram, w, u, s, taps, rate, bias, gain)


def after(values, *others):
    single = not isinstance(values, (list, tuple))
    values = [values] if single else list(values)
    others = [one for one in others if one is not None]
    out = pl.pallas_call(
        lambda *refs: None,
        out_shape=[jax.ShapeDtypeStruct(one.shape, one.dtype) for one in values],
        in_specs=[pl.BlockSpec(memory_space=pl.ANY)] * (len(values) + len(others)),
        out_specs=[pl.BlockSpec(memory_space=pl.ANY)] * len(values),
        input_output_aliases={i: i for i in range(len(values))},
    )(*values, *others)
    return out[0] if single else list(out)


def once(shape):
    return pl.BlockSpec(shape, lambda *_: (0,) * len(shape), pipeline_mode=pl.Buffered(1))


def params():
    return pltpu.CompilerParams(dimension_semantics=("arbitrary",), vmem_limit_bytes=VMEM_BYTES)


def project_kernel(sizes, *refs):
    parts, refs = split_pieces(refs, sizes)
    gain_ref, weights, outs, held = refs[0], refs[1:6], refs[-7:-1], refs[-1]
    if len(sizes) > 1:
        pick(len(sizes), parts, held)
        x = held[...].astype(f32)
    else:
        x = whole(parts[0]).astype(f32)
    scale = lax.rsqrt(jnp.mean(x * x, axis=-1, keepdims=True) + epsilon)
    normed = (x * scale * gain_ref[...]).astype(bf16)
    outs[5][...] = normed
    for weight, out in zip(weights, outs[:5]):
        out[...] = dot(normed, weight[...]).astype(out.dtype)


def project(parts, first, total, gain, weights, held, *others):
    rows, depth = sum(one.shape[0] for one in parts[0]), parts[0][0].shape[1]
    flat, sizes = [one for part in parts for one in part], [len(part) for part in parts]
    shapes = [jax.ShapeDtypeStruct((total, w.shape[1]), f32 if i == 4 else bf16) for i, w in enumerate(weights)]
    shapes.append(jax.ShapeDtypeStruct((total, depth), bf16))
    return pl.pallas_call(
        partial(project_kernel, sizes),
        grid=(len(parts),),
        in_specs=[once(one.shape) for one in flat]
        + [once(gain.shape)]
        + [once(w.shape) for w in weights]
        + [pl.BlockSpec(memory_space=pl.ANY)] * (len(held) + len(others)),
        out_specs=[pl.BlockSpec((rows, s.shape[1]), lambda i: (first + i, 0)) for s in shapes],
        out_shape=shapes,
        scratch_shapes=[pltpu.VMEM((rows, depth), bf16)],
        input_output_aliases={len(flat) + 6 + i: i for i in range(len(held))},
        compiler_params=params(),
        cost_estimate=SMALL,
    )(*flat, gain, *weights, *held, *others)


def pick(count, refs, held):
    step = pl.program_id(0)
    for which in range(count):
        @pl.when(step == which)
        def _():
            held[...] = whole(refs[which]) if isinstance(refs[which], (list, tuple)) else refs[which][...]


def middle_kernel(sizes, *refs):
    count = len(sizes)
    x_refs, refs = split_pieces(refs, sizes)
    g_refs = refs[:count]
    own_weight, far_weight, gain_ref, normed_ref, own_ref, scr, x_scr = refs[count:]
    pick(count, x_refs, x_scr)
    gated = jnp.concatenate([one[...] for one in g_refs], axis=1)
    width = gated.shape[1] // count
    for a, b in column_cuts(scr.shape[1]):
        weight = [own_weight[:, a:b]] + [far_weight[:, m, :, a:b].reshape(width, b - a) for m in range(count - 1)]
        scr[:, a:b] = dot(gated, jnp.concatenate(weight, axis=0)) + x_scr[:, a:b].astype(f32)
    middle = scr[...]
    scale = lax.rsqrt(jnp.mean(middle * middle, axis=-1, keepdims=True) + epsilon)
    normed_ref[...] = (middle * scale * gain_ref[...]).astype(bf16)

    @pl.when(pl.program_id(0) == 0)
    def _():
        own_ref[...] = middle


def middle_rows(x_parts, gated_parts, own_weight, far_weight, gain):
    count = len(x_parts)
    rows, depth = x_parts[0][0].shape
    width = gated_parts[0].shape[1]
    flat = [one for part in x_parts for one in part]
    return pl.pallas_call(
        partial(middle_kernel, [len(part) for part in x_parts]),
        grid=(count,),
        in_specs=[once(one.shape) for one in flat]
        + [pl.BlockSpec((rows, width), lambda i, at=at: (i ^ at, 0)) for at in range(count)]
        + [once(own_weight.shape), once(far_weight.shape), once(gain.shape)],
        out_specs=[pl.BlockSpec((rows, depth), lambda i: (i, 0)), once((rows, depth))],
        out_shape=[jax.ShapeDtypeStruct((count * rows, depth), bf16), jax.ShapeDtypeStruct((rows, depth), f32)],
        scratch_shapes=[pltpu.VMEM((rows, depth), f32), pltpu.VMEM((rows, depth), bf16)],
        compiler_params=params(),
        cost_estimate=SMALL,
    )(*flat, *gated_parts, own_weight, far_weight, gain)


def gated_grad_kernel(rank_ref, rows_ref, weight_ref, *refs):
    refs[-1][...] = dot(rows_ref[...], weight_ref[...], ((1,), (1,))).astype(bf16)


def gated_grads(count, rank, gathered, weight, *others):
    rows, depth = gathered.shape[0] // count, gathered.shape[1]
    width = weight.shape[0]
    return pl.pallas_call(
        gated_grad_kernel,
        grid_spec=pltpu.PrefetchScalarGridSpec(
            num_scalar_prefetch=1,
            grid=(count,),
            in_specs=[pl.BlockSpec((rows, depth), lambda i, s: (i ^ s[0], 0)), once(weight.shape)]
            + [pl.BlockSpec(memory_space=pl.ANY)] * len(others),
            out_specs=pl.BlockSpec((rows, width), lambda i, s: (i, 0)),
        ),
        out_shape=jax.ShapeDtypeStruct((count * rows, width), bf16),
        compiler_params=params(),
        cost_estimate=SMALL,
    )(rank, gathered, weight, *others)


def column_cuts(width, chunk=512):
    return [(lo, min(lo + chunk, width)) for lo in range(0, width, chunk)]


def hidden_kernel(x_ref, wg_ref, wu_ref, *refs):
    gate_ref, up_ref, hidden_ref = refs[-3:]
    x = x_ref[...]
    for a, b in column_cuts(wg_ref.shape[1]):
        gate, up = dot(x, wg_ref[:, a:b]), dot(x, wu_ref[:, a:b])
        gate_ref[:, a:b] = gate.astype(bf16)
        up_ref[:, a:b] = up.astype(bf16)
        hidden_ref[:, a:b] = (gate * jax.nn.sigmoid(gate) * up).astype(bf16)


def hidden_units(x, gate_weight, up_weight, *others):
    rows, depth = x.shape
    width = gate_weight.shape[1]
    block = rows // 4
    out = pl.BlockSpec((block, width), lambda i: (i, 0))
    return pl.pallas_call(
        hidden_kernel,
        grid=(4,),
        in_specs=[pl.BlockSpec((block, depth), lambda i: (i, 0)), once(gate_weight.shape), once(up_weight.shape)]
        + [pl.BlockSpec(memory_space=pl.ANY)] * len(others),
        out_specs=[out] * 3,
        out_shape=[jax.ShapeDtypeStruct((rows, width), bf16)] * 3,
        compiler_params=params(),
        cost_estimate=SMALL,
    )(x, gate_weight, up_weight, *others)


def whole(refs):
    values = [one[...] for one in refs]
    return values[0] if len(values) == 1 else jnp.concatenate(values, axis=0)


def outer_kernel(parts, info_ref, *refs):
    total, at = None, 0
    for count in parts:
        term = dot(whole(refs[at:at + count]), refs[at + count][...], ((0,), (0,)))
        total = term if total is None else total + term
        at += count + 1
    refs[-1][...] = total.astype(bf16)


def half_column(count, own):
    return lambda i, s: (s[0] if own else 1 - s[0]) * count + i


def outer_half(info, own, sides, *others):
    lefts, right = sides[0]
    half, block = lefts[0].shape[1] // 2, 2 * TILE
    count, units = half // block, right.shape[1]
    column = half_column(count, own)
    in_specs, values = [], []
    for lefts, right in sides:
        in_specs += [pl.BlockSpec((one.shape[0], block), lambda i, s: (0, column(i, s))) for one in lefts] + [once(right.shape)]
        values += list(lefts) + [right]
    return pl.pallas_call(
        partial(outer_kernel, [len(lefts) for lefts, _ in sides]),
        grid_spec=pltpu.PrefetchScalarGridSpec(
            num_scalar_prefetch=1,
            grid=(count,),
            in_specs=in_specs + [pl.BlockSpec(memory_space=pl.ANY)] * len(others),
            out_specs=pl.BlockSpec((block, units), lambda i, s: (i, 0)),
        ),
        out_shape=jax.ShapeDtypeStruct((half, units), bf16),
        compiler_params=params(),
        cost_estimate=SMALL,
    )(info, *values, *others)


def split_pieces(refs, sizes):
    pieces, at = [], 0
    for size in sizes:
        pieces.append(refs[at:at + size])
        at += size
    return pieces, refs[at:]


def hidden_grad_kernel(sizes, rank_ref, *refs):
    c_refs, refs = split_pieces(refs, sizes)
    gate_ref, up_ref, wg_ref, wu_ref, wd_ref = refs[:5]
    gg_ref, ug_ref, mid_ref, held = refs[-4:]
    pick(len(sizes), c_refs, held)
    grad_rows = held[...]
    nt = ((1,), (1,))
    for a, b in column_cuts(wg_ref.shape[1]):
        grad = dot(grad_rows, wd_ref[a:b, :], nt)
        gate, up = gate_ref[:, a:b].astype(f32), up_ref[:, a:b].astype(f32)
        sig = jax.nn.sigmoid(gate)
        gg_ref[:, a:b] = (grad * up * sig * (1.0 + gate * (1.0 - sig))).astype(bf16)
        ug_ref[:, a:b] = (grad * gate * sig).astype(bf16)
    gate_grad, up_grad = gg_ref[...], ug_ref[...]
    for a, b in column_cuts(wg_ref.shape[0]):
        mid_ref[:, a:b] = (dot(gate_grad, wg_ref[a:b, :], nt) + dot(up_grad, wu_ref[a:b, :], nt)).astype(bf16)


def hidden_grads(rank, cot_parts, gates, ups, gate_weight, up_weight, down_weight, *others):
    count = len(cot_parts)
    rows, depth = cot_parts[0][0].shape
    width = gate_weight.shape[1]
    spec = pl.BlockSpec((rows, width), lambda i, s: (i, 0))
    flat = [one for part in cot_parts for one in part]
    return pl.pallas_call(
        partial(hidden_grad_kernel, [len(part) for part in cot_parts]),
        grid_spec=pltpu.PrefetchScalarGridSpec(
            num_scalar_prefetch=1,
            grid=(count,),
            in_specs=[once(one.shape) for one in flat]
            + [spec] * 2
            + [once(gate_weight.shape), once(up_weight.shape), once(down_weight.shape)]
            + [pl.BlockSpec(memory_space=pl.ANY)] * len(others),
            out_specs=[spec, spec, pl.BlockSpec((rows, depth), lambda i, s: (i ^ s[0], 0))],
            scratch_shapes=[pltpu.VMEM((rows, depth), bf16)],
        ),
        out_shape=[jax.ShapeDtypeStruct((count * rows, width), bf16)] * 2 + [jax.ShapeDtypeStruct((count * rows, depth), bf16)],
        compiler_params=params(),
        cost_estimate=SMALL,
    )(rank, *flat, gates, ups, gate_weight, up_weight, down_weight, *others)


def input_grad_kernel(rank_ref, grad_ref, scalar_ref, *refs):
    weights, out = refs[:5], refs[-1]
    grad = jnp.concatenate([grad_ref[...], scalar_ref[...]], axis=1)
    for a, b in column_cuts(out.shape[1]):
        weight = jnp.concatenate([one[a:b, :] for one in weights], axis=1)
        out[:, a:b] = dot(grad, weight, ((1,), (1,))).astype(bf16)


def input_grads(count, rank, grad, scalar_grad, weights, *others):
    rows, depth = grad.shape[0] // count, weights[0].shape[0]
    return pl.pallas_call(
        input_grad_kernel,
        grid_spec=pltpu.PrefetchScalarGridSpec(
            num_scalar_prefetch=1,
            grid=(count,),
            in_specs=[pl.BlockSpec((rows, one.shape[1]), lambda i, s: (i, 0)) for one in (grad, scalar_grad)]
            + [once(one.shape) for one in weights]
            + [pl.BlockSpec(memory_space=pl.ANY)] * len(others),
            out_specs=pl.BlockSpec((rows, depth), lambda i, s: (i ^ s[0], 0)),
        ),
        out_shape=jax.ShapeDtypeStruct((count * rows, depth), bf16),
        compiler_params=params(),
        cost_estimate=SMALL,
    )(rank, grad, scalar_grad, *weights, *others)


def result_kernel(rank_ref, hidden_ref, weight_ref, *refs):
    out = refs[-1]
    for a, b in column_cuts(out.shape[1]):
        out[:, a:b] = dot(hidden_ref[...], weight_ref[:, a:b]).astype(bf16)


def result_rows(count, rank, hidden, weight, *others):
    rows, depth = hidden.shape[0] // count, weight.shape[1]
    return pl.pallas_call(
        result_kernel,
        grid_spec=pltpu.PrefetchScalarGridSpec(
            num_scalar_prefetch=1,
            grid=(count,),
            in_specs=[pl.BlockSpec((rows, hidden.shape[1]), lambda i, s: (i, 0)), once(weight.shape)]
            + [pl.BlockSpec(memory_space=pl.ANY)] * len(others),
            out_specs=pl.BlockSpec((rows, depth), lambda i, s: (i ^ s[0], 0)),
        ),
        out_shape=jax.ShapeDtypeStruct((count * rows, depth), bf16),
        compiler_params=params(),
        cost_estimate=SMALL,
    )(rank, hidden, weight, *others)


def small_call(kernel, outs, *values):
    return pl.pallas_call(
        kernel,
        out_shape=outs,
        compiler_params=pltpu.CompilerParams(vmem_limit_bytes=VMEM_BYTES),
        cost_estimate=SMALL,
    )(*values)


def merge_kernel(across_ref, down_ref, top_ref, low_ref, *refs):
    half = top_ref.shape[0]
    across_out, down_out = refs[-2:]
    down_out[:half] = (down_ref[:half].astype(f32) + top_ref[...].astype(f32)).astype(bf16)
    down_out[half:] = down_ref[half:]
    across_out[:half] = across_ref[:half]
    across_out[half:] = (across_ref[half:].astype(f32) + low_ref[...].astype(f32)).astype(bf16)


def halves_kernel(across_ref, down_ref, top_out, low_out):
    top_out[...] = down_ref[...]
    low_out[...] = across_ref[...]


def far_halves(across, down):
    rows, columns = across.shape[0] // 2, across.shape[1]
    top, low = pl.BlockSpec((rows, columns), lambda i: (0, 0)), pl.BlockSpec((rows, columns), lambda i: (1, 0))
    return pl.pallas_call(
        halves_kernel,
        grid=(1,),
        in_specs=[low, top],
        out_specs=[top, top],
        out_shape=[jax.ShapeDtypeStruct((rows, columns), across.dtype)] * 2,
        compiler_params=params(),
        cost_estimate=SMALL,
    )(across, down)


def norm_grad_kernel(count, *refs):
    terms, (x_ref, cot_ref, gain_ref, grad_out, low_out, gain_out) = refs[:count], refs[count:]
    grad = terms[0][...].astype(f32)
    for one in terms[1:]:
        grad = grad + one[...].astype(f32)
    x = x_ref[...].astype(f32)
    scale = lax.rsqrt(jnp.mean(x * x, axis=-1, keepdims=True) + epsilon)
    unit = x * scale
    gain_out[...] = jnp.sum(grad * unit, axis=0, keepdims=True)
    inner = grad * gain_ref[...]
    total = cot_ref[...].astype(f32) + scale * (inner - unit * jnp.mean(inner * unit, axis=-1, keepdims=True))
    if grad_out is not None:
        grad_out[...] = total
    low_out[...] = total.astype(bf16)


def norm_grad(terms, x, cot, gain):
    rows, depth = x.shape
    return small_call(
        partial(norm_grad_kernel, len(terms)),
        [jax.ShapeDtypeStruct((rows, depth), f32), jax.ShapeDtypeStruct((rows, depth), bf16), jax.ShapeDtypeStruct((1, depth), f32)],
        *terms, x, cot, gain,
    )


def total_kernel(*refs):
    refs[-1][...] = (refs[0][...] + refs[1][...].astype(f32)).astype(bf16)


def wide_call(kernel, out_dtype, values, *others):
    rows, columns = values[0].shape
    block = next(size for size in (256, 128, 64, 32, 16) if rows % size == 0)
    spec = pl.BlockSpec((block, columns), lambda i, *_: (i, 0))
    return pl.pallas_call(
        kernel,
        grid=(rows // block,),
        in_specs=[spec] * len(values) + [pl.BlockSpec(memory_space=pl.ANY)] * len(others),
        out_specs=spec,
        out_shape=jax.ShapeDtypeStruct((rows, columns), out_dtype),
        compiler_params=params(),
        cost_estimate=SMALL,
    )(*values, *others)


def add_kernel(left, right, *refs):
    refs[-1][...] = (left[...].astype(f32) + right[...].astype(f32)).astype(bf16)


def cast_kernel(value, *refs):
    refs[-1][...] = value[...].astype(f32)


def choose_kernel(flag_ref, left, right, *refs):
    refs[-1][...] = jnp.where(flag_ref[0] == 1, left[...], right[...])


def choose(flag, left, right, *others):
    rows, columns = left.shape
    block = next(size for size in (256, 128, 64, 32, 16) if rows % size == 0)
    spec = pl.BlockSpec((block, columns), lambda i, s: (i, 0))
    return pl.pallas_call(
        choose_kernel,
        grid_spec=pltpu.PrefetchScalarGridSpec(
            num_scalar_prefetch=1,
            grid=(rows // block,),
            in_specs=[spec, spec] + [pl.BlockSpec(memory_space=pl.ANY)] * len(others),
            out_specs=spec,
        ),
        out_shape=jax.ShapeDtypeStruct((rows, columns), left.dtype),
        compiler_params=params(),
        cost_estimate=SMALL,
    )(flag, left, right, *others)


def head_outer_kernel(parts, info_ref, *refs):
    attn, (gated_ref, in_ref, flat_ref, scalar_ref) = refs[:parts], refs[parts:parts + 4]
    one, two = refs[-2:]
    units = one.shape[1]
    tn = ((0,), (0,))
    left = in_ref[...]
    columns = [dot(whole(attn), gated_ref[...], tn), dot(left, flat_ref[...], tn), dot(left, scalar_ref[...], tn)]
    joined = jnp.concatenate([one.astype(bf16) for one in columns], axis=1)
    spare = 2 * units - joined.shape[1]
    if spare:
        joined = jnp.concatenate([joined, jnp.zeros((joined.shape[0], spare), bf16)], axis=1)
    one[...] = joined[:, :units]
    two[...] = joined[:, units:]


def head_outer(info, own, parts, attn, gated, normed, flat, scalar, units, *others):
    tokens, width = normed.shape
    half, block = width // 2, 2 * TILE
    count, rows = half // block, tokens // parts
    column = half_column(count, own)
    attn_specs = [pl.BlockSpec((rows, block), lambda i, s, m=m: (s[2] ^ m, column(i, s))) for m in range(parts)]
    out = pl.BlockSpec((block, units), lambda i, s: (i, 0))
    return pl.pallas_call(
        partial(head_outer_kernel, parts),
        grid_spec=pltpu.PrefetchScalarGridSpec(
            num_scalar_prefetch=1,
            grid=(count,),
            in_specs=attn_specs
            + [once(gated.shape), pl.BlockSpec((tokens, block), lambda i, s: (0, column(i, s))), once(flat.shape), once(scalar.shape)]
            + [pl.BlockSpec(memory_space=pl.ANY)] * len(others),
            out_specs=[out, out],
        ),
        out_shape=[jax.ShapeDtypeStruct((half, units), bf16)] * 2,
        compiler_params=params(),
        cost_estimate=SMALL,
    )(info, *[attn] * parts, gated, normed, flat, scalar, *others)


SLAB = 128


def summed(refs):
    total = refs[0][...].astype(f32)
    for one in refs[1:]:
        total = total + one[...].astype(f32)
    return total


def line_start_kernel(count, info_ref, *refs):
    refs[-1][...] = summed(refs[:count]).astype(bf16)


def line_step_kernel(now_count, later_count, info_ref, *refs):
    now, later, refs = refs[:now_count], refs[now_count:now_count + later_count], refs[now_count + later_count:]
    right_sent, left_sent, right_came, left_came = refs[:4]
    result_ref, right_ref, left_ref = refs[-3:]
    center, upper = info_ref[1] == 1, info_ref[3] == 1
    add = lambda one, two: one[...].astype(f32) + two[...].astype(f32)

    @pl.when(jnp.logical_not(center))
    def _():
        value = summed(later or now).astype(bf16)
        right_ref[...] = value
        left_ref[...] = value
        result_ref[...] = jnp.where(upper, right_came[...], left_came[...])

    @pl.when(center & upper)
    def _():
        result_ref[...] = right_sent[...]
        right_ref[...] = add(left_sent, right_came).astype(bf16)
        left_ref[...] = (summed(now) + left_came[...].astype(f32)).astype(bf16)

    @pl.when(center & jnp.logical_not(upper))
    def _():
        result_ref[...] = left_sent[...]
        left_ref[...] = add(right_sent, left_came).astype(bf16)
        right_ref[...] = (summed(now) + right_came[...].astype(f32)).astype(bf16)


class Line:
    def __init__(self, info, rows, chunks):
        self.info, self.rows, self.chunks, self.step = info, rows, chunks, 0
        size = lax.axis_size("dp")
        self.stride = size // 4
        self.sent = self.came = None
        self.results = []

    def send(self, right, left):
        count, step = len(self.chunks), self.step
        inner, middle, outer_hop = step < count, 1 <= step <= count, step >= 2
        hops = lambda pairs: [(j + a * self.stride, j + b * self.stride) for a, b in pairs for j in range(self.stride)]
        rightward = [(0, 1)] * inner + [(1, 2)] * middle + [(2, 3)] * outer_hop
        leftward = [(3, 2)] * inner + [(2, 1)] * middle + [(1, 0)] * outer_hop
        self.sent = (right, left)
        self.came = (lax.ppermute(right, "dp", hops(rightward)), lax.ppermute(left, "dp", hops(leftward)))

    def land(self, *others):
        self.came = tuple(after(list(self.came), *others))
        return self.came[0]

    def begin(self, *others):
        *sources, row = self.chunks[0]()
        units = sources[0].shape[1]
        spec = pl.BlockSpec((SLAB, units), lambda i, s: (row * (self.rows // SLAB) + i, 0))
        value = pl.pallas_call(
            partial(line_start_kernel, len(sources)),
            grid_spec=pltpu.PrefetchScalarGridSpec(
                num_scalar_prefetch=1,
                grid=(self.rows // SLAB,),
                in_specs=[spec] * len(sources) + [pl.BlockSpec(memory_space=pl.ANY)] * len(others),
                out_specs=pl.BlockSpec((SLAB, units), lambda i, s: (i, 0)),
            ),
            out_shape=jax.ShapeDtypeStruct((self.rows, units), bf16),
            compiler_params=params(),
            cost_estimate=SMALL,
        )(self.info, *sources, *others)
        self.send(value, value)
        return value

    def advance(self, *others):
        count, step = len(self.chunks), self.step
        *now, first = self.chunks[min(step, count - 1)]()
        *later, second = self.chunks[min(step + 1, count - 1)]()
        per = self.rows // SLAB
        units = now[0].shape[1]
        if now[0] is later[0]:
            later = []
            specs = [pl.BlockSpec((SLAB, units), lambda i, s: (jnp.where(s[1] == 1, first, second) * per + i, 0))] * len(now)
        else:
            specs = [pl.BlockSpec((SLAB, units), lambda i, s: (first * per + i, 0))] * len(now)
            specs += [pl.BlockSpec((SLAB, units), lambda i, s: (second * per + i, 0))] * len(later)
        slab = pl.BlockSpec((SLAB, units), lambda i, s: (i, 0))
        result, right, left = pl.pallas_call(
            partial(line_step_kernel, len(now), len(later)),
            grid_spec=pltpu.PrefetchScalarGridSpec(
                num_scalar_prefetch=1,
                grid=(per,),
                in_specs=specs + [slab] * 4 + [pl.BlockSpec(memory_space=pl.ANY)] * len(others),
                out_specs=[slab] * 3,
            ),
            out_shape=[jax.ShapeDtypeStruct((self.rows, units), bf16)] * 3,
            compiler_params=params(),
            cost_estimate=SMALL,
        )(self.info, *now, *later, *self.sent, *self.came, *others)
        self.step += 1
        if step >= 2:
            self.results.append(result)
        if self.step < count + 2:
            self.send(right, left)
        return result


def place_kernel(turned, info_ref, mine_ref, other_ref, *refs):
    value = jnp.where(pl.program_id(0) == info_ref[0], mine_ref[...], other_ref[...]).astype(f32)
    refs[-2][...] = value.T if turned else value
    refs[-1][...] = jnp.zeros(refs[-1].shape, f32)


def place(info, held, shape, mine, other, row, turned, *others):
    rows, units = mine.shape
    block = 2 * TILE
    per, inner = (shape[1] if turned else shape[0]) // 2 // block, rows // block
    both = pl.BlockSpec((block, units), lambda i, j, s: (j, 0))
    if turned:
        out = pl.BlockSpec((units, block), lambda i, j, s: (0, i * per + row * inner + j))
    else:
        out = pl.BlockSpec((block, units), lambda i, j, s: (i * per + row * inner + j, 0))
    extra = ([] if held is None else [held]) + list(others)
    return pl.pallas_call(
        partial(place_kernel, turned),
        grid_spec=pltpu.PrefetchScalarGridSpec(
            num_scalar_prefetch=1,
            grid=(2, inner),
            in_specs=[both, both] + [pl.BlockSpec(memory_space=pl.ANY)] * len(extra),
            out_specs=[out, pl.BlockSpec((8, HEAD_DIM), lambda i, j, s: (0, 0))],
        ),
        out_shape=[jax.ShapeDtypeStruct(shape, f32), jax.ShapeDtypeStruct((8, HEAD_DIM), f32)],
        input_output_aliases={} if held is None else {3: 0},
        compiler_params=pltpu.CompilerParams(dimension_semantics=("arbitrary", "arbitrary"), vmem_limit_bytes=VMEM_BYTES),
        cost_estimate=SMALL,
    )(info, mine, other, *extra)


def place_heads_kernel(info_ref, *refs):
    own = pl.program_id(0) == info_ref[0]
    one = jnp.where(own, refs[0][...], refs[2][...]).astype(f32)
    two = jnp.where(own, refs[1][...], refs[3][...]).astype(f32)
    out, query, key, value, gate, scalars, token = refs[-7:]
    token[...] = jnp.zeros(token.shape, f32)
    local, units = query.shape[1], one.shape[1]
    out[...] = one[:, :local].T
    query[...] = one[:, local:2 * local]
    cut = units - 2 * local
    key[:, :cut] = one[:, 2 * local:]
    key[:, cut:] = two[:, :local - cut]
    at = local - cut
    value[...] = two[:, at:at + local]
    gate[...] = two[:, at + local:at + 2 * local]
    scalars[...] = two[:, at + 2 * local:at + 2 * local + HEAD_DIM]


def place_heads(info, held, width, local, mine, other, row):
    rows, units = mine[0].shape
    block = 2 * TILE
    per, inner = width // 2 // block, rows // block
    both = pl.BlockSpec((block, units), lambda i, j, s: (j, 0))
    tall = lambda columns: pl.BlockSpec((block, columns), lambda i, j, s: (i * per + row * inner + j, 0))
    return pl.pallas_call(
        place_heads_kernel,
        grid_spec=pltpu.PrefetchScalarGridSpec(
            num_scalar_prefetch=1,
            grid=(2, inner),
            in_specs=[both] * 4 + [pl.BlockSpec(memory_space=pl.ANY)] * len(held),
            out_specs=[pl.BlockSpec((local, block), lambda i, j, s: (0, i * per + row * inner + j))] + [tall(local)] * 4 + [tall(HEAD_DIM), pl.BlockSpec((8, HEAD_DIM), lambda i, j, s: (0, 0))],
        ),
        out_shape=[jax.ShapeDtypeStruct((local, width), f32)]
        + [jax.ShapeDtypeStruct((width, local), f32)] * 4
        + [jax.ShapeDtypeStruct((width, HEAD_DIM), f32), jax.ShapeDtypeStruct((8, HEAD_DIM), f32)],
        input_output_aliases={5 + i: i for i in range(len(held))},
        compiler_params=pltpu.CompilerParams(dimension_semantics=("arbitrary", "arbitrary"), vmem_limit_bytes=VMEM_BYTES),
        cost_estimate=SMALL,
    )(info, *mine, *other, *held)


def xor_pairs(size, mask):
    return [(i, i ^ mask) for i in range(size)]


def swap(values, axis, mask):
    return lax.ppermute(values, axis, xor_pairs(lax.axis_size(axis), mask))


def gather_rows(mine, *others):
    size = lax.axis_size("tp")
    if size != 4:
        parts, mask = [mine], 1
        while mask < size:
            parts = parts + [swap(one, "tp", mask) for one in parts]
            mask *= 2
        return [[one] for one in parts]
    across, down = after([swap(mine, "tp", 1), swap(mine, "tp", 2)], *others)
    top, low = far_halves(across, down)
    return [[mine], [across], [down], [swap(top, "tp", 1), swap(low, "tp", 2)]]


def joined(part):
    return part[0] if len(part) == 1 else jnp.concatenate(part, axis=0)


def gather_weight(weight, before, last):
    places = lax.axis_size("dp")
    rows = weight.shape[0] // places
    piece = lax.dynamic_slice_in_dim(weight, lax.axis_index("dp") * rows, rows, axis=0)
    piece = after(piece, before)
    parts = after([swap(piece, "tp", mask) for mask in range(1, lax.axis_size("tp"))], last)
    return lax.all_gather(jnp.stack(parts, axis=0), "dp", axis=0)


def sum_over(values, axis):
    for i in range(lax.axis_size(axis).bit_length() - 1):
        values = values + swap(values, axis, 1 << i)
    return values


def body(
    tokens,
    seq_lengths,
    out_cotangent,
    attn_norm_gain,
    query_weight,
    key_weight,
    value_weight,
    out_gate_weight,
    head_scalar_weight,
    conv_weight,
    decay_log,
    decay_bias,
    head_norm_gain,
    output_weight,
    mlp_norm_gain,
    mlp_gate_weight,
    mlp_up_weight,
    mlp_down_weight,
):
    rows, width = tokens.shape[1:]
    half = width // 2
    heads = decay_log.shape[0]
    local = output_weight.shape[0]
    units = mlp_gate_weight.shape[1]
    place_at = lax.axis_index("dp") // (lax.axis_size("dp") // 4)
    core = (lax.axis_index("dp") % 2).astype(jnp.int32)
    rank = lax.axis_index("tp").astype(jnp.int32)
    lengths = seq_lengths[0]
    center = (place_at == 1) | (place_at == 2)
    info = jnp.stack([core, center.astype(jnp.int32), rank, (place_at >= 2).astype(jnp.int32)])
    lines = lax.axis_size("dp") == 8 and units % HEAD_DIM == 0
    starts = jnp.stack([rank, lengths[0], lengths[0] + lengths[1]])

    count = lax.axis_size("tp")
    total = count * rows
    scalar_weight = jnp.pad(
        jnp.transpose(head_scalar_weight, (0, 2, 1)).reshape(width, 2 * heads), ((0, 0), (0, HEAD_DIM - 2 * heads))
    )
    pad_row = lambda row: jnp.pad(row, (0, HEAD_DIM - heads))[None]
    rates, biases = pad_row(decay_log), pad_row(decay_bias)
    taps = conv_weight.reshape(3 * CONV, -1)
    in_weights = (query_weight, key_weight, value_weight, out_gate_weight, scalar_weight)
    in_gain, mid_gain = attn_norm_gain[None], mlp_norm_gain[None]
    across = lambda one: swap(one, "dp", 1)
    early = [taps, rates, biases, starts, info]
    held = project([[tokens[0]]], 0, total, in_gain, in_weights, [], *early)
    token_parts = gather_rows(tokens[0], held[-1])
    held = project(token_parts[1:3], 1, total, in_gain, in_weights, held)
    if count == 4:
        token_parts[-1] = after(token_parts[-1], held[-1])
    held = project(token_parts[3:], 3, total, in_gain, in_weights, held)
    far_weight = gather_weight(output_weight, token_parts[-1][-1], held[-1])
    query_proj, key_proj, value_proj, gate_proj, scalar_proj, normed_in = held
    gated, *kept = mixer_forward(
        count, starts, query_proj, key_proj, value_proj, gate_proj, scalar_proj, taps, rates, biases, head_norm_gain[None]
    )
    gated_parts = [joined(one) for one in gather_rows(gated)]
    cot_mine = after(out_cotangent[0], gated_parts[-1])
    normed_mid, middle = middle_rows(token_parts, gated_parts, output_weight, far_weight, mid_gain)

    cot_parts = [[cot_mine]] + [[swap(cot_mine, "tp", mask)] for mask in range(1, count)]
    gates, ups, hidden = hidden_units(normed_mid, mlp_gate_weight, mlp_up_weight)
    mid_other = after(across(normed_mid), hidden)
    cot_parts[-1] = after(cot_parts[-1], hidden)
    cot_flat = [one for part in cot_parts for one in part]
    if lines:
        sources = {}
        chunk = lambda name, row: lambda: (*sources[name], row)
        names = ["down", "gate", "up"]
        even = Line(info, half // 4, [chunk(name, row) for name in names for row in (0, 2)] + [chunk("one", row) for row in range(4)])
        odd = Line(info, half // 4, [chunk(name, row) for name in names for row in (1, 3)] + [chunk("two", row) for row in range(4)])
        placed, waiting = {}, []

        def settle(step):
            if not waiting:
                return step
            name, row, mine, other = waiting.pop(0)
            if name in names:
                shape = (units, width) if name == "down" else (width, units)
                placed[name], step = place(info, placed.get(name), shape, mine, other, row, name == "down", step)
                return step
            *placed["heads"], step = place_heads(
                info, placed.get("heads", []), width, local, mine, [after(one, step) for one in other], row
            )
            return step

        order = {
            id(even): [(name, row) for name in names for row in (0, 2)] + [("one", row) for row in range(4)],
            id(odd): [(name, row) for name in names for row in (1, 3)] + [("two", row) for row in range(4)],
        }
        firsts = {}

        def tick(line, *others):
            before = len(line.results)
            step = line.advance(*others)
            if len(line.results) > before:
                name, row = order[id(line)][before]
                value = line.results[-1]
                other = across(value)
                if name == "one":
                    firsts[row] = (value, other)
                elif name == "two":
                    waiting.append((name, row, [firsts[row][0], value], [firsts[row][1], other]))
                else:
                    waiting.append((name, row, value, other))
            return step

        def land(step, lines=(even, odd)):
            for line in lines:
                step = line.land(step)
            return step

        def ticks(step, lines=(even, odd)):
            for line in lines:
                step = tick(line, step)
            return step

        send = outer_half(info, False, [(cot_flat, hidden)])
        sources["down"] = outer_half(info, True, [(cot_flat, hidden)], send), across(send)
        step = even.begin()
        step = odd.begin(step)

        gate_grad, up_grad, mid_partial = hidden_grads(
            rank[None], cot_parts, gates, ups, mlp_gate_weight, mlp_up_weight, mlp_down_weight, step
        )
        step = land(mid_partial)
        mid_normed_grad = lax.psum_scatter(after(mid_partial, step), "tp", scatter_dimension=0, tiled=True)
        gate_other = across(gate_grad)
        step = ticks(step)
        gate_other = after(gate_other, step)
        up_other = across(up_grad)
        sources["gate"] = (outer_half(info, True, [([normed_mid], gate_grad), ([mid_other], gate_other)], up_other),)
        step = ticks(sources["gate"][0])
        mid_normed_grad = after(mid_normed_grad, step)
        middle_grad, attn_low, gain_mid = norm_grad([mid_normed_grad], middle, out_cotangent[0], mid_gain)
        attn_all = lax.all_gather(attn_low, "tp", axis=0, tiled=True)
        sources["up"] = (outer_half(info, True, [([normed_mid], up_grad), ([mid_other], up_other)], attn_low),)
        result_partial = result_rows(count, rank[None], hidden, mlp_down_weight, sources["up"][0])
        result_sum = lax.psum_scatter(result_partial, "tp", scatter_dimension=0, tiled=True)
        step = ticks(result_partial)
        step = settle(step)
        step = ticks(step)
        gated_grad = gated_grads(count, rank[None], attn_all, output_weight, step)
        grads = mixer_backward(
            count, starts, gated_grad, gate_proj, query_proj, key_proj, value_proj, scalar_proj, kept, taps, rates, biases, head_norm_gain[None]
        )
        flat_low, scalar_low, grad_taps, misc = grads
        step = land(flat_low)
        step = ticks(step)
        one_send, two_send = head_outer(info, False, count, attn_all, gated, normed_in, flat_low, scalar_low, units, step)
        one_keep, two_keep = head_outer(info, True, count, attn_all, gated, normed_in, flat_low, scalar_low, units, one_send)
        step = land(one_keep)
        one_other = across(after(one_send, step))
        step = settle(step)
        sources["one"] = one_keep, after(one_other, step)
        two_other = across(after(two_send, sources["one"][1]))
        step = tick(even, sources["one"][1])
        sources["two"] = two_keep, after(two_other, step)
        step = tick(odd, step)
        in_partial = input_grads(count, rank[None], flat_low, scalar_low, in_weights, step, result_sum)
        step = land(in_partial)
        in_normed_grad = lax.psum_scatter(after(in_partial, step), "tp", scatter_dimension=0, tiled=True)
        step = settle(step)
        hops = [("tp", 1 << i) for i in range(count.bit_length() - 1)] + [("dp", 1 << i) for i in range(lax.axis_size("dp").bit_length() - 1)]
        small = None
        while len(odd.results) < len(odd.chunks):
            for line in (even, odd):
                step = settle(step)
                step = tick(line, step) if small is None else tick(line, step, small)
                if line is even and even.step == 8:
                    in_normed_grad = after(in_normed_grad, step)
                    _, input_grad, gain_in = norm_grad([in_normed_grad], tokens[0], middle_grad, in_gain)
                    result = small_call(total_kernel, jax.ShapeDtypeStruct((rows, width), bf16), middle, result_sum)
                    small = jnp.concatenate([gain_in[0], gain_mid[0], misc[2]])
                elif small is not None and hops:
                    axis, mask = hops.pop(0)
                    small = small + after(swap(small, axis, mask), step)
                    if hops and hops[0] == ("dp", 1):
                        small = jnp.concatenate([small, grad_taps.reshape(-1), misc[0, :heads], misc[1, :heads]])
        while waiting:
            step = settle(step)
        grad_output, grad_query, grad_key, grad_value, grad_gate, scalar_sum = placed["heads"]
        scalar_sum = scalar_sum[:, :2 * heads]
        grad_down, grad_mlp_gate, grad_mlp_up = placed["down"], placed["gate"], placed["up"]
    else:
        over = lambda left, right: lax.psum(jnp.einsum("ta,tb->ab", left, right, preferred_element_type=f32).astype(bf16), "dp").astype(f32)
        gate_grad, up_grad, mid_partial = hidden_grads(
            rank[None], cot_parts, gates, ups, mlp_gate_weight, mlp_up_weight, mlp_down_weight
        )
        mid_normed_grad = lax.psum_scatter(mid_partial, "tp", scatter_dimension=0, tiled=True)
        middle_grad, attn_low, gain_mid = norm_grad([mid_normed_grad], middle, out_cotangent[0], mid_gain)
        attn_all = lax.all_gather(attn_low, "tp", axis=0, tiled=True)
        gated_grad = gated_grads(count, rank[None], attn_all, output_weight)
        flat_low, scalar_low, grad_taps, misc = mixer_backward(
            count, starts, gated_grad, gate_proj, query_proj, key_proj, value_proj, scalar_proj, kept, taps, rates, biases, head_norm_gain[None]
        )
        in_partial = input_grads(count, rank[None], flat_low, scalar_low, in_weights)
        in_normed_grad = lax.psum_scatter(in_partial, "tp", scatter_dimension=0, tiled=True)
        _, input_grad, gain_in = norm_grad([in_normed_grad], tokens[0], middle_grad, in_gain)
        result_partial = result_rows(count, rank[None], hidden, mlp_down_weight)
        result_sum = lax.psum_scatter(result_partial, "tp", scatter_dimension=0, tiled=True)
        result = small_call(total_kernel, jax.ShapeDtypeStruct((rows, width), bf16), middle, result_sum)
        grad_down = over(hidden, jnp.concatenate([one for part in cot_parts for one in part], axis=0))
        grad_mlp_gate, grad_mlp_up = over(normed_mid, gate_grad), over(normed_mid, up_grad)
        blocks = attn_all.reshape(count, rows, width)
        attn_rows = jnp.concatenate([lax.dynamic_index_in_dim(blocks, rank ^ m, 0, keepdims=False) for m in range(count)], axis=0)
        grad_output = over(gated, attn_rows)
        grad_query, grad_key, grad_value, grad_gate = [
            over(normed_in, flat_low[:, i * local:(i + 1) * local]) for i in range(4)
        ]
        scalar_sum = over(normed_in, scalar_low[:, :2 * heads])
        small = sum_over(jnp.concatenate([gain_in[0], gain_mid[0], misc[2]]), "tp")
        small = jnp.concatenate([small, grad_taps.reshape(-1), misc[0, :heads], misc[1, :heads]])
        hops = [("dp", 1 << i) for i in range(lax.axis_size("dp").bit_length() - 1)]
    for axis, mask in hops:
        small = small + swap(small, axis, mask)
    pieces = []
    at = 0
    for size in (width, width, HEAD_DIM, grad_taps.size, heads, heads):
        pieces.append(small[at:at + size])
        at += size
    gain_in, gain_mid, gain_head, taps_sum, log_sum, bias_sum = pieces
    return (
        result[None],
        input_grad[None],
        gain_in,
        grad_query,
        grad_key,
        grad_value,
        grad_gate,
        jnp.transpose(scalar_sum.reshape(width, 2, heads), (0, 2, 1)),
        taps_sum.reshape(conv_weight.shape),
        log_sum,
        bias_sum,
        gain_head,
        grad_output,
        gain_mid,
        grad_mlp_gate,
        grad_mlp_up,
        grad_down,
    )


def solution(mesh):
    return jax.shard_map(
        body,
        mesh=mesh,
        in_specs=(
            P("dp", "tp", None),
            P("dp", None),
            P("dp", "tp", None),
            P(),
            P(None, "tp"),
            P(None, "tp"),
            P(None, "tp"),
            P(None, "tp"),
            P(None, "tp", None),
            P(None, None, "tp"),
            P("tp"),
            P("tp"),
            P(),
            P("tp", None),
            P(),
            P(None, "tp"),
            P(None, "tp"),
            P("tp", None),
        ),
        out_specs=(
            P("dp", "tp", None),
            P("dp", "tp", None),
            P(),
            P(None, "tp"),
            P(None, "tp"),
            P(None, "tp"),
            P(None, "tp"),
            P(None, "tp", None),
            P(None, None, "tp"),
            P("tp"),
            P("tp"),
            P(),
            P("tp", None),
            P(),
            P(None, "tp"),
            P(None, "tp"),
            P("tp", None),
        ),
        check_vma=False,
    )
```
